32 devices in a mesh: batch: 16 (over z, y, x), tensor: 2 (over core).
Axes of the slice: x: 2, y: 2, z: 4, core: 2. Of those that a mesh axis runs over, the one named last changes fastest.
Arguments:
- tokens: bfloat16 [32768, 768], P('batch'), may hold values from -6 to 6
- cotangent: bfloat16 [32768, 768], P('batch'), may hold values from -6 to 6
- phase_of: int32 [16], P('batch'), may hold values from 0 to 1
- unit_slot: int32 [144], replicated, may hold values from 0 to 287, as said below
- step_count: int32 [1], replicated, may hold values from 2 to 8
- learn_rates: float32 [5], replicated, as said below
- decay_rates: float32 [3], replicated, may hold values from 0.5 to 0.7
- master: float32 [288, 64, 768], P('batch', None, 'tensor')
- first_moment: float32 [288, 64, 768], P('batch', None, 'tensor')
- second_moment: float32 [288, 64, 768], P('batch', None, 'tensor')
- average: float32 [288, 64, 768], P('batch', None, 'tensor')
- vector_state: float32 [4, 12, 768], replicated
Outputs:
- out: bfloat16 [32768, 768], P('batch')
- input_grad: float32 [32768, 768], P('batch')
- new_master: float32 [288, 64, 768], P('batch', None, 'tensor')
- new_first: float32 [288, 64, 768], P('batch', None, 'tensor')
- new_second: float32 [288, 64, 768], P('batch', None, 'tensor')
- new_average: float32 [288, 64, 768], P('batch', None, 'tensor')
- vector_out: float32 [2, 12, 768], replicated
- vector_grads_out: float32 [2, 12, 768], replicated
- vector_second: float32 [12, 768], replicated
The draws below stay inside these ranges and needn't reach their ends.
Inputs may be any that keep to these rules, and one draw needn't show every extreme that they name: `unit_slot`: distinct slots; slot s belongs to batch index s // 18; some batch index holds 18 blocks. `phase_of`: 1: the batch index's tokens form sequences of 512 tokens; 0: of 128. `learn_rates`: Positive.
All inputs are finite; a program needn't handle non-finite values.
Results may differ from the reference program's by a relative error of at most 0.012.
The reference program's roundings to bfloat16 on the way count: a program that leaves them out, or rounds other values in their place, can miss the bound.
Values may be sent and summed in bfloat16 or wider, within the bound.
No kernel may reach another device: no remote copies, remote signals or barrier semaphores. Data moves between devices by JAX's collectives and lax.ppermute only.
A program may use at most 192 MiB of HBM per device.

```python
import math
import jax
import jax.numpy as jnp
from jax import lax

D = 768
HEADS = 12
HD = 64
FF = 3072
SHORT = 128
LONG = 512
TOK_DEV = 2048
UROWS = 64
UCOLS = 384
UNITS = 144
CAP = 18
SLOTS = 288
TOKENS = 32768
N_BATCH = 16


def slot_table(key):
    base_key = jax.random.fold_in(key, 11)
    full_owner = jax.random.randint(jax.random.fold_in(base_key, 1), (), 0, SLOTS // CAP)
    slot_ranks = jax.random.permutation(jax.random.fold_in(base_key, 2), SLOTS)
    slot_ids = jnp.arange(SLOTS)
    priority = jnp.where(slot_ids // CAP == full_owner, 0, SLOTS) + slot_ranks
    chosen = jnp.argsort(priority)[:UNITS]
    unit_order = jax.random.permutation(jax.random.fold_in(base_key, 3), UNITS)
    return chosen[unit_order].astype(jnp.int32)


def slot_scales(key):
    slot_of = slot_table(key)
    row_blocks = D // UROWS
    unit_ids = jnp.arange(UNITS)
    kinds_unit = (unit_ids >= 3 * row_blocks).astype(jnp.int32) + (unit_ids >= 4 * row_blocks).astype(jnp.int32) + (unit_ids >= 4 * row_blocks + row_blocks * (FF // D)).astype(jnp.int32)
    weight_table = jnp.array([D ** (-0.5), 8.0 * D ** (-0.5), D ** (-0.5), FF ** (-0.5)], jnp.float32)
    grad_table = jnp.array([0.5, 0.08, 0.25, 0.5], jnp.float32) * TOKENS ** 0.5
    slot_kind = jnp.zeros((SLOTS,), jnp.int32).at[slot_of].set(kinds_unit)
    return (weight_table[slot_kind][:, None, None], grad_table[slot_kind][:, None, None])


def draw_unit_slot(key, part):
    return slot_table(key)


def draw_master(key, part):
    weight_scale, grad_scale = slot_scales(key)
    noise_all = jnp.clip(jax.random.normal(jax.random.fold_in(key, 21), (SLOTS, UROWS, D), jnp.float32), -6.0, 6.0)
    return noise_all * weight_scale


def draw_average(key, part):
    weight_scale, grad_scale = slot_scales(key)
    noise_all = jnp.clip(jax.random.normal(jax.random.fold_in(key, 22), (SLOTS, UROWS, D), jnp.float32), -6.0, 6.0)
    return noise_all * weight_scale


def draw_first_moment(key, part):
    weight_scale, grad_scale = slot_scales(key)
    noise_all = jnp.clip(jax.random.normal(jax.random.fold_in(key, 23), (SLOTS, UROWS, D), jnp.float32), -6.0, 6.0)
    return noise_all * grad_scale


def draw_second_moment(key, part):
    weight_scale, grad_scale = slot_scales(key)
    factor = jnp.exp(jax.random.uniform(jax.random.fold_in(key, 24), (SLOTS, UROWS, D), jnp.float32, 0.0, math.log(4.0)))
    return grad_scale * grad_scale * factor


def draw_learn_rates(key, part):
    base_rates = jnp.array([D ** (-0.5), 8.0 * D ** (-0.5), D ** (-0.5), FF ** (-0.5), 0.25], jnp.float32)
    return base_rates * jax.random.uniform(jax.random.fold_in(key, 31), (5,), jnp.float32, 0.5, 1.0)


def draw_vector_state(key, part):
    noise_all = jnp.clip(jax.random.normal(jax.random.fold_in(key, 41), (3, 12, D), jnp.float32), -6.0, 6.0)
    gain_rows = jnp.zeros((12,), jnp.float32).at[3].set(1.0).at[10].set(1.0)[:, None]
    grad_rows = jnp.array([0.6, 5.8, 0.73, 0.95, 0.95, 0.25, 0.25, 0.25, 0.25, 0.8, 1.0, 1.0], jnp.float32)[:, None]
    params = gain_rows + 0.1 * noise_all[0]
    average_rows = gain_rows + 0.1 * noise_all[1]
    moment = grad_rows * noise_all[2]
    factor = jnp.exp(jax.random.uniform(jax.random.fold_in(key, 42), (12, D), jnp.float32, 0.0, math.log(4.0)))
    square = grad_rows * grad_rows * factor
    return jnp.stack([params, moment, square, average_rows])


def set_ends(values, key, smallest, top_value):
    spot = [jax.random.randint(jax.random.fold_in(key, axis), (), 0, length) for axis, length in enumerate(values.shape)]
    longest = values.shape.index(max(values.shape))
    neighbour = spot[:longest] + [(spot[longest] + 1) % values.shape[longest]] + spot[longest + 1:]
    return values.at[tuple(spot)].set(smallest).at[tuple(neighbour)].set(top_value)


def level_of(key, extent, pieces, least, largest):
    def one(dim, parts):
        draws = jax.random.uniform(jax.random.fold_in(jax.random.fold_in(key, 6), dim), (parts,), jnp.float32, least / len(pieces), largest / len(pieces))
        return jnp.repeat(jnp.exp(draws), extent[dim] // parts).reshape((-1,) + (1,) * (len(extent) - dim - 1))

    level = one(*pieces[0])
    for cut in pieces[1:]:
        level = level * one(*cut)
    return level


def scatter_about(rng, dims, deviation, most, cuts=(), kind=jnp.bfloat16):
    values = jax.random.normal(rng, dims, jnp.float32) * deviation
    if len(cuts) > 0:
        values = level_of(rng, dims, cuts, -0.22, 0.18) * values
    return jnp.clip(values, min=-most, max=most).astype(kind)


def setup_inputs(seed: int = 0) -> dict:
    splits = jax.random.split(jax.random.key(seed), 13)
    return {
        "tokens": scatter_about(splits[0], (TOKENS, D), 1.0, 6.0, ((0, 16),)),
        "cotangent": scatter_about(splits[1], (TOKENS, D), 1.0, 6.0, ((0, 16),)),
        "phase_of": set_ends(jax.random.randint(splits[2], (N_BATCH,), 0, 2), jax.random.fold_in(splits[2], 1), 0, 1).astype(jnp.int32),
        "unit_slot": draw_unit_slot(jax.random.fold_in(splits[12], 71), 0),
        "step_count": jax.random.randint(splits[4], (1,), 2, 9).astype(jnp.int32),
        "learn_rates": draw_learn_rates(jax.random.fold_in(splits[12], 71), 0),
        "decay_rates": jnp.clip(jax.random.uniform(splits[6], (3,), jnp.float32, 0.5, 0.7), 0.5, 0.7),
        "master": draw_master(jax.random.fold_in(splits[12], 71), 0),
        "first_moment": draw_first_moment(jax.random.fold_in(splits[12], 71), 0),
        "second_moment": draw_second_moment(jax.random.fold_in(splits[12], 71), 0),
        "average": draw_average(jax.random.fold_in(splits[12], 71), 0),
        "vector_state": draw_vector_state(jax.random.fold_in(splits[12], 71), 0),
    }


@jax.custom_vjp
def low(v):
    return lax.optimization_barrier(v.astype(jnp.bfloat16)).astype(jnp.float32)

@jax.custom_vjp
def low_back(v):
    return v

def low_keep(v):
    return (low(v), None)

def low_pass(kept, grad):
    return (grad,)

def back_keep(v):
    return (v, None)

def back_low(kept, grad):
    return (low(grad),)
low.defvjp(low_keep, low_pass)
low_back.defvjp(back_keep, back_low)

def product(first_mat, second_mat):
    return jnp.dot(first_mat, second_mat, precision=lax.Precision.HIGHEST)

def layer_norm(centre_in, gain_row, shift_row):
    mean_rows = lax.optimization_barrier(jnp.mean(centre_in, axis=-1, keepdims=True))
    centred = centre_in - mean_rows
    variance = lax.optimization_barrier(jnp.mean(centred * centred, axis=-1, keepdims=True))
    return centred * lax.rsqrt(variance + 1e-12) * gain_row + shift_row

def unpack(unit_blocks):
    row_blocks = D // UROWS
    col_blocks = FF // D

    def stacked(first_unit):
        return unit_blocks[first_unit:first_unit + row_blocks].reshape(D, D)

    def widened(first_unit):
        blocks = unit_blocks[first_unit:first_unit + row_blocks * col_blocks]
        blocks = blocks.reshape(row_blocks, col_blocks, UROWS, 2, UCOLS)
        return blocks.transpose(0, 2, 3, 1, 4).reshape(D, FF)
    return (stacked(0), stacked(row_blocks), stacked(2 * row_blocks), stacked(3 * row_blocks), widened(4 * row_blocks), widened(4 * row_blocks + row_blocks * col_blocks))

def attend_group(queries, keys_in, values, phase_flag):
    scores = jnp.einsum('qhd,khd->hqk', queries, keys_in, precision=lax.Precision.HIGHEST) * HD ** (-0.5)
    scores = low_back(scores)
    seq_span = jnp.where(phase_flag == 1, jnp.int32(LONG), jnp.int32(SHORT))
    position = jnp.arange(LONG, dtype=jnp.int32)
    same_seq = position[:, None] // seq_span == position[None, :] // seq_span
    scores = jnp.where(same_seq[None], scores, -1e+30)
    weights = low(jax.nn.softmax(scores, axis=-1))
    return jnp.einsum('hqk,khd->qhd', weights, values, precision=lax.Precision.HIGHEST)

def forward_pass(inputs, unit_blocks, vectors, group_flags):
    w_query, w_key, w_value, w_out, w_up, w_down = [low(matrix) for matrix in unpack(unit_blocks)]
    queries = low(low_back(product(inputs, w_query) + vectors[0]))
    keys_all = low(low_back(product(inputs, w_key)))
    values = low(low_back(product(inputs, w_value) + vectors[1]))
    head_shape = (TOKENS // LONG, LONG, HEADS, HD)
    context = lax.map(jax.checkpoint(lambda operands: attend_group(*operands)), (queries.reshape(head_shape), keys_all.reshape(head_shape), values.reshape(head_shape), group_flags))
    context = low(low_back(context.reshape(TOKENS, D)))
    attended = low_back(product(context, w_out.T))
    hidden_one = layer_norm(inputs + attended + vectors[2], vectors[3], vectors[4])
    upper_in = low_back(product(low(hidden_one), w_up) + vectors[5:9].reshape(FF))
    activated = low(jax.nn.gelu(upper_in, approximate=False))
    branch = low_back(product(activated, w_down.T))
    return layer_norm(hidden_one + branch + vectors[9], vectors[10], vectors[11])

def adamw_update(weights_in, moment, square, average_in, gradient, rate_all, decay_rates, step_count):
    count_f = step_count[0].astype(jnp.float32)
    beta_one = decay_rates[0]
    beta_two = decay_rates[1]
    ema_decay = decay_rates[2]
    moment_new = beta_one * moment + (1.0 - beta_one) * gradient
    square_new = beta_two * square + (1.0 - beta_two) * gradient * gradient
    moment_hat = moment_new / (1.0 - beta_one ** count_f)
    square_hat = square_new / (1.0 - beta_two ** count_f)
    weights_new = weights_in - rate_all * (moment_hat / (jnp.sqrt(square_hat) + 1e-08) + 0.01 * weights_in)
    average_new = ema_decay * average_in + (1.0 - ema_decay) * weights_new
    return (weights_new, moment_new, square_new, average_new)

def slot_kinds(unit_slot):
    row_blocks = D // UROWS
    unit_ids = jnp.arange(UNITS, dtype=jnp.int32)
    kinds_unit = (unit_ids >= 3 * row_blocks).astype(jnp.int32) + (unit_ids >= 4 * row_blocks).astype(jnp.int32) + (unit_ids >= 4 * row_blocks + row_blocks * (FF // D)).astype(jnp.int32)
    return jnp.zeros((SLOTS,), jnp.int32).at[unit_slot].set(kinds_unit)

def reference(tokens, cotangent, phase_of, unit_slot, step_count, learn_rates, decay_rates, master, first_moment, second_moment, average, vector_state):
    unit_blocks = master[unit_slot]
    inputs = tokens.astype(jnp.float32)
    group_flags = jnp.repeat(phase_of, TOK_DEV // LONG)
    output_f, pull_back = jax.vjp(lambda inputs_in, blocks_in, vectors_in: forward_pass(inputs_in, blocks_in, vectors_in, group_flags), inputs, unit_blocks, vector_state[0])
    input_grad, unit_grads, vector_grads = pull_back(cotangent.astype(jnp.float32))
    slot_grads = jnp.zeros_like(master).at[unit_slot].set(unit_grads)
    slot_rates = learn_rates[slot_kinds(unit_slot)][:, None, None]
    new_master, new_first, new_second, new_average = adamw_update(master, first_moment, second_moment, average, slot_grads, slot_rates, decay_rates, step_count)
    grads_scaled = vector_grads * float(TOKENS) ** (-0.5)
    vec_weights, vec_first, vec_second, vec_average = adamw_update(vector_state[0], vector_state[1], vector_state[2], vector_state[3], grads_scaled, learn_rates[4], decay_rates, step_count)
    return (output_f.astype(jnp.bfloat16), input_grad, new_master, new_first, new_second, new_average, jnp.stack([vec_weights, vec_average]), jnp.stack([grads_scaled, vec_first]), vec_second)
```

```python
import functools

import jax
import jax.numpy as jnp
from jax import lax
from jax.experimental import pallas as pl
from jax.experimental.pallas import tpu as pltpu
from jax.sharding import PartitionSpec as P

HD = 64
FF = 3072
SHORT = 128
LONG = 512
EPS = 1e-12
BF = jnp.bfloat16
F32 = jnp.float32
VMEM_BYTES = 60 * 2**20
BOTH = ("batch", "tensor")
ANY = pl.BlockSpec(memory_space=pl.ANY)
PLANES = 4
FAST_BATCH = 16


def dot(first_mat, second_mat):
    return lax.dot_general(
        first_mat, second_mat, (((1,), (0,)), ((), ())), preferred_element_type=F32
    )


def dot_nt(first_mat, second_mat):
    return lax.dot_general(
        first_mat, second_mat, (((1,), (1,)), ((), ())), preferred_element_type=F32
    )


def normalized(rows):
    centred = rows - jnp.mean(rows, axis=-1, keepdims=True)
    inverse = lax.rsqrt(jnp.mean(centred * centred, axis=-1, keepdims=True) + EPS)
    return centred * inverse, inverse


def norm_back(grad_scaled, normal, inverse):
    mean_grad = jnp.mean(grad_scaled, axis=-1, keepdims=True)
    mean_both = jnp.mean(grad_scaled * normal, axis=-1, keepdims=True)
    return inverse * (grad_scaled - mean_grad - normal * mean_both)


def row_sum(array_in):
    return jnp.sum(array_in, axis=0, keepdims=True)


def load_blocks(mine_ref, theirs_ref, blocks, weight_ref, sem_ref):
    cols = mine_ref.shape[2]
    copies = []
    for spot, (half, block) in enumerate(blocks):
        source = (mine_ref, theirs_ref)[half]
        copies.append(
            pltpu.make_async_copy(
                source.at[block],
                weight_ref.at[:, pl.ds(spot * cols, cols)],
                sem_ref.at[spot],
            )
        )
    return copies


PAIRED = [(half, block) for block in range(4) for half in range(2)]
HALVED = [(half, block) for half in range(2) for block in range(4)]


def call(kernel, grid, in_specs, out_specs, out_shape, scratch, prefetch, flops, moved, exps=0):
    return pl.pallas_call(
        kernel,
        out_shape=out_shape,
        grid_spec=pltpu.PrefetchScalarGridSpec(
            num_scalar_prefetch=prefetch,
            grid=grid,
            in_specs=in_specs,
            out_specs=out_specs,
            scratch_shapes=scratch,
        ),
        compiler_params=pltpu.CompilerParams(vmem_limit_bytes=VMEM_BYTES),
        cost_estimate=pl.CostEstimate(
            flops=flops, bytes_accessed=moved, transcendentals=exps
        ),
    )


def struct(shape, kind):
    return jax.ShapeDtypeStruct(shape, kind)


def spread_kernel(base, row_step, block_step, cap, rows, info_ref, slot_ref, master_ref, *outs):
    block = pl.program_id(0)
    for out_ref, half in zip(outs, (1 - info_ref[0], info_ref[0])):
        count = out_ref.shape[1] // rows
        for step in range(count):
            unit = base + (half * count + step) * row_step + block * block_step
            local = slot_ref[unit] - info_ref[1]
            own = (local >= 0) & (local < cap)
            spot = pl.ds(step * rows, rows)

            @pl.when(own)
            def _():
                out_ref[0, spot, :] = master_ref[local].astype(BF)

            @pl.when(jnp.logical_not(own))
            def _():
                out_ref[0, spot, :] = jnp.zeros((rows, out_ref.shape[2]), BF)


def spread(master, unit_slot, info, chunk):
    cap, rows, cols = master.shape
    base, row_step, block_step = chunk
    half_rows = 6 * rows
    shape = struct((4, half_rows, cols), BF)
    block = pl.BlockSpec((1, half_rows, cols), lambda i, *_: (i, 0, 0))
    return call(
        functools.partial(spread_kernel, base, row_step, block_step, cap, rows),
        (4,),
        [pl.BlockSpec((cap, rows, cols), lambda i, *_: (0, 0, 0))],
        [block, block],
        [shape, shape],
        [],
        2,
        0,
        8 * 2**20,
    )(info, unit_slot, master)


def swap_pairs(orient, stage):
    pairs = []
    for place in range(FAST_BATCH):
        for core in range(2):
            first_bit = 2 if (core + orient) % 2 == 0 else 1
            bit = first_bit if stage == 1 else 3 - first_bit
            pairs.append((place * 2 + core, (place ^ bit) * 2 + core))
    return pairs


def plane_pairs(step):
    return [
        (place * 2 + core, (place + 4 * step) % FAST_BATCH * 2 + core)
        for place in range(FAST_BATCH)
        for core in range(2)
    ]


def cut(array_in, start, size):
    return lax.dynamic_slice_in_dim(array_in, start, size, 1)


def total(*terms):
    result = terms[0].astype(F32)
    for term in terms[1:]:
        result = result + term.astype(F32)
    return result.astype(BF)


def packed(parts):
    if len(parts) == 1:
        return parts[0]
    return jnp.concatenate([part.reshape(-1, part.shape[2]) for part in parts], axis=0)


def unpacked(array_in, likes):
    if len(likes) == 1:
        return [array_in]
    at, parts = 0, []
    for like in likes:
        count = like.shape[0] * like.shape[1]
        parts.append(array_in[at : at + count].reshape(like.shape))
        at += count
    return parts


def send(parts, pairs):
    return unpacked(lax.ppermute(packed(parts), BOTH, pairs), parts)


def reduce_parts(sends, keeps, orient, where):
    first_at, second_at, plane = where
    got_one = send(sends, swap_pairs(orient, 1))
    halves = [keep.shape[1] // 2 for keep in keeps]
    outgoing = [
        total(cut(keep, (1 - second_at) * half, half), cut(one, (1 - second_at) * half, half))
        for keep, one, half in zip(keeps, got_one, halves)
    ]
    got_two = send(outgoing, swap_pairs(orient, 2))

    def local(which):
        return [
            (
                cut(keep, second_at * half + which * (half // PLANES), half // PLANES),
                cut(one, second_at * half + which * (half // PLANES), half // PLANES),
                cut(two, which * (half // PLANES), half // PLANES),
            )
            for keep, one, two, half in zip(keeps, got_one, got_two, halves)
        ]

    arrived = []
    for step in range(1, PLANES):
        pieces = [total(*terms) for terms in local((plane + step) % PLANES)]
        arrived.append(send(pieces, plane_pairs(step)))
    return [
        total(*terms, *[pieces[at] for pieces in arrived])
        for at, terms in enumerate(local(plane))
    ]


def join(flag, here, there):
    low_first = flag == 0
    return jnp.concatenate(
        [jnp.where(low_first, here, there), jnp.where(low_first, there, here)], axis=1
    )


def gather_parts(owned, orient, where):
    first_at, second_at, plane = where
    pieces = [owned] + [send(owned, plane_pairs(step)) for step in range(1, PLANES)]
    level = []
    for at in range(len(owned)):
        choices = [piece[at] for piece in pieces]
        level.append(
            jnp.concatenate(
                [
                    lax.select_n((plane - row) % PLANES, *choices)
                    for row in range(PLANES)
                ],
                axis=1,
            )
        )
    level = [
        join(second_at, here, there)
        for here, there in zip(level, send(level, swap_pairs(orient, 2)))
    ]
    return [
        join(first_at, here, there)
        for here, there in zip(level, send(level, swap_pairs(orient, 1)))
    ]


def core_swap(array_in):
    return lax.ppermute(array_in, "tensor", [(0, 1), (1, 0)])


def seen_mask():
    key_at = lax.broadcasted_iota(jnp.int32, (LONG, LONG), 0) // SHORT
    query_at = lax.broadcasted_iota(jnp.int32, (LONG, LONG), 1) // SHORT
    return key_at == query_at


def low_lanes(rows):
    return lax.broadcasted_iota(jnp.int32, (rows, 2 * HD), 1) < HD


def pair_lanes(pair):
    return pl.ds(pl.multiple_of(pair * 2 * HD, 2 * HD), 2 * HD)


def head_part(array_in, head):
    lanes = low_lanes(array_in.shape[0])
    keep = lanes if head == 0 else jnp.logical_not(lanes)
    return jnp.where(keep, array_in, jnp.zeros_like(array_in))


def attend_pair(pair, short, q_ref, k_ref, v_ref, ctx_ref, lse_ref):
    lanes = pair_lanes(pair)
    queries = q_ref[:, lanes] * BF(HD**-0.5)
    keys_here = k_ref[:, lanes]
    values_t = v_ref[:, lanes].T
    outs = []
    for head in range(2):
        scores = dot_nt(head_part(keys_here, head), queries)
        if short:
            scores = jnp.where(seen_mask(), scores, -1e30)
        top = jnp.max(scores, axis=0, keepdims=True)
        weights = jnp.exp(scores - top)
        norm = jnp.sum(weights, axis=0, keepdims=True)
        probs = (weights * (1.0 / norm)).astype(BF)
        outs.append(dot(values_t[head * HD : (head + 1) * HD], probs))
        lse_ref[0, pl.ds(pair * 2 + head, 1), :] = top + jnp.log(norm)
    ctx_ref[:, lanes] = jnp.concatenate(outs, axis=0).T.astype(BF)


def forward_kernel(
    info_ref, x_ref, rows_ref, mine_ref, theirs_ref,
    q_ref, k_ref, v_ref, ctx_ref, lse_ref, z_ref, xt_ref, w_ref, sem_ref,
):
    width = x_ref.shape[1]

    @pl.when(pl.program_id(0) == 0)
    def _():
        copies = load_blocks(mine_ref, theirs_ref, PAIRED, w_ref, sem_ref)
        for copy in copies:
            copy.start()
        for copy in copies:
            copy.wait()

    tokens = x_ref[...]
    q_ref[...] = (dot(tokens, w_ref[:, :width]) + rows_ref[0:1]).astype(BF)
    k_ref[...] = dot(tokens, w_ref[:, width : 2 * width]).astype(BF)
    v_ref[...] = (dot(tokens, w_ref[:, 2 * width : 3 * width]) + rows_ref[1:2]).astype(BF)
    xt_ref[...] = tokens.T
    pairs = width // (2 * HD)

    def all_pairs(short):
        @pl.loop(0, pairs)
        def _(pair):
            attend_pair(pair, short, q_ref, k_ref, v_ref, ctx_ref, lse_ref)

    @pl.when(info_ref[0] == 1)
    def _():
        all_pairs(False)

    @pl.when(info_ref[0] != 1)
    def _():
        all_pairs(True)

    attended = dot_nt(ctx_ref[...], w_ref[:, 3 * width :])
    z_ref[...] = tokens.astype(F32) + attended + rows_ref[2:3]


def forward(info, tokens, rows, mine, theirs):
    tok = tokens.shape[0] // 2
    width = tokens.shape[1]
    groups = tok // LONG
    tile = pl.BlockSpec((LONG, width), lambda i, *_: (i, 0))
    low = struct((tok, width), BF)
    return call(
        forward_kernel,
        (groups,),
        [
            pl.BlockSpec((LONG, width), lambda i, info: (info[1] * groups + i, 0)),
            pl.BlockSpec((8, width), lambda i, *_: (0, 0)),
            ANY,
            ANY,
        ],
        [
            tile, tile, tile, tile,
            pl.BlockSpec((1, 16, LONG), lambda i, *_: (i, 0, 0)),
            tile,
            pl.BlockSpec((width, LONG), lambda i, *_: (0, i)),
        ],
        [
            low, low, low, low,
            struct((groups, 16, LONG), F32),
            struct((tok, width), F32),
            struct((width, tok), BF),
        ],
        [pltpu.VMEM((width, 4 * width), BF), pltpu.SemaphoreType.DMA((8,))],
        1,
        2 * tok * width * (4 * width + 2 * LONG) * 2,
        20 * 2**20,
        tok * LONG * 12,
    )(info, tokens, rows, mine, theirs)


def up_kernel(z_ref, rows_ref, bias_ref, mine_ref, theirs_ref, act_ref, slope_ref, ht_ref, w_ref, sem_ref):
    width = z_ref.shape[1]

    @pl.when(pl.program_id(0) == 0)
    def _():
        copies = load_blocks(mine_ref, theirs_ref, HALVED, w_ref, sem_ref)
        for copy in copies:
            copy.start()
        for copy in copies:
            copy.wait()

    normal, _ = normalized(z_ref[...])
    low = (normal * rows_ref[3:4] + rows_ref[4:5]).astype(BF)
    ht_ref[...] = low.T
    for part in range(FF // width):
        spot = slice(part * width, (part + 1) * width)
        upper = dot(low, w_ref[:, spot]) + bias_ref[part : part + 1]
        phi_sum = 0.5 + 0.5 * lax.erf(upper * (0.5**0.5))
        density = jnp.exp(-0.5 * upper * upper) * 0.3989422804014327
        act_ref[:, spot] = (upper * phi_sum).astype(BF)
        slope_ref[:, spot] = (phi_sum + upper * density).astype(BF)


TILE = 256


def feed_up(first, rows, bias, mine, theirs):
    tok, width = first.shape
    wide = struct((tok, FF), BF)
    return call(
        up_kernel,
        (tok // TILE,),
        [
            pl.BlockSpec((TILE, width), lambda i: (i, 0)),
            pl.BlockSpec((8, width), lambda i: (0, 0)),
            pl.BlockSpec((4, width), lambda i: (0, 0)),
            ANY,
            ANY,
        ],
        [
            pl.BlockSpec((TILE, FF), lambda i: (i, 0)),
            pl.BlockSpec((TILE, FF), lambda i: (i, 0)),
            pl.BlockSpec((width, TILE), lambda i: (0, i)),
        ],
        [wide, wide, struct((width, tok), BF)],
        [pltpu.VMEM((width, FF), BF), pltpu.SemaphoreType.DMA((8,))],
        0,
        2 * tok * width * FF,
        20 * 2**20,
        tok * FF * 2,
    )(first, rows, bias, mine, theirs)


def split_grad(grad, width, mine_ref, theirs_ref):
    cols = mine_ref.shape[2]
    for ref in (mine_ref, theirs_ref):
        for block in range(ref.shape[0]):
            ref[block] = grad[:, block * cols : (block + 1) * cols].astype(BF)


def down_kernel(
    info_ref, z_ref, act_ref, cot_ref, rows_ref, mine_ref, theirs_ref,
    out_ref, dz_ref, gm_ref, gt_ref, sum_ref, w_ref, dyt_ref, sem_ref,
):
    step = pl.program_id(0)
    width = z_ref.shape[1]
    tiles = act_ref.shape[0] // TILE

    @pl.when(step == 0)
    def _():
        copies = load_blocks(mine_ref, theirs_ref, HALVED, w_ref, sem_ref)
        for copy in copies:
            copy.start()
        sum_ref[...] = jnp.zeros_like(sum_ref)
        for copy in copies:
            copy.wait()

    @pl.when(step < tiles)
    def _():
        spot = pl.ds(pl.multiple_of(step * TILE, TILE), TILE)
        branch = dot_nt(act_ref[spot, :], w_ref[...])
        normal, _ = normalized(z_ref[...])
        hidden = normal * rows_ref[3:4] + rows_ref[4:5]
        normal_two, inverse = normalized(hidden + branch + rows_ref[5:6])
        out_ref[...] = (normal_two * rows_ref[6:7] + rows_ref[7:8]).astype(BF)
        cot = cot_ref[...].astype(F32)
        grad = norm_back(cot * rows_ref[6:7], normal_two, inverse)
        dz_ref[...] = grad
        dyt_ref[:, spot] = grad.astype(BF).T
        sum_ref[0:1] += row_sum(grad)
        sum_ref[1:2] += row_sum(cot * normal_two)
        sum_ref[2:3] += row_sum(cot)

    for part in range(4):
        @pl.when(step == tiles + part)
        def _():
            spot = slice((part ^ 2) * width, ((part ^ 2) + 1) * width)
            grad = dot(dyt_ref[...], act_ref[:, spot])
            ref = gt_ref if part < 2 else gm_ref
            cols = ref.shape[2]
            for block in range(2):
                ref[block] = grad[:, block * cols : (block + 1) * cols].astype(BF)


def grad_specs(tiles, width):
    cols = width // 2
    mine = pl.BlockSpec((2, width, cols), lambda i, *_: (jnp.clip(i - tiles - 2, 0, 1), 0, 0))
    theirs = pl.BlockSpec((2, width, cols), lambda i, *_: (jnp.clip(i - tiles, 0, 1), 0, 0))
    return [mine, theirs]


def feed_down(info, first, act, cot, rows, mine, theirs):
    tok, width = first.shape
    tiles = tok // TILE
    last = tiles - 1
    row_tile = pl.BlockSpec((TILE, width), lambda i, *_: (jnp.minimum(i, last), 0))
    grads = struct((4, width, width // 2), BF)
    return call(
        down_kernel,
        (tiles + 4,),
        [
            row_tile,
            pl.BlockSpec((tok, FF), lambda i, *_: (0, 0)),
            pl.BlockSpec(
                (TILE, width), lambda i, info: (info[1] * tiles + jnp.minimum(i, last), 0)
            ),
            pl.BlockSpec((8, width), lambda i, *_: (0, 0)),
            ANY,
            ANY,
        ],
        [row_tile, row_tile]
        + grad_specs(tiles, width)
        + [pl.BlockSpec((8, width), lambda i, *_: (0, 0))],
        [struct((tok, width), BF), struct((tok, width), F32), grads, grads, struct((8, width), F32)],
        [
            pltpu.VMEM((width, FF), BF),
            pltpu.VMEM((width, tok), BF),
            pltpu.SemaphoreType.DMA((8,)),
        ],
        1,
        4 * tok * width * FF,
        30 * 2**20,
    )(info, first, act, cot, rows, mine, theirs)


def back_kernel(
    z_ref, dz2_ref, slope_ref, ht_ref, rows_ref, dm_ref, dt_ref, um_ref, ut_ref, om_ref, ot_ref,
    dz1_ref, dctx_ref, dtt_ref, gm_ref, gt_ref, sum_ref,
    wd_ref, wu_ref, wo_ref, da_ref, dsem_ref, usem_ref, osem_ref,
):
    step = pl.program_id(0)
    width = z_ref.shape[1]
    tiles = da_ref.shape[0] // TILE

    @pl.when(step == 0)
    def _():
        copies = load_blocks(dm_ref, dt_ref, HALVED, wd_ref, dsem_ref)
        copies += load_blocks(um_ref, ut_ref, HALVED, wu_ref, usem_ref)
        copies += load_blocks(om_ref, ot_ref, [(0, 3), (1, 3)], wo_ref, osem_ref)
        for copy in copies:
            copy.start()
        sum_ref[...] = jnp.zeros_like(sum_ref)
        for copy in copies:
            copy.wait()

    @pl.when(step < tiles)
    def _():
        spot = pl.ds(pl.multiple_of(step * TILE, TILE), TILE)
        grad_two = dz2_ref[...]
        low_two = grad_two.astype(BF)
        grad_hidden = grad_two
        for part in range(FF // width):
            lanes = slice(part * width, (part + 1) * width)
            grad_act = dot(low_two, wd_ref[:, lanes])
            grad_up = (grad_act * slope_ref[:, lanes].astype(F32)).astype(BF)
            da_ref[spot, lanes] = grad_up
            sum_ref[4 + part : 5 + part] += row_sum(grad_up.astype(F32))
            grad_hidden = grad_hidden + dot_nt(grad_up, wu_ref[:, lanes])
        normal, inverse = normalized(z_ref[...])
        grad_one = norm_back(grad_hidden * rows_ref[3:4], normal, inverse)
        sum_ref[0:1] += row_sum(grad_one)
        sum_ref[1:2] += row_sum(grad_hidden * normal)
        sum_ref[2:3] += row_sum(grad_hidden)
        dz1_ref[...] = grad_one
        low_one = grad_one.astype(BF)
        dtt_ref[...] = low_one.T
        dctx_ref[...] = dot(low_one, wo_ref[...]).astype(BF)

    for part in range(4):
        @pl.when(step == tiles + part)
        def _():
            spot = slice((part ^ 2) * width, ((part ^ 2) + 1) * width)
            grad = dot(ht_ref[...], da_ref[:, spot])
            ref = gt_ref if part < 2 else gm_ref
            cols = ref.shape[2]
            for block in range(2):
                ref[block] = grad[:, block * cols : (block + 1) * cols].astype(BF)


def feed_back(first, dz2, slope, hidden_t, rows, down, upper, other):
    tok, width = first.shape
    tiles = tok // TILE
    last = tiles - 1
    row_tile = pl.BlockSpec((TILE, width), lambda i: (jnp.minimum(i, last), 0))
    grads = struct((4, width, width // 2), BF)
    return call(
        back_kernel,
        (tiles + 4,),
        [
            row_tile,
            row_tile,
            pl.BlockSpec((TILE, FF), lambda i: (jnp.minimum(i, last), 0)),
            pl.BlockSpec((width, tok), lambda i: (0, 0)),
            pl.BlockSpec((8, width), lambda i: (0, 0)),
        ]
        + [ANY] * 6,
        [row_tile, row_tile, pl.BlockSpec((width, TILE), lambda i: (0, jnp.minimum(i, last)))]
        + grad_specs(tiles, width)
        + [pl.BlockSpec((8, width), lambda i: (0, 0))],
        [
            struct((tok, width), F32),
            struct((tok, width), BF),
            struct((width, tok), BF),
            grads,
            grads,
            struct((8, width), F32),
        ],
        [
            pltpu.VMEM((width, FF), BF),
            pltpu.VMEM((width, FF), BF),
            pltpu.VMEM((width, width), BF),
            pltpu.VMEM((tok, FF), BF),
            pltpu.SemaphoreType.DMA((8,)),
            pltpu.SemaphoreType.DMA((8,)),
            pltpu.SemaphoreType.DMA((2,)),
        ],
        0,
        6 * tok * width * FF,
        40 * 2**20,
    )(first, dz2, slope, hidden_t, rows, *down, *upper, *other)


def attend_pair_back(pair, short, base, q_ref, k_ref, v_ref, dctx_ref, lse_ref, dqkv_ref):
    width = q_ref.shape[1]
    lanes = pair_lanes(pair)
    queries = q_ref[:, lanes] * BF(HD**-0.5)
    keys_here = k_ref[:, lanes]
    values = v_ref[:, lanes]
    grads = dctx_ref[:, lanes]
    keys_t = keys_here.T
    grad_q, grad_k, grad_v = [], [], []
    for head in range(2):
        scores = dot_nt(head_part(keys_here, head), queries)
        if short:
            scores = jnp.where(seen_mask(), scores, -1e30)
        probs = jnp.exp(scores - lse_ref[0, pl.ds(pair * 2 + head, 1), :])
        grad_probs = dot_nt(head_part(values, head), grads)
        inner = jnp.sum(probs * grad_probs, axis=0, keepdims=True)
        grad_scores = (probs * (grad_probs - inner)).astype(BF)
        grad_k.append(dot(grad_scores, queries))
        grad_v.append(dot(probs.astype(BF), grads))
        grad_q.append(dot(keys_t[head * HD : (head + 1) * HD], grad_scores))
    low = low_lanes(LONG)
    rows = pl.ds(pl.multiple_of(base, LONG), LONG)

    def store(part, values_in):
        spot = pl.ds(pl.multiple_of(part * width + pair * 2 * HD, 2 * HD), 2 * HD)
        dqkv_ref[rows, spot] = values_in.astype(BF)

    store(0, jnp.concatenate(grad_q, axis=0).T * HD**-0.5)
    store(1, jnp.where(low, grad_k[0], grad_k[1]))
    store(2, jnp.where(low, grad_v[0], grad_v[1]))


def attend_back_kernel(
    info_ref, q_ref, k_ref, v_ref, dctx_ref, lse_ref, dz_ref, xt_ref, dtt_ref, ctx_ref,
    mine_ref, theirs_ref, gm_ref, gt_ref, gx_ref, sum_ref, w_ref, dqkv_ref, sem_ref,
):
    step = pl.program_id(0)
    width = q_ref.shape[1]
    groups = dqkv_ref.shape[0] // LONG
    cols = gm_ref.shape[2]

    @pl.when(step == 0)
    def _():
        copies = load_blocks(mine_ref, theirs_ref, PAIRED[:6], w_ref, sem_ref)
        for copy in copies:
            copy.start()
        sum_ref[...] = jnp.zeros_like(sum_ref)
        for copy in copies:
            copy.wait()

    def all_pairs(short):
        @pl.loop(0, width // (2 * HD))
        def _(pair):
            attend_pair_back(
                pair, short, step * LONG, q_ref, k_ref, v_ref, dctx_ref, lse_ref, dqkv_ref
            )

    @pl.when((step < groups) & (info_ref[0] == 1))
    def _():
        all_pairs(False)

    @pl.when((step < groups) & (info_ref[0] != 1))
    def _():
        all_pairs(True)

    @pl.when(step < groups)
    def _():
        rows = pl.ds(pl.multiple_of(step * LONG, LONG), LONG)
        grads = dqkv_ref[rows, :]
        gx_ref[...] = (dz_ref[...] + dot_nt(grads, w_ref[...])).astype(BF)
        sum_ref[0:1] += row_sum(dqkv_ref[rows, :width].astype(F32))
        sum_ref[1:2] += row_sum(dqkv_ref[rows, 2 * width :].astype(F32))

    def put(grad):
        gm_ref[0] = grad[:, :cols].astype(BF)
        gt_ref[0] = grad[:, cols:].astype(BF)

    for part in range(3):
        @pl.when(step == groups + part)
        def _():
            put(dot(xt_ref[...], dqkv_ref[:, part * width : (part + 1) * width]))

    @pl.when(step == groups + 3)
    def _():
        put(dot(dtt_ref[...], ctx_ref[...]))


def attend_back(info, q, k, v, dctx, lse, dz, x_t, dt_t, ctx, mine, theirs):
    tok, width = q.shape
    groups = tok // LONG
    last = groups - 1
    tile = pl.BlockSpec((LONG, width), lambda i, *_: (jnp.minimum(i, last), 0))
    whole = pl.BlockSpec((width, tok), lambda i, *_: (0, 0))
    block = pl.BlockSpec((1, width, width // 2), lambda i, *_: (jnp.clip(i - groups, 0, 3), 0, 0))
    grads = struct((4, width, width // 2), BF)
    return call(
        attend_back_kernel,
        (groups + 4,),
        [
            tile, tile, tile, tile,
            pl.BlockSpec((1, 16, LONG), lambda i, *_: (jnp.minimum(i, last), 0, 0)),
            tile, whole, whole,
            pl.BlockSpec((tok, width), lambda i, *_: (0, 0)),
            ANY, ANY,
        ],
        [block, block, tile, pl.BlockSpec((8, width), lambda i, *_: (0, 0))],
        [grads, grads, struct((tok, width), BF), struct((8, width), F32)],
        [
            pltpu.VMEM((width, 3 * width), BF),
            pltpu.VMEM((tok, 3 * width), BF),
            pltpu.SemaphoreType.DMA((6,)),
        ],
        1,
        2 * tok * width * (7 * width + 5 * LONG),
        30 * 2**20,
        tok * LONG * 12,
    )(info, q, k, v, dctx, lse, dz, x_t, dt_t, ctx, mine, theirs)


def adamw_update(weights_in, moment, square, average_in, gradient, rate, scalars):
    beta_one, beta_two, ema_decay, scale_one, scale_two = scalars
    moment_new = beta_one * moment + (1.0 - beta_one) * gradient
    square_new = beta_two * square + (1.0 - beta_two) * gradient * gradient
    moment_hat = moment_new * scale_one
    square_hat = square_new * scale_two
    weights_new = weights_in - rate * (
        moment_hat / (jnp.sqrt(square_hat) + 1e-08) + 0.01 * weights_in
    )
    average_new = ema_decay * average_in + (1.0 - ema_decay) * weights_new
    return weights_new, moment_new, square_new, average_new


def adamw_kernel(table_ref, scale_ref, w_ref, m_ref, s_ref, a_ref, *refs):
    slot = pl.program_id(0)
    grads, outs = refs[:3], refs[3:]
    chunk = table_ref[0, slot]
    gradient = jnp.zeros(w_ref.shape[1:], F32)
    for at, ref in enumerate(grads):
        gradient = gradient + ref[0].astype(F32) * jnp.where(chunk == at, 1.0, 0.0)
    results = adamw_update(
        w_ref[0], m_ref[0], s_ref[0], a_ref[0], gradient,
        scale_ref[8 + slot], [scale_ref[at] for at in range(5)],
    )
    for ref, value in zip(outs, results):
        ref[0] = value


def adamw_slots(table, scales, states, grads):
    cap, rows, cols = states[0].shape
    own = pl.BlockSpec((1, rows, cols), lambda i, *_: (i, 0, 0))

    def chosen(at):
        def index(i, table, scales):
            here = table[0, i] == at
            return jnp.where(here, table[1, i], 0), jnp.where(here, table[2, i], 0), 0

        return pl.BlockSpec((1, rows, cols), index)

    return call(
        adamw_kernel,
        (cap,),
        [own] * 4 + [chosen(at) for at in range(3)],
        [own] * 4,
        [struct(states[0].shape, F32)] * 4,
        [],
        2,
        20 * cap * rows * cols,
        40 * cap * rows * cols,
    )(table, scales, *states, *grads)


def on_device(
    tokens,
    cotangent,
    phase_of,
    unit_slot,
    step_count,
    learn_rates,
    decay_rates,
    master,
    first_moment,
    second_moment,
    average,
    vector_state,
):
    cap, unit_rows, cols = master.shape
    tok_rows, width = tokens.shape
    batch_count = lax.axis_size("batch")
    row_blocks = width // unit_rows
    col_blocks = FF // width
    core = lax.axis_index("tensor")
    place = lax.axis_index("batch")
    fast = batch_count == FAST_BATCH
    plane, y_at, x_at = place // 4, (place // 2) % 2, place % 2
    up_base = 4 * row_blocks
    down_base = up_base + row_blocks * col_blocks
    chunks = [(0, 1, row_blocks), (up_base, col_blocks, 1), (down_base, col_blocks, 1)]
    orients = [0, 1, 0]

    def coords(orient):
        y_first = (core + orient) % 2 == 0
        return jnp.where(y_first, y_at, x_at), jnp.where(y_first, x_at, y_at), plane

    def chunk_units(chunk):
        base, row_step, block_step = chunk
        return base + jnp.arange(4)[:, None] * block_step + jnp.arange(row_blocks)[None] * row_step

    def weights_of(at):
        chunk, orient = chunks[at], orients[at]
        if fast:
            where = coords(orient)
            info = jnp.stack([where[0], place * cap]).astype(jnp.int32)
            going, kept = spread(master, unit_slot, info, chunk)
            owned = reduce_parts([going], [kept], orient, where)
            mine = gather_parts(owned, orient, where)[0]
        else:
            local = unit_slot[chunk_units(chunk)] - place * cap
            own = (local >= 0) & (local < cap)
            blocks = jnp.take(master, jnp.clip(local, 0, cap - 1), axis=0)
            blocks = jnp.where(own[..., None, None], blocks, 0.0).astype(BF)
            mine = lax.psum(blocks.reshape(4, width, cols), "batch")
        return mine, core_swap(mine)

    def grads_of(at, mine, theirs, vec_mine=None, vec_theirs=None):
        orient = orients[at]
        grad = total(mine, core_swap(theirs))
        parts = [grad]
        if vec_mine is not None:
            parts.append(total(vec_mine, core_swap(vec_theirs))[None])
        if not fast:
            return [lax.psum(part, "batch") for part in parts]
        where = coords(orient)
        halves = [part.shape[1] // 2 for part in parts]
        going = [cut(part, (1 - where[0]) * half, half) for part, half in zip(parts, halves)]
        kept = [cut(part, where[0] * half, half) for part, half in zip(parts, halves)]
        return gather_parts(reduce_parts(going, kept, orient, where), orient, where)

    def halves_of(array_in):
        other = lax.dynamic_slice_in_dim(array_in, (1 - core) * cols, cols, array_in.ndim - 1)
        return lax.dynamic_slice_in_dim(array_in, core * cols, cols, array_in.ndim - 1), other

    def swapped(array_in):
        return jnp.concatenate(halves_of(array_in), axis=-1)

    info = jnp.stack([phase_of[0], core]).astype(jnp.int32)
    vectors = vector_state[0]
    rows = jnp.concatenate(
        [swapped(vectors[0:2]), vectors[2:5], vectors[9:12]], axis=0
    )
    upper = vectors[5:9].reshape(2, FF // 2)
    bias_up = jnp.where(core == 0, upper, upper[::-1]).reshape(4, width)

    weights_io = weights_of(0)
    weights_up = weights_of(1)
    weights_down = weights_of(2)
    q, k, v, ctx, lse, first, x_t = forward(info, tokens, rows, *weights_io)
    act, slope, hidden_t = feed_up(first, rows, bias_up, *weights_up)
    out_half, dz2, down_mine, down_theirs, sums_two = feed_down(
        info, first, act, cotangent, rows, *weights_down
    )
    (grad_down,) = grads_of(2, down_mine, down_theirs)
    out_other = core_swap(out_half)
    dz1, dctx, dt_t, up_mine, up_theirs, sums_one = feed_back(
        first, dz2, slope, hidden_t, rows, weights_down, weights_up, weights_io
    )
    (grad_up,) = grads_of(1, up_mine, up_theirs)
    io_mine, io_theirs, grad_x, sums_zero = attend_back(
        info, q, k, v, dctx, lse, dz1, x_t, dt_t, ctx, *weights_io
    )
    grad_x_other = core_swap(grad_x)

    full_mine, full_theirs = halves_of(jnp.concatenate([sums_one[0:3], sums_two[0:3]], axis=0))
    up_rows = sums_one[4:8].reshape(2, 4, cols)

    def vec_rows(at, full):
        head_rows = sums_zero[0:2, at * cols : (at + 1) * cols]
        pad = jnp.zeros((4, cols), F32)
        return jnp.concatenate([head_rows, full[0:3], up_rows[at], full[3:6], pad], axis=0)

    grad_io, vec_half = grads_of(
        0, io_mine, io_theirs, vec_rows(0, full_mine), vec_rows(1, full_theirs)
    )
    vec_here = vec_half[0].astype(F32)
    vec_there = core_swap(vec_half[0]).astype(F32)
    left = jnp.where(core == 0, vec_here, vec_there)
    right = jnp.where(core == 0, vec_there, vec_here)
    wide_rows = jnp.concatenate([left, right], axis=1)
    vector_grads = jnp.concatenate(
        [
            wide_rows[0:5],
            left[5:9].reshape(2, width),
            right[5:9].reshape(2, width),
            wide_rows[9:12],
        ],
        axis=0,
    )

    count_f = step_count[0].astype(F32)
    scalars = [
        decay_rates[0],
        decay_rates[1],
        decay_rates[2],
        1.0 / (1.0 - decay_rates[0] ** count_f),
        1.0 / (1.0 - decay_rates[1] ** count_f),
    ]
    my_ids = place * cap + jnp.arange(cap, dtype=jnp.int32)
    matches = unit_slot[None, :] == my_ids[:, None]
    unit_ids = jnp.arange(unit_slot.shape[0], dtype=jnp.int32)
    unit = jnp.sum(jnp.where(matches, unit_ids[None, :], 0), axis=1)
    occupied = jnp.any(matches, axis=1)
    is_up = (unit >= up_base) & (unit < down_base)
    is_down = unit >= down_base
    chunk_at = jnp.where(is_down, 2, jnp.where(is_up, 1, 0))
    local = unit - jnp.where(is_down, down_base, up_base)
    block_at = jnp.where(chunk_at == 0, unit // row_blocks, local % col_blocks)
    row_at = jnp.where(chunk_at == 0, unit % row_blocks, local // col_blocks)
    kind = jnp.where(
        occupied,
        (unit >= 3 * row_blocks).astype(jnp.int32) + is_up.astype(jnp.int32) + 2 * is_down,
        0,
    )
    rates = jnp.sum(
        jnp.where(kind[:, None] == jnp.arange(4)[None, :], learn_rates[None, :4], 0.0), axis=1
    )
    table = jnp.stack([jnp.where(occupied, chunk_at, 3), block_at, row_at]).astype(jnp.int32)
    scales = jnp.concatenate([jnp.stack(scalars), jnp.zeros((3,), F32), rates])
    new_states = adamw_slots(
        table,
        scales,
        (master, first_moment, second_moment, average),
        (grad_io, grad_up, grad_down),
    )
    grads_scaled = vector_grads * float(tok_rows * batch_count) ** (-0.5)
    vec_weights, vec_first, vec_second, vec_average = adamw_update(
        vector_state[0], vector_state[1], vector_state[2], vector_state[3],
        grads_scaled, learn_rates[4], scalars,
    )

    def both(here, there):
        low_first = core == 0
        return jnp.concatenate(
            [jnp.where(low_first, here, there), jnp.where(low_first, there, here)], axis=0
        )

    return (
        both(out_half, out_other),
        both(grad_x, grad_x_other).astype(F32),
        *new_states,
        jnp.stack([vec_weights, vec_average]),
        jnp.stack([grads_scaled, vec_first]),
        vec_second,
    )


def solution(mesh):
    return jax.shard_map(
        on_device,
        mesh=mesh,
        in_specs=(
            P("batch", None),
            P("batch", None),
            P("batch"),
            P(),
            P(),
            P(),
            P(),
            P("batch", None, "tensor"),
            P("batch", None, "tensor"),
            P("batch", None, "tensor"),
            P("batch", None, "tensor"),
            P(),
        ),
        out_specs=(
            P("batch", None),
            P("batch", None),
            P("batch", None, "tensor"),
            P("batch", None, "tensor"),
            P("batch", None, "tensor"),
            P("batch", None, "tensor"),
            P(),
            P(),
            P(),
        ),
        check_vma=False,
    )
```

```python
import functools

import jax
import jax.numpy as jnp
from jax import lax
from jax.experimental import pallas as pl
from jax.experimental.pallas import tpu as pltpu
from jax.sharding import PartitionSpec as P

HD = 64
FF = 3072
SHORT = 128
LONG = 512
EPS = 1e-12
BF = jnp.bfloat16
F32 = jnp.float32
VMEM_BYTES = 60 * 2**20
BOTH = ("batch", "tensor")
ANY = pl.BlockSpec(memory_space=pl.ANY)
PLANES = 4
FAST_BATCH = 16


def dot(first_mat, second_mat):
    return lax.dot_general(
        first_mat, second_mat, (((1,), (0,)), ((), ())), preferred_element_type=F32
    )


def dot_nt(first_mat, second_mat):
    return lax.dot_general(
        first_mat, second_mat, (((1,), (1,)), ((), ())), preferred_element_type=F32
    )


def normalized(rows):
    centred = rows - jnp.mean(rows, axis=-1, keepdims=True)
    inverse = lax.rsqrt(jnp.mean(centred * centred, axis=-1, keepdims=True) + EPS)
    return centred * inverse, inverse


def norm_back(grad_scaled, normal, inverse):
    mean_grad = jnp.mean(grad_scaled, axis=-1, keepdims=True)
    mean_both = jnp.mean(grad_scaled * normal, axis=-1, keepdims=True)
    return inverse * (grad_scaled - mean_grad - normal * mean_both)


def row_sum(array_in):
    return jnp.sum(array_in, axis=0, keepdims=True)


def load_blocks(info_ref, parts, blocks, weight_ref, sem_ref):
    _, half_rows, cols = parts[0].shape
    copies = []
    for spot, (half, block) in enumerate(blocks):
        first = info_ref[2 + half]
        pair = []
        for at in range(2):
            start = pl.multiple_of((first if at == 0 else 1 - first) * half_rows, half_rows)
            pair.append(
                pltpu.make_async_copy(
                    parts[2 * half + at].at[block],
                    weight_ref.at[pl.ds(start, half_rows), pl.ds(spot * cols, cols)],
                    sem_ref.at[2 * spot + at],
                )
            )
        copies.append(pair)
    return copies


def after(array_in, *others):
    return lax.optimization_barrier((array_in, others))[0]


def first_time(copies):
    @pl.when(pl.program_id(0) == 0)
    def _():
        for pair in copies:
            for copy in pair:
                copy.wait()


def start_first(copies):
    @pl.when(pl.program_id(0) == 0)
    def _():
        for pair in copies:
            for copy in pair:
                copy.start()


PAIRED = [(half, block) for block in range(4) for half in range(2)]
SHARES = [(half, block) for half in range(2) for block in range(3)]
HALVED = [(half, block) for half in range(2) for block in range(4)]


def call(
    kernel, grid, in_specs, out_specs, out_shape, scratch, prefetch, flops, moved, exps=0, kept=None
):
    aliases = {}
    if kept is not None:
        given = prefetch + len(in_specs)
        count = len(kept)
        in_specs = in_specs + [ANY] * count
        aliases = {given + at: at for at in range(count)}
        inner = kernel

        def kernel(*refs):
            inner(*refs[:given], *refs[given + count :])

    return pl.pallas_call(
        kernel,
        input_output_aliases=aliases,
        out_shape=out_shape,
        grid_spec=pltpu.PrefetchScalarGridSpec(
            num_scalar_prefetch=prefetch,
            grid=grid,
            in_specs=in_specs,
            out_specs=out_specs,
            scratch_shapes=scratch,
        ),
        compiler_params=pltpu.CompilerParams(vmem_limit_bytes=VMEM_BYTES),
        cost_estimate=pl.CostEstimate(
            flops=30 * flops, bytes_accessed=moved, transcendentals=exps
        ),
    )


def struct(shape, kind):
    return jax.ShapeDtypeStruct(shape, kind)


def spread_kernel(
    base, row_step, block_step, cap, rows, info_ref, slot_ref, *refs
):
    sources, outs, (held_ref, quarter_ref, sem_ref) = refs[:4], refs[4:8], refs[8:]
    block = pl.program_id(0)
    quarter, plane, place = info_ref[0], info_ref[1], info_ref[2]
    copies = [
        [
            pltpu.make_async_copy(
                ref, held_ref.at[pl.ds(info_ref[3 + at] * cap, cap)], sem_ref.at[at]
            )
        ]
        for at, ref in enumerate(sources)
    ]
    start_first(copies)
    first_time(copies)
    total_slots = PLANES * cap
    for step in range(3):
        unit = base + (quarter * 3 + step) * row_step + block * block_step
        local = slot_ref[unit] - plane * total_slots
        here = (local >= 0) & (local < total_slots)
        spot = slice(step * rows, (step + 1) * rows)

        @pl.when(here)
        def _():
            quarter_ref[spot, :] = held_ref[local]

        @pl.when(jnp.logical_not(here))
        def _():
            quarter_ref[spot, :] = jnp.zeros((rows, quarter_ref.shape[1]), BF)

    for ahead, out_ref in enumerate(outs):
        size = out_ref.shape[1]
        start = pl.multiple_of(lax.rem(plane + ahead, PLANES) * size, size)
        out_ref[0] = quarter_ref[pl.ds(start, size), :]


def spread(sources, unit_slot, info, chunk):
    cap, rows, cols = sources[0].shape
    base, row_step, block_step = chunk
    size = 3 * rows // PLANES
    block = pl.BlockSpec((1, size, cols), lambda i, *_: (i, 0, 0))
    return call(
        functools.partial(spread_kernel, base, row_step, block_step, cap, rows),
        (4,),
        [ANY] * 4,
        [block] * 4,
        [struct((4, size, cols), BF)] * 4,
        [
            pltpu.VMEM((PLANES * cap, rows, cols), BF),
            pltpu.VMEM((3 * rows, cols), BF),
            pltpu.SemaphoreType.DMA((4,)),
        ],
        2,
        0,
        5 * 2**20,
    )(info, unit_slot, *sources)


def swap_pairs(orient, stage):
    pairs = []
    for place in range(FAST_BATCH):
        for core in range(2):
            first_bit = 2 if (core + orient) % 2 == 0 else 1
            bit = first_bit if stage == 1 else 3 - first_bit
            pairs.append((place * 2 + core, (place ^ bit) * 2 + core))
    return pairs


def flip_pairs(bit):
    return [
        (place * 2 + core, (place ^ bit) * 2 + core)
        for place in range(FAST_BATCH)
        for core in range(2)
    ]


def plane_pairs(step):
    return [
        (place * 2 + core, (place + 4 * step) % FAST_BATCH * 2 + core)
        for place in range(FAST_BATCH)
        for core in range(2)
    ]


def total(*terms):
    result = terms[0].astype(F32)
    for term in terms[1:]:
        result = result + term.astype(F32)
    return result.astype(BF)


def send(array_in, pairs):
    return lax.ppermute(array_in, BOTH, pairs)


def cut(array_in, start, size):
    return lax.dynamic_slice_in_dim(array_in, start, size, 1)


def first_split(info, mine, other):
    half = mine.shape[1] // 2
    return [
        total(cut(mine, at * half, half), cut(other, at * half, half))
        for at in (1 - info[0], info[0])
    ]


def second_split(info, kept, got):
    half = kept.shape[1] // 2
    start = (1 - info[1]) * half
    return total(cut(kept, start, half), cut(got, start, half))


def third_split(info, kept, one, two):
    half = two.shape[1]
    size = half // PLANES
    pieces = []
    for ahead in range(PLANES):
        start = (info[2] + ahead) % PLANES * size
        pieces.append(
            total(
                cut(kept, info[1] * half + start, size),
                cut(one, info[1] * half + start, size),
                cut(two, start, size),
            )
        )
    return pieces


def plane_join(info, pieces):
    return jnp.concatenate(
        [lax.select_n((info[2] - row) % PLANES, *pieces) for row in range(PLANES)], axis=1
    )


def half_join(info, here, there):
    low_first = info[1] == 0
    return jnp.concatenate(
        [jnp.where(low_first, here, there), jnp.where(low_first, there, here)], axis=1
    )


def exchange(going, kept, orient, info):
    (one,) = yield [(going, swap_pairs(orient, 1))]
    outgoing = second_split(info, kept, one)
    (two,) = yield [(outgoing, swap_pairs(orient, 2))]
    own, *pieces = third_split(info, kept, one, two)
    return (yield from spreading([own] + pieces, orient, info))


def spreading(pieces, orient, info):
    arrived = yield [(pieces[step], plane_pairs(step)) for step in range(1, PLANES)]
    owned = total(pieces[0], *arrived)
    others = yield [(owned, plane_pairs(step)) for step in range(1, PLANES)]
    level = plane_join(info, [owned] + others)
    (there,) = yield [(level, swap_pairs(orient, 2))]
    level = half_join(info, level, there)
    (there,) = yield [(level, swap_pairs(orient, 1))]
    return level, there


def quarters(info, mine, other):
    size = mine.shape[1] // 4
    at = info[0]
    return [
        total(cut(mine, (at ^ away) * size, size), cut(other, (at ^ away) * size, size))
        for away in range(4)
    ]


def plane_exchange(pieces, info):
    own, *going = pieces
    got = yield [(piece, flip_pairs(away)) for away, piece in zip((1, 2, 3), going)]
    size = own.shape[1] // PLANES
    parts = []
    for ahead in range(PLANES):
        start = (info[2] + ahead) % PLANES * size
        parts.append(total(*[cut(piece, start, size) for piece in [own] + got]))
    arrived = yield [(parts[step], plane_pairs(step)) for step in range(1, PLANES)]
    owned = total(parts[0], *arrived)
    others = yield [(owned, plane_pairs(step)) for step in range(1, PLANES)]
    level = plane_join(info, [owned] + others)
    there = yield [(level, flip_pairs(away)) for away in (1, 2, 3)]
    return [level] + there


def doubling(array_in):
    cores = [(at, at ^ 1) for at in range(2 * FAST_BATCH)]
    for pairs in [cores] + [flip_pairs(bit) for bit in (1, 2, 4, 8)]:
        (other,) = yield [(array_in, pairs)]
        array_in = array_in + other
    return array_in


class Chain:
    def __init__(self, steps):
        self.steps = steps
        self.result = None
        self.pending = next(steps)

    @property
    def ready(self):
        return [parts for parts, _ in self.pending]

    def take(self, arrived):
        try:
            self.pending = self.steps.send(arrived)
        except StopIteration as stop:
            self.pending, self.result = [], stop.value


def phase(chains=(), swaps=(), work=None):
    ready, swaps = lax.optimization_barrier(([chain.ready for chain in chains], list(swaps)))
    arrived = [
        [send(parts, pairs) for parts, (_, pairs) in zip(given, chain.pending)]
        for given, chain in zip(ready, chains)
    ]
    swapped = [core_swap(array) for array in swaps]
    done = None if work is None else work((ready, swaps))
    arrived, swapped, done = lax.optimization_barrier((arrived, swapped, done))
    for chain, parts in zip(chains, arrived):
        chain.take(parts)
    return swapped, done


def core_swap(array_in):
    return lax.ppermute(array_in, "tensor", [(0, 1), (1, 0)])


def seen_mask():
    key_at = lax.broadcasted_iota(jnp.int32, (2 * LONG, LONG), 0) % LONG // SHORT
    query_at = lax.broadcasted_iota(jnp.int32, (2 * LONG, LONG), 1) // SHORT
    return key_at == query_at


def low_lanes(rows):
    return lax.broadcasted_iota(jnp.int32, (rows, 2 * HD), 1) < HD


def pair_lanes(pair):
    return pl.ds(pl.multiple_of(pair * 2 * HD, 2 * HD), 2 * HD)


def both_heads(array_in):
    low = low_lanes(array_in.shape[0])
    none = jnp.zeros_like(array_in)
    return jnp.concatenate(
        [jnp.where(low, array_in, none), jnp.where(low, none, array_in)], axis=0
    )


def by_head(array_in):
    return array_in.reshape(2, LONG, array_in.shape[1])


def pair_columns(array_in):
    return jnp.where(low_lanes(LONG), array_in[:LONG], array_in[LONG:])


FORWARD_PAIRS = 2
BACKWARD_PAIRS = 1


def attend_pairs(first, short, q_ref, k_ref, v_ref, ctx_ref, lse_ref):
    pairs = range(FORWARD_PAIRS)
    lanes = [pair_lanes(first + pair) for pair in pairs]
    queries = [q_ref[:, at] * BF(HD**-0.5) for at in lanes]
    keys_here = [both_heads(k_ref[:, at]) for at in lanes]
    values_t = [v_ref[:, at].T for at in lanes]
    scores = [dot_nt(keys_here[pair], queries[pair]) for pair in pairs]
    if short:
        scores = [jnp.where(seen_mask(), score, -1e30) for score in scores]
    scores = [by_head(score) for score in scores]
    tops = [jnp.max(score, axis=1, keepdims=True) for score in scores]
    weights = [jnp.exp(score - top) for score, top in zip(scores, tops)]
    norms = [jnp.sum(weight, axis=1, keepdims=True) for weight in weights]
    probs = [(weight * (1.0 / norm)).astype(BF) for weight, norm in zip(weights, norms)]
    for pair in pairs:
        outs = [
            dot(values_t[pair][head * HD : (head + 1) * HD], probs[pair][head])
            for head in range(2)
        ]
        ctx_ref[:, lanes[pair]] = jnp.concatenate(outs, axis=0).T.astype(BF)
        for head in range(2):
            spot = pl.ds((first + pair) * 2 + head, 1)
            lse_ref[0, spot, :] = tops[pair][head] + jnp.log(norms[pair][head])


def forward_kernel(
    info_ref, x_ref, rows_ref, w0_ref, w1_ref, w2_ref, w3_ref,
    q_ref, k_ref, v_ref, ctx_ref, lse_ref, z_ref, xt_ref, w_ref, sem_ref,
):
    width = x_ref.shape[1]
    parts = (w0_ref, w1_ref, w2_ref, w3_ref)
    copies = load_blocks(info_ref, parts, PAIRED, w_ref, sem_ref)
    start_first(copies)
    tokens = x_ref[...]
    xt_ref[...] = tokens.T
    first_time(copies[:2])
    q_ref[...] = (dot(tokens, w_ref[:, :width]) + rows_ref[0:1]).astype(BF)
    first_time(copies[2:4])
    k_ref[...] = dot(tokens, w_ref[:, width : 2 * width]).astype(BF)
    first_time(copies[4:6])
    v_ref[...] = (dot(tokens, w_ref[:, 2 * width : 3 * width]) + rows_ref[1:2]).astype(BF)
    pairs = width // (2 * HD)

    def all_pairs(short):
        @pl.loop(0, pairs, step=FORWARD_PAIRS)
        def _(first):
            attend_pairs(first, short, q_ref, k_ref, v_ref, ctx_ref, lse_ref)

    @pl.when(info_ref[0] == 1)
    def _():
        all_pairs(False)

    @pl.when(info_ref[0] != 1)
    def _():
        all_pairs(True)

    first_time(copies[6:8])
    attended = dot_nt(ctx_ref[...], w_ref[:, 3 * width :])
    z_ref[...] = tokens.astype(F32) + attended + rows_ref[2:3]


def forward(group, info, tokens, rows, weights, kept=None):
    tok = tokens.shape[0] // 2
    width = tokens.shape[1]
    groups = tok // LONG
    tile = pl.BlockSpec((LONG, width), lambda i, *_: (group, 0))
    low = struct((tok, width), BF)
    return call(
        forward_kernel,
        (1,),
        [
            pl.BlockSpec((LONG, width), lambda i, info: (info[1] * groups + group, 0)),
            pl.BlockSpec((8, width), lambda i, *_: (0, 0)),
        ]
        + [ANY] * 4,
        [
            tile, tile, tile, tile,
            pl.BlockSpec((1, 16, LONG), lambda i, *_: (group, 0, 0)),
            tile,
            pl.BlockSpec((width, LONG), lambda i, *_: (0, group)),
        ],
        [
            low, low, low, low,
            struct((groups, 16, LONG), F32),
            struct((tok, width), F32),
            struct((width, tok), BF),
        ],
        [pltpu.VMEM((width, 4 * width), BF), pltpu.SemaphoreType.DMA((16,))],
        1,
        2 * LONG * width * (4 * width + 2 * LONG) * 2,
        12 * 2**20,
        LONG * LONG * 12,
        kept,
    )(info, tokens, rows, *weights, *(kept or ()))


def up_kernel(
    info_ref, z_ref, rows_ref, bias_ref, w0_ref, w1_ref, w2_ref, w3_ref,
    act_ref, slope_ref, ht_ref, hidden_ref, w_ref, sem_ref,
):
    width = z_ref.shape[1]
    parts = (w0_ref, w1_ref, w2_ref, w3_ref)
    copies = load_blocks(info_ref, parts, HALVED, w_ref, sem_ref)
    start_first(copies)
    normal, _ = normalized(z_ref[...])
    hidden = normal * rows_ref[3:4] + rows_ref[4:5]
    hidden_ref[...] = hidden
    low = hidden.astype(BF)
    ht_ref[...] = low.T
    for part in range(FF // width):
        spot = slice(part * width, (part + 1) * width)
        first_time(copies[2 * part : 2 * part + 2])
        upper = dot(low, w_ref[:, spot]) + bias_ref[part : part + 1]
        phi_sum = 0.5 + 0.5 * lax.erf(upper * (0.5**0.5))
        density = jnp.exp(-0.5 * upper * upper) * 0.3989422804014327
        act_ref[:, spot] = (upper * phi_sum).astype(BF)
        slope_ref[:, spot] = (phi_sum + upper * density).astype(BF)


TILE = 512
ROWS, COLUMNS, NORM_ROWS = 256, 256, 64
UP_TILE = 256


def feed_up(info, first, rows, bias, weights):
    tok, width = first.shape
    wide = struct((tok, FF), BF)
    return call(
        up_kernel,
        (tok // UP_TILE,),
        [
            pl.BlockSpec((UP_TILE, width), lambda i, *_: (i, 0)),
            pl.BlockSpec((8, width), lambda i, *_: (0, 0)),
            pl.BlockSpec((4, width), lambda i, *_: (0, 0)),
        ]
        + [ANY] * 4,
        [
            pl.BlockSpec((UP_TILE, FF), lambda i, *_: (i, 0)),
            pl.BlockSpec((UP_TILE, FF), lambda i, *_: (i, 0)),
            pl.BlockSpec((width, UP_TILE), lambda i, *_: (0, i)),
            pl.BlockSpec((UP_TILE, width), lambda i, *_: (i, 0)),
        ],
        [wide, wide, struct((width, tok), BF), struct((tok, width), F32)],
        [pltpu.VMEM((width, FF), BF), pltpu.SemaphoreType.DMA((16,))],
        1,
        2 * tok * width * FF,
        20 * 2**20,
        tok * FF * 2,
    )(info, first, rows, bias, *weights)


def down_kernel(
    info_ref, h_ref, act_ref, cot_ref, rows_ref, w0_ref, w1_ref, w2_ref, w3_ref,
    out_ref, dz_ref, gt_ref, dyt_ref, sum_ref, w_ref, branch_ref, low_ref, sem_ref,
):
    step = pl.program_id(0)
    width = h_ref.shape[1]
    tiles = act_ref.shape[0] // TILE

    parts = (w0_ref, w1_ref, w2_ref, w3_ref)
    copies = load_blocks(info_ref, parts, HALVED, w_ref, sem_ref)
    start_first(copies)

    @pl.when(step == 0)
    def _():
        sum_ref[...] = jnp.zeros_like(sum_ref)

    first_time(copies)

    @pl.when(step < tiles)
    def _():
        base = pl.multiple_of(step * TILE, TILE)
        for row in range(0, TILE, ROWS):
            spot = slice(row, row + ROWS)
            branch_ref[spot, :] = dot_nt(act_ref[pl.ds(base + row, ROWS), :], w_ref[...])
        gains = rows_ref[6:7]
        sums = [0.0, 0.0, 0.0]
        for row in range(0, TILE, NORM_ROWS):
            spot = slice(row, row + NORM_ROWS)
            normal, inverse = normalized(h_ref[spot, :] + branch_ref[spot, :] + rows_ref[5:6])
            out_ref[spot, :] = (normal * gains + rows_ref[7:8]).astype(BF)
            cot = cot_ref[spot, :].astype(F32)
            grad = norm_back(cot * gains, normal, inverse)
            dz_ref[spot, :] = grad
            low_ref[spot, :] = grad.astype(BF)
            for at, value in enumerate((grad, cot * normal, cot)):
                sums[at] = sums[at] + row_sum(value)
        dyt_ref[:, pl.ds(base, TILE)] = low_ref[...].T
        for at in range(3):
            sum_ref[at : at + 1] += sums[at]

    for part in range(2):
        @pl.when(step == tiles + part)
        def _():
            grad = dot(dyt_ref[...], act_ref[:, (part + 2) * width : (part + 3) * width])
            put_blocks(gt_ref, grad)


def put_blocks(ref, grad):
    cols = ref.shape[2]
    for block in range(ref.shape[0]):
        ref[block] = grad[:, block * cols : (block + 1) * cols].astype(BF)


def feed_down(info, hidden, act, cot, rows, weights):
    tok, width = hidden.shape
    tiles = tok // TILE
    last = tiles - 1
    row_tile = pl.BlockSpec((TILE, width), lambda i, *_: (jnp.minimum(i, last), 0))
    grads = struct((4, width, width // 2), BF)
    return call(
        down_kernel,
        (tiles + 2,),
        [
            row_tile,
            pl.BlockSpec((tok, FF), lambda i, *_: (0, 0)),
            pl.BlockSpec(
                (TILE, width), lambda i, info: (info[1] * tiles + jnp.minimum(i, last), 0)
            ),
            pl.BlockSpec((8, width), lambda i, *_: (0, 0)),
        ]
        + [ANY] * 4,
        [
            row_tile,
            row_tile,
            pl.BlockSpec((2, width, width // 2), lambda i, *_: (jnp.clip(i - tiles, 0, 1), 0, 0)),
            pl.BlockSpec((width, tok), lambda i, *_: (0, 0)),
            pl.BlockSpec((8, width), lambda i, *_: (0, 0)),
        ],
        [
            struct((tok, width), BF),
            struct((tok, width), F32),
            grads,
            struct((width, tok), BF),
            struct((8, width), F32),
        ],
        [
            pltpu.VMEM((width, FF), BF),
            pltpu.VMEM((TILE, width), F32),
            pltpu.VMEM((TILE, width), BF),
            pltpu.SemaphoreType.DMA((16,)),
        ],
        1,
        3 * tok * width * FF,
        30 * 2**20,
    )(info, hidden, act, cot, rows, *weights)


def back_kernel(info_ref, z_ref, dz2_ref, slope_ref, rows_ref, *refs):
    down, upper, other = refs[:4], refs[4:8], refs[8:12]
    dz1_ref, dctx_ref, dtt_ref, da_ref, sum_ref = refs[12:17]
    wd_ref, wu_ref, wo_ref, hidden_ref, low_ref, dsem_ref, usem_ref, osem_ref = refs[17:]
    width = z_ref.shape[1]
    downs = load_blocks(info_ref, down, HALVED, wd_ref, dsem_ref)
    ups = load_blocks(info_ref, upper, HALVED, wu_ref, usem_ref)
    outs = load_blocks(info_ref, other, [(0, 3), (1, 3)], wo_ref, osem_ref)
    for at in range(0, 8, 2):
        start_first(downs[at : at + 2] + ups[at : at + 2])
    start_first(outs)

    @pl.when(pl.program_id(0) == 0)
    def _():
        sum_ref[...] = jnp.zeros_like(sum_ref)

    tile = z_ref.shape[0]
    low_two = dz2_ref[...].astype(BF)
    for part in range(FF // width):
        first_time(downs[2 * part : 2 * part + 2])
        place = 4 + (part ^ (2 * info_ref[1]))
        for start in range(0, width, COLUMNS):
            lanes = slice(part * width + start, part * width + start + COLUMNS)
            grad_sum = 0.0
            for row in range(0, tile, ROWS):
                spot = slice(row, row + ROWS)
                grad_act = dot(low_two[spot], wd_ref[:, lanes])
                grad_up = (grad_act * slope_ref[spot, lanes].astype(F32)).astype(BF)
                da_ref[spot, lanes] = grad_up
                grad_sum = grad_sum + row_sum(grad_up.astype(F32))
            sum_ref[pl.ds(place, 1), start : start + COLUMNS] += grad_sum
    first_time(ups)
    for row in range(0, tile, ROWS):
        spot = slice(row, row + ROWS)
        hidden_ref[spot, :] = dz2_ref[spot, :] + dot_nt(da_ref[spot, :], wu_ref[...])
    gains = rows_ref[3:4]
    sums = [0.0, 0.0, 0.0]
    for row in range(0, tile, NORM_ROWS):
        spot = slice(row, row + NORM_ROWS)
        grad_hidden = hidden_ref[spot, :]
        normal, inverse = normalized(z_ref[spot, :])
        grad_one = norm_back(grad_hidden * gains, normal, inverse)
        sums[0] = sums[0] + row_sum(grad_one)
        sums[1] = sums[1] + row_sum(grad_hidden * normal)
        sums[2] = sums[2] + row_sum(grad_hidden)
        dz1_ref[spot, :] = grad_one
        low_ref[spot, :] = grad_one.astype(BF)
    for at in range(3):
        sum_ref[at : at + 1] += sums[at]
    dtt_ref[...] = low_ref[...].T
    first_time(outs)
    dctx_ref[...] = dot(low_ref[...], wo_ref[...]).astype(BF)


def feed_back(info, first, dz2, slope, rows, down, upper, other):
    tok, width = first.shape
    row_tile = pl.BlockSpec((TILE, width), lambda i, *_: (i, 0))
    wide_tile = pl.BlockSpec((TILE, FF), lambda i, *_: (i, 0))
    fixed = pl.BlockSpec((8, width), lambda i, *_: (0, 0))
    return call(
        back_kernel,
        (tok // TILE,),
        [row_tile, row_tile, wide_tile, fixed] + [ANY] * 12,
        [row_tile, row_tile, pl.BlockSpec((width, TILE), lambda i, *_: (0, i)), wide_tile, fixed],
        [
            struct((tok, width), F32),
            struct((tok, width), BF),
            struct((width, tok), BF),
            struct((tok, FF), BF),
            struct((8, width), F32),
        ],
        [
            pltpu.VMEM((width, FF), BF),
            pltpu.VMEM((width, FF), BF),
            pltpu.VMEM((width, width), BF),
            pltpu.VMEM((TILE, width), F32),
            pltpu.VMEM((TILE, width), BF),
            pltpu.SemaphoreType.DMA((16,)),
            pltpu.SemaphoreType.DMA((16,)),
            pltpu.SemaphoreType.DMA((4,)),
        ],
        1,
        4 * tok * width * FF,
        30 * 2**20,
    )(info, first, dz2, slope, rows, *down, *upper, *other)


def product_kernel(left_ref, right_ref, *outs):
    grad = dot(left_ref[...], right_ref[...])
    step = pl.program_id(0)
    for at, ref in enumerate(outs):
        @pl.when(step // 2 == at)
        def _():
            put_blocks(ref, grad)


def wide_grad(left_t, right, halves, blocks=4):
    width, tok = left_t.shape
    first = halves[0]
    spec = [
        pl.BlockSpec(
            (2, width, width // 2), lambda i, at=at: (jnp.clip(i - 2 * at, 0, 1), 0, 0)
        )
        for at in range(len(halves))
    ]
    return call(
        product_kernel,
        (2 * len(halves),),
        [
            pl.BlockSpec((width, tok), lambda i: (0, 0)),
            pl.BlockSpec((tok, width), lambda i: (0, (i + 2 * first) % 4)),
        ],
        spec,
        [struct((blocks, width, width // 2), BF)] * len(halves),
        [],
        0,
        tok * width * FF * len(halves),
        10 * 2**20 * len(halves),
    )(left_t, right)


def square_kernel(left_ref, right_ref, gm_ref, gt_ref):
    grad = dot(left_ref[...], right_ref[...])
    cols = gm_ref.shape[2]
    gm_ref[0] = grad[:, :cols].astype(BF)
    gt_ref[0] = grad[:, cols:].astype(BF)


def share_kernel(left_ref, right_ref, out_ref):
    put_blocks(out_ref, dot(left_ref[...], right_ref[...]))


def share_grad(left_t, right, half):
    width, tok = left_t.shape
    cols = right.shape[1] // 2
    shape = (3, width, cols // 3)
    return call(
        share_kernel,
        (1,),
        [
            pl.BlockSpec((width, tok), lambda i: (0, 0)),
            pl.BlockSpec((tok, cols), lambda i: (0, half)),
        ],
        [pl.BlockSpec(shape, lambda i: (0, 0, 0))],
        [struct(shape, BF)],
        [],
        0,
        2 * tok * width * cols,
        6 * 2**20,
    )(left_t, right)[0]


def square_grad(left_t, right, first=0, kept=None):
    width, tok = left_t.shape
    count = right.shape[1] // width
    block = pl.BlockSpec((1, width, width // 2), lambda i: (first + i, 0, 0))
    return call(
        square_kernel,
        (count,),
        [
            pl.BlockSpec((width, tok), lambda i: (0, 0)),
            pl.BlockSpec((tok, width), lambda i: (0, i)),
        ],
        [block, block],
        [struct((first + count, width, width // 2), BF)] * 2,
        [],
        0,
        2 * tok * width * width * count,
        4 * 2**20 * count,
        0,
        kept,
    )(left_t, right, *(kept or ()))


def attend_pairs_back(first, short, q_ref, k_ref, v_ref, dctx_ref, lse_ref, dqkv_ref):
    width = q_ref.shape[1]
    pairs = range(BACKWARD_PAIRS)
    lanes = [pair_lanes(first + pair) for pair in pairs]
    queries = [q_ref[:, at] * BF(HD**-0.5) for at in lanes]
    keys_here = [k_ref[:, at] for at in lanes]
    grads = [dctx_ref[:, at] for at in lanes]
    keys_t = [keys.T for keys in keys_here]
    scores = [dot_nt(both_heads(keys_here[pair]), queries[pair]) for pair in pairs]
    grad_probs = [
        by_head(dot_nt(both_heads(v_ref[:, lanes[pair]]), grads[pair])) for pair in pairs
    ]
    if short:
        scores = [jnp.where(seen_mask(), score, -1e30) for score in scores]
    probs = [
        jnp.exp(
            by_head(scores[pair])
            - jnp.stack(
                [lse_ref[0, pl.ds((first + pair) * 2 + head, 1), :] for head in range(2)]
            )
        )
        for pair in pairs
    ]
    grad_v = [
        dot(prob.astype(BF).reshape(2 * LONG, LONG), grads[pair])
        for pair, prob in enumerate(probs)
    ]
    inners = [
        jnp.sum(prob * grad, axis=1, keepdims=True) for prob, grad in zip(probs, grad_probs)
    ]
    grad_scores = [
        (prob * (grad - inner)).astype(BF)
        for prob, grad, inner in zip(probs, grad_probs, inners)
    ]
    grad_k = [
        dot(grad.reshape(2 * LONG, LONG), queries[pair]) for pair, grad in enumerate(grad_scores)
    ]
    for pair in pairs:
        grad_q = [
            dot(keys_t[pair][head * HD : (head + 1) * HD], grad_scores[pair][head])
            for head in range(2)
        ]

        def store(part, values_in):
            at = first + pair
            half = at // 3
            start = half * (3 * width // 2) + part * (width // 2) + (at - 3 * half) * 2 * HD
            dqkv_ref[:, pl.ds(pl.multiple_of(start, 2 * HD), 2 * HD)] = values_in.astype(BF)

        store(0, jnp.concatenate(grad_q, axis=0).T * HD**-0.5)
        store(1, pair_columns(grad_k[pair]))
        store(2, pair_columns(grad_v[pair]))


def attend_back_kernel(
    info_ref, q_ref, k_ref, v_ref, dctx_ref, lse_ref, dz_ref, w0_ref, w1_ref, w2_ref, w3_ref,
    dqkv_ref, gx_ref, sum_ref, w_ref, sem_ref,
):
    width = q_ref.shape[1]
    parts = (w0_ref, w1_ref, w2_ref, w3_ref)
    copies = load_blocks(info_ref, parts, SHARES, w_ref, sem_ref)
    start_first(copies)

    def all_pairs(short):
        @pl.loop(0, width // (2 * HD), step=BACKWARD_PAIRS)
        def _(first):
            attend_pairs_back(first, short, q_ref, k_ref, v_ref, dctx_ref, lse_ref, dqkv_ref)

    @pl.when(info_ref[0] == 1)
    def _():
        all_pairs(False)

    @pl.when(info_ref[0] != 1)
    def _():
        all_pairs(True)

    sum_ref[...] = jnp.zeros_like(sum_ref)
    cols = width // 2
    for half in range(2):
        core = info_ref[1] if half == 0 else 1 - info_ref[1]
        spot = pl.ds(pl.multiple_of(core * cols, cols), cols)
        for row, part in enumerate((0, 2)):
            start = (3 * half + part) * cols
            sum_ref[row : row + 1, spot] = row_sum(dqkv_ref[:, start : start + cols].astype(F32))
    first_time(copies)
    gx_ref[...] = (dz_ref[...] + dot_nt(dqkv_ref[...], w_ref[...])).astype(BF)


def attend_back(group, info, q, k, v, dctx, lse, dz, weights, kept=None):
    tok, width = q.shape
    tile = pl.BlockSpec((LONG, width), lambda i, *_: (group, 0))
    *results, sums = call(
        attend_back_kernel,
        (1,),
        [
            tile, tile, tile, tile,
            pl.BlockSpec((1, 16, LONG), lambda i, *_: (group, 0, 0)),
            tile,
        ]
        + [ANY] * 4,
        [
            pl.BlockSpec((LONG, 3 * width), lambda i, *_: (group, 0)),
            tile,
            pl.BlockSpec((8, width), lambda i, *_: (0, 0)),
        ],
        [struct((tok, 3 * width), BF), struct((tok, width), BF), struct((8, width), F32)],
        [pltpu.VMEM((width, 3 * width), BF), pltpu.SemaphoreType.DMA((12,))],
        1,
        2 * LONG * width * (3 * width + 10 * LONG),
        15 * 2**20,
        LONG * LONG * 12,
        kept,
    )(info, q, k, v, dctx, lse, dz, *weights, *(kept or ()))
    return results, sums


def adamw_update(weights_in, moment, square, average_in, gradient, rate, scalars):
    beta_one, beta_two, ema_decay, scale_one, scale_two = scalars
    moment_new = beta_one * moment + (1.0 - beta_one) * gradient
    square_new = beta_two * square + (1.0 - beta_two) * gradient * gradient
    moment_hat = moment_new * scale_one
    square_hat = square_new * scale_two
    weights_new = weights_in - rate * (
        moment_hat / (jnp.sqrt(square_hat) + 1e-08) + 0.01 * weights_in
    )
    average_new = ema_decay * average_in + (1.0 - ema_decay) * weights_new
    return weights_new, moment_new, square_new, average_new


SLOT_STEPS = 3
LATE = 4


def fetch_gradient(ref, table_ref, slot, held_ref, sem_ref, rows):
    spot = pl.ds(pl.multiple_of(table_ref[2, slot] * rows, rows), rows)
    return pltpu.make_async_copy(
        ref.at[table_ref[1, slot], spot], held_ref.at[slot], sem_ref.at[slot]
    )


def adamw_kernel(table_ref, scale_ref, w_ref, m_ref, s_ref, a_ref, *refs):
    grads, outs, (held_ref, sem_ref) = refs[:4], refs[4:8], refs[8:]
    step = pl.program_id(0)
    count, rows, _ = w_ref.shape

    @pl.when(step == 0)
    def _():
        @pl.loop(0, held_ref.shape[0])
        def _(slot):
            for at, ref in enumerate(grads):
                chosen = table_ref[0, slot] == at + LATE
                if at == 0:
                    chosen = table_ref[0, slot] <= LATE

                @pl.when(chosen)
                def _():
                    fetch_gradient(ref, table_ref, slot, held_ref, sem_ref, rows).start()

    scalars = [scale_ref[at] for at in range(5)]

    @pl.loop(0, count)
    def _(at):
        slot = step * count + at
        fetch_gradient(grads[0], table_ref, slot, held_ref, sem_ref, rows).wait()
        gradient = held_ref[slot].astype(F32) * scale_ref[8 + 2 * slot]
        results = adamw_update(
            w_ref[at], m_ref[at], s_ref[at], a_ref[at], gradient,
            scale_ref[9 + 2 * slot], scalars,
        )
        for ref, value in zip(outs, results):
            ref[at] = value


def adamw_slots(table, scales, states, grads):
    cap, rows, cols = states[0].shape
    steps = SLOT_STEPS if cap % SLOT_STEPS == 0 else 1
    own = pl.BlockSpec((cap // steps, rows, cols), lambda i, *_: (i, 0, 0))
    return call(
        adamw_kernel,
        (steps,),
        [own] * 4 + [ANY] * 4,
        [own] * 4,
        [struct(states[0].shape, F32)] * 4,
        [pltpu.VMEM((cap, rows, cols), BF), pltpu.SemaphoreType.DMA((cap,))],
        2,
        20 * cap * rows * cols,
        40 * cap * rows * cols,
    )(table, scales, *states, *grads)


def late_kernel(table_ref, scale_ref, *refs):
    states, grads, outs, scratch = refs[:4], refs[4:8], refs[8:12], refs[12:]
    state_ref, result_ref, held_ref, sem_ref, state_sem_ref, out_sem_ref = scratch
    cap, rows, _ = held_ref.shape
    scalars = [scale_ref[at] for at in range(5)]

    def loads(slot):
        return [
            pltpu.make_async_copy(ref.at[slot], state_ref.at[slot, at], state_sem_ref.at[slot, at])
            for at, ref in enumerate(states)
        ]

    def stores(slot):
        return [
            pltpu.make_async_copy(result_ref.at[slot, at], ref.at[slot], out_sem_ref.at[slot, at])
            for at, ref in enumerate(outs)
        ]

    def each(work):
        @pl.loop(0, cap)
        def _(slot):
            @pl.when(table_ref[0, slot] < LATE)
            def _():
                work(slot)

    def begin(slot):
        for at, ref in enumerate(grads):
            @pl.when(table_ref[0, slot] == at)
            def _():
                fetch_gradient(ref, table_ref, slot, held_ref, sem_ref, rows).start()
        for copy in loads(slot):
            copy.start()

    def update(slot):
        fetch_gradient(grads[0], table_ref, slot, held_ref, sem_ref, rows).wait()
        for copy in loads(slot):
            copy.wait()
        gradient = held_ref[slot].astype(F32) * scale_ref[8 + 2 * slot]
        results = adamw_update(
            *[state_ref[slot, at] for at in range(4)], gradient, scale_ref[9 + 2 * slot], scalars
        )
        for at, value in enumerate(results):
            result_ref[slot, at] = value
        for copy in stores(slot):
            copy.start()

    def finish(slot):
        for copy in stores(slot):
            copy.wait()

    each(begin)
    each(update)
    each(finish)


def adamw_late(table, scales, states, grads, kept):
    cap, rows, cols = states[0].shape
    return call(
        late_kernel,
        (1,),
        [ANY] * 8,
        [ANY] * 4,
        [struct(states[0].shape, F32)] * 4,
        [
            pltpu.VMEM((cap, 4, rows, cols), F32),
            pltpu.VMEM((cap, 4, rows, cols), F32),
            pltpu.VMEM((cap, rows, cols), BF),
            pltpu.SemaphoreType.DMA((cap,)),
            pltpu.SemaphoreType.DMA((cap, 4)),
            pltpu.SemaphoreType.DMA((cap, 4)),
        ],
        2,
        20 * cap * rows * cols,
        40 * cap * rows * cols,
        0,
        kept,
    )(table, scales, *states, *grads, *kept)


def on_device(
    tokens,
    cotangent,
    phase_of,
    unit_slot,
    step_count,
    learn_rates,
    decay_rates,
    master,
    first_moment,
    second_moment,
    average,
    vector_state,
):
    cap, unit_rows, cols = master.shape
    tok_rows, width = tokens.shape
    batch_count = lax.axis_size("batch")
    row_blocks = width // unit_rows
    col_blocks = FF // width
    core = lax.axis_index("tensor")
    place = lax.axis_index("batch")
    fast = batch_count == FAST_BATCH
    plane, y_at, x_at = place // 4, (place // 2) % 2, place % 2
    up_base = 4 * row_blocks
    down_base = up_base + row_blocks * col_blocks
    chunks = [(0, 1, row_blocks), (up_base, col_blocks, 1), (down_base, col_blocks, 1)]
    corner = jnp.stack([place % 4, place % 4, plane]).astype(jnp.int32)

    def coords(orient):
        y_first = (core + orient) % 2 == 0
        first = jnp.where(y_first, y_at, x_at)
        second = jnp.where(y_first, x_at, y_at)
        return jnp.stack([first, second, plane]).astype(jnp.int32)

    places = [coords(orient) for orient in range(2)]

    def chunk_units(chunk):
        base, row_step, block_step = chunk
        return base + jnp.arange(4)[:, None] * block_step + jnp.arange(row_blocks)[None] * row_step

    def spreads(sources, which):
        first_bit = jnp.where(core == 0, 2, 1)
        inner = place % 4
        numbers = jnp.stack(
            [
                places[0][0] * 2 + places[0][1], plane, place,
                inner, inner ^ first_bit, inner ^ (3 - first_bit), inner ^ 3,
            ]
        ).astype(jnp.int32)
        return [spread(sources, unit_slot, numbers, chunks[at]) for at in which]

    def weights_chain(pieces):
        return Chain(spreading(pieces, 0, places[0]))

    def weights_plain(at):
        local = unit_slot[chunk_units(chunks[at])] - place * cap
        own = (local >= 0) & (local < cap)
        blocks = jnp.take(master, jnp.clip(local, 0, cap - 1), axis=0)
        blocks = jnp.where(own[..., None, None], blocks, 0.0).astype(BF)
        return lax.psum(blocks.reshape(4, width, cols), "batch")

    def grads_chain(mine, other):
        going, kept = first_split(places[0], mine, other)
        return Chain(exchange(going, kept, 0, places[0]))

    def shared(array_in):
        half = array_in.shape[1] // 2
        parts = [array_in[:, :half], array_in[:, half:]]
        return parts + [core_swap(part) for part in parts]

    def halves_of(array_in):
        other = lax.dynamic_slice_in_dim(array_in, (1 - core) * cols, cols, array_in.ndim - 1)
        return lax.dynamic_slice_in_dim(array_in, core * cols, cols, array_in.ndim - 1), other

    def swapped(array_in):
        return jnp.concatenate(halves_of(array_in), axis=-1)

    def both(here, there):
        low_first = core == 0
        return jnp.concatenate(
            [jnp.where(low_first, here, there), jnp.where(low_first, there, here)], axis=0
        )

    count_f = step_count[0].astype(F32)
    scalars = [
        decay_rates[0],
        decay_rates[1],
        decay_rates[2],
        1.0 / (1.0 - decay_rates[0] ** count_f),
        1.0 / (1.0 - decay_rates[1] ** count_f),
    ]

    def vec_update(sums):
        vector_grads = jnp.concatenate(
            [sums[0:2], sums[8:11], sums[12:16], sums[16:19]], axis=0
        )
        grads_scaled = vector_grads * float(tok_rows * batch_count) ** (-0.5)
        vec_weights, vec_first, vec_second, vec_average = adamw_update(
            vector_state[0], vector_state[1], vector_state[2], vector_state[3],
            grads_scaled, learn_rates[4], scalars,
        )
        return (
            jnp.stack([vec_weights, vec_average]),
            jnp.stack([grads_scaled, vec_first]),
            vec_second,
        )

    my_ids = place * cap + jnp.arange(cap, dtype=jnp.int32)
    matches = unit_slot[None, :] == my_ids[:, None]
    unit_ids = jnp.arange(unit_slot.shape[0], dtype=jnp.int32)
    unit = jnp.sum(jnp.where(matches, unit_ids[None, :], 0), axis=1)
    occupied = jnp.any(matches, axis=1)
    is_up = (unit >= up_base) & (unit < down_base)
    is_down = unit >= down_base
    is_other = (unit >= 3 * row_blocks) & (unit < up_base)
    is_wide = is_up | is_down
    chunk_at = jnp.where(is_down, 2, jnp.where(is_up | is_other, 1, 0))
    local = unit - jnp.where(is_down, down_base, up_base)
    block_at = jnp.where(
        is_wide, local % col_blocks, jnp.where(is_other, col_blocks, unit // row_blocks)
    )
    row_at = jnp.where(is_wide, local // col_blocks, unit % row_blocks)
    kind = jnp.where(
        occupied,
        (unit >= 3 * row_blocks).astype(jnp.int32) + is_up.astype(jnp.int32) + 2 * is_down,
        0,
    )
    rates = jnp.sum(
        jnp.where(kind[:, None] == jnp.arange(4)[None, :], learn_rates[None, :4], 0.0), axis=1
    )
    quarter_rows, half_rows = row_blocks // 4, row_blocks // 2
    first_quarter, first_half = (corner[0], places[0][0]) if fast else (0, 0)
    array_at = jnp.where(
        chunk_at == 0,
        (row_at // quarter_rows) ^ first_quarter,
        2 + 2 * chunk_at + ((row_at // half_rows) ^ first_half),
    )
    row_at = jnp.where(chunk_at == 0, row_at % quarter_rows, row_at % half_rows)
    table = jnp.stack([array_at, block_at, row_at]).astype(jnp.int32)
    states = (master, first_moment, second_moment, average)
    scales = jnp.concatenate(
        [
            jnp.stack(scalars),
            jnp.zeros((3,), F32),
            jnp.stack([occupied.astype(F32), rates], axis=1).reshape(-1),
        ]
    )
    firsts = [places[0][0], places[1][0]] if fast else [0, 0]
    info = jnp.stack([phase_of[0], core, *firsts]).astype(jnp.int32)
    vectors = vector_state[0]
    rows = jnp.concatenate(
        [swapped(vectors[0:2]), vectors[2:5], vectors[9:12]], axis=0
    )
    upper = vectors[5:9].reshape(2, FF // 2)
    turned = jnp.concatenate([upper[1:], upper[:1]], axis=0)
    bias_up = jnp.where(core == 0, upper, turned).reshape(4, width)

    if fast:
        low_master = master.astype(BF)
        beside = lax.ppermute(low_master, BOTH, swap_pairs(0, 1))
        across = lax.ppermute(low_master, BOTH, swap_pairs(0, 2))
        diagonal = lax.ppermute(beside, BOTH, swap_pairs(0, 2))
        sources = (low_master, beside, across, diagonal)
        io = weights_chain(spreads(sources, (0,))[0])
        _, (up, down) = phase([io], work=lambda _: spreads(sources, (1, 2)))
        up, down = weights_chain(up), weights_chain(down)
        phase([io])
        phase([io, up])
        theirs_first, _ = phase([io, up], io.ready)
        theirs_last, _ = phase([up, down], io.result[1:])
        weights_io = [*io.result, *theirs_first, *theirs_last]
        theirs_first, stage = phase(
            [up, down],
            up.ready,
            lambda late: forward(0, after(info, late), tokens, rows, weights_io),
        )
        theirs_last, stage = phase(
            [down],
            up.result[1:],
            lambda late: forward(1, after(info, late), tokens, rows, weights_io, kept=stage),
        )
        weights_up = [*up.result, *theirs_first, *theirs_last]
        q, k, v, ctx, lse, first, x_t = stage
        theirs_first, (act, slope, hidden_t, hidden) = phase(
            [down],
            down.ready,
            lambda late: feed_up(after(info, late), first, rows, bias_up, weights_up),
        )
        theirs_last, _ = phase(swaps=down.result[1:])
        weights_down = [*down.result, *theirs_first, *theirs_last]
    else:
        weights_io, weights_up, weights_down = [shared(weights_plain(at)) for at in range(3)]
        stage = None
        for group in range(tok_rows // 2 // LONG):
            stage = forward(group, info, tokens, rows, weights_io, kept=stage)
        q, k, v, ctx, lse, first, x_t = stage
        act, slope, hidden_t, hidden = feed_up(info, first, rows, bias_up, weights_up)

    out_half, dz2, down_theirs, grad_two_t, sums_two = feed_down(
        info, hidden, act, cotangent, rows, weights_down
    )
    heads = (q, k, v)

    def back(info):
        return feed_back(
            info, first, dz2, slope, rows, weights_down, weights_up, weights_io
        )

    def heads_back(group, info, dctx, dz1, kept=None):
        return attend_back(group, info, *heads, dctx, lse, dz1, weights_io, kept=kept)

    if fast:
        (other,), (down_mine,) = phase(
            swaps=[down_theirs], work=lambda late: wide_grad(after(grad_two_t, late), act, (0,))
        )
        down = grads_chain(down_mine, other)
        (out_other,), (dz1, dctx, dt_t, grad_up, sums_one) = phase(
            [down], [out_half], lambda late: back(after(info, late))
        )
        _, (up_mine, up_theirs) = phase(
            [down],
            work=lambda late: square_grad(
                dt_t, ctx, 4, wide_grad(after(hidden_t, late), grad_up, (0, 1), 5)
            ),
        )
        (other,), (kept, sums_zero) = phase(
            [down], [up_theirs], lambda late: heads_back(0, after(info, late), dctx, dz1)
        )
        up = grads_chain(up_mine, other)
        _, (kept, sums_extra) = phase(
            [down, up],
            work=lambda late: heads_back(1, after(info, late), dctx, dz1, kept),
        )
        dqkv, grad_x = kept
        vec = Chain(doubling(jnp.concatenate([sums_zero + sums_extra, sums_one, sums_two])))
        _, io_theirs = phase(
            [down, up, vec], work=lambda late: share_grad(after(x_t, late), dqkv, 1)
        )
        (other,), io_mine = phase(
            [down, up, vec], [io_theirs], lambda late: share_grad(after(x_t, late), dqkv, 0)
        )
        io = Chain(plane_exchange(quarters(corner, io_mine, other), corner))
        (grad_x_other,), out = phase(
            [io, up, vec], [grad_x], lambda late: both(after(out_half, late), out_other)
        )
        _, input_grad = phase(
            [io, up, vec],
            work=lambda late: both(after(grad_x, late), grad_x_other).astype(F32),
        )
        phase([io, up, vec])
        _, (new_states, vec_outs) = phase(
            [io],
            work=lambda late: (
                adamw_slots(after(table, late), scales, states, [*up.result, *down.result]),
                vec_update(after(vec.result, late)),
            ),
        )
        grads = io.result
    else:
        dz1, dctx, dt_t, grad_up, sums_one = back(info)
        kept, sums_zero = None, 0.0
        for group in range(tok_rows // 2 // LONG):
            kept, sums_extra = heads_back(group, info, dctx, dz1, kept)
            sums_zero = sums_zero + sums_extra
        dqkv, grad_x = kept
        up_mine, up_theirs = square_grad(
            dt_t, ctx, 4, wide_grad(hidden_t, grad_up, (0, 1), 5)
        )
        (down_mine,) = wide_grad(grad_two_t, act, (0,))
        grads = []
        for mine, theirs, parts in (
            (share_grad(x_t, dqkv, 0), share_grad(x_t, dqkv, 1), 4),
            (up_mine, up_theirs, 2),
            (down_mine, down_theirs, 2),
        ):
            grad = lax.psum(total(mine, core_swap(theirs)), "batch")
            grads += jnp.split(grad, parts, axis=1)
        new_states = adamw_slots(table, scales, states, grads[4:])
        grads = grads[:4]
        vec_outs = vec_update(
            lax.psum(jnp.concatenate([sums_zero, sums_one, sums_two]), BOTH)
        )
        out = both(out_half, core_swap(out_half))
        input_grad = both(grad_x, core_swap(grad_x)).astype(F32)

    new_states = adamw_late(table, scales, states, grads, new_states)
    return (out, input_grad, *new_states, *vec_outs)


def solution(mesh):
    return jax.shard_map(
        on_device,
        mesh=mesh,
        in_specs=(
            P("batch", None),
            P("batch", None),
            P("batch"),
            P(),
            P(),
            P(),
            P(),
            P("batch", None, "tensor"),
            P("batch", None, "tensor"),
            P("batch", None, "tensor"),
            P("batch", None, "tensor"),
            P(),
        ),
        out_specs=(
            P("batch", None),
            P("batch", None),
            P("batch", None, "tensor"),
            P("batch", None, "tensor"),
            P("batch", None, "tensor"),
            P("batch", None, "tensor"),
            P(),
            P(),
            P(),
        ),
        check_vma=False,
    )
```

```python
import functools

import jax
import jax.numpy as jnp
from jax import lax
from jax.experimental import pallas as pl
from jax.experimental.pallas import tpu as pltpu
from jax.sharding import PartitionSpec as P

HD = 64
FF = 3072
SHORT = 128
LONG = 512
EPS = 1e-12
BF = jnp.bfloat16
F32 = jnp.float32
VMEM_BYTES = 60 * 2**20
BOTH = ("batch", "tensor")
ANY = pl.BlockSpec(memory_space=pl.ANY)
PLANES = 4
FAST_BATCH = 16


def dot(first_mat, second_mat):
    return lax.dot_general(
        first_mat, second_mat, (((1,), (0,)), ((), ())), preferred_element_type=F32
    )


def dot_nt(first_mat, second_mat):
    return lax.dot_general(
        first_mat, second_mat, (((1,), (1,)), ((), ())), preferred_element_type=F32
    )


def normalized(rows):
    centred = rows - jnp.mean(rows, axis=-1, keepdims=True)
    inverse = lax.rsqrt(jnp.mean(centred * centred, axis=-1, keepdims=True) + EPS)
    return centred * inverse, inverse


def norm_back(grad_scaled, normal, inverse):
    mean_grad = jnp.mean(grad_scaled, axis=-1, keepdims=True)
    mean_both = jnp.mean(grad_scaled * normal, axis=-1, keepdims=True)
    return inverse * (grad_scaled - mean_grad - normal * mean_both)


def fold_rows(array_in):
    rows, cols = array_in.shape
    return jnp.sum(array_in.reshape(rows // 8, 8, cols), axis=0)


def row_sum(array_in):
    return jnp.sum(array_in, axis=0, keepdims=True)


def load_blocks(info_ref, parts, blocks, weight_ref, sem_ref):
    _, half_rows, cols = parts[0].shape
    copies = []
    for spot, (half, block) in enumerate(blocks):
        first = info_ref[2 + half]
        pair = []
        for at in range(2):
            start = pl.multiple_of((first if at == 0 else 1 - first) * half_rows, half_rows)
            pair.append(
                pltpu.make_async_copy(
                    parts[2 * half + at].at[block],
                    weight_ref.at[pl.ds(start, half_rows), pl.ds(spot * cols, cols)],
                    sem_ref.at[2 * spot + at],
                )
            )
        copies.append(pair)
    return copies


def after(array_in, *others):
    return lax.optimization_barrier((array_in, others))[0]


def first_time(copies):
    @pl.when(pl.program_id(0) == 0)
    def _():
        for pair in copies:
            for copy in pair:
                copy.wait()


def start_first(copies):
    @pl.when(pl.program_id(0) == 0)
    def _():
        for pair in copies:
            for copy in pair:
                copy.start()


PAIRED = [(half, block) for block in range(4) for half in range(2)]
SHARES = [(half, block) for half in range(2) for block in range(3)]
HALVED = [(half, block) for half in range(2) for block in range(4)]


def call(
    kernel, grid, in_specs, out_specs, out_shape, scratch, prefetch, flops, moved, exps=0, kept=None
):
    aliases = {}
    if kept is not None:
        given = prefetch + len(in_specs)
        count = len(kept)
        in_specs = in_specs + [ANY] * count
        aliases = {given + at: at for at in range(count)}
        inner = kernel

        def kernel(*refs):
            inner(*refs[:given], *refs[given + count :])

    return pl.pallas_call(
        kernel,
        input_output_aliases=aliases,
        out_shape=out_shape,
        grid_spec=pltpu.PrefetchScalarGridSpec(
            num_scalar_prefetch=prefetch,
            grid=grid,
            in_specs=in_specs,
            out_specs=out_specs,
            scratch_shapes=scratch,
        ),
        compiler_params=pltpu.CompilerParams(vmem_limit_bytes=VMEM_BYTES),
        cost_estimate=pl.CostEstimate(
            flops=30 * flops, bytes_accessed=moved, transcendentals=exps
        ),
    )


def struct(shape, kind):
    return jax.ShapeDtypeStruct(shape, kind)


def spread_kernel(
    base, row_step, block_step, cap, rows, info_ref, slot_ref, *refs
):
    sources, outs, (held_ref, quarter_ref, sem_ref) = refs[:4], refs[4:8], refs[8:]
    block = pl.program_id(0)
    quarter, plane, place = info_ref[0], info_ref[1], info_ref[2]
    copies = [
        [
            pltpu.make_async_copy(
                ref, held_ref.at[pl.ds(info_ref[3 + at] * cap, cap)], sem_ref.at[at]
            )
        ]
        for at, ref in enumerate(sources)
    ]
    start_first(copies)
    first_time(copies)
    total_slots = PLANES * cap
    for step in range(3):
        unit = base + (quarter * 3 + step) * row_step + block * block_step
        local = slot_ref[unit] - plane * total_slots
        here = (local >= 0) & (local < total_slots)
        spot = slice(step * rows, (step + 1) * rows)

        @pl.when(here)
        def _():
            quarter_ref[spot, :] = held_ref[local]

        @pl.when(jnp.logical_not(here))
        def _():
            quarter_ref[spot, :] = jnp.zeros((rows, quarter_ref.shape[1]), BF)

    for ahead, out_ref in enumerate(outs):
        size = out_ref.shape[1]
        start = pl.multiple_of(lax.rem(plane + ahead, PLANES) * size, size)
        out_ref[0] = quarter_ref[pl.ds(start, size), :]


def spread(sources, unit_slot, info, chunk):
    cap, rows, cols = sources[0].shape
    base, row_step, block_step = chunk
    size = 3 * rows // PLANES
    block = pl.BlockSpec((1, size, cols), lambda i, *_: (i, 0, 0))
    return call(
        functools.partial(spread_kernel, base, row_step, block_step, cap, rows),
        (4,),
        [ANY] * 4,
        [block] * 4,
        [struct((4, size, cols), BF)] * 4,
        [
            pltpu.VMEM((PLANES * cap, rows, cols), BF),
            pltpu.VMEM((3 * rows, cols), BF),
            pltpu.SemaphoreType.DMA((4,)),
        ],
        2,
        0,
        5 * 2**20,
    )(info, unit_slot, *sources)


def swap_pairs(orient, stage):
    pairs = []
    for place in range(FAST_BATCH):
        for core in range(2):
            first_bit = 2 if (core + orient) % 2 == 0 else 1
            bit = first_bit if stage == 1 else 3 - first_bit
            pairs.append((place * 2 + core, (place ^ bit) * 2 + core))
    return pairs


def flip_pairs(bit):
    return [
        (place * 2 + core, (place ^ bit) * 2 + core)
        for place in range(FAST_BATCH)
        for core in range(2)
    ]


def plane_pairs(step):
    return [
        (place * 2 + core, (place + 4 * step) % FAST_BATCH * 2 + core)
        for place in range(FAST_BATCH)
        for core in range(2)
    ]


def total(*terms):
    result = terms[0].astype(F32)
    for term in terms[1:]:
        result = result + term.astype(F32)
    return result.astype(BF)


def send(array_in, pairs):
    return lax.ppermute(array_in, BOTH, pairs)


def cut(array_in, start, size):
    return lax.dynamic_slice_in_dim(array_in, start, size, 1)


def first_split(info, terms):
    half = terms[0].shape[1] // 2
    return total(*[cut(term, (1 - info[0]) * half, half) for term in terms])


def second_split(info, terms, got):
    half = got.shape[1] // 2
    start = (1 - info[1]) * half
    kept = [cut(term, info[0] * got.shape[1] + start, half) for term in terms]
    return total(*kept, cut(got, start, half))


def third_split(info, terms, one, two):
    half = two.shape[1]
    size = half // PLANES
    pieces = []
    for ahead in range(PLANES):
        start = (info[2] + ahead) % PLANES * size
        first = info[1] * half + start
        kept = [cut(term, info[0] * one.shape[1] + first, size) for term in terms]
        pieces.append(total(*kept, cut(one, first, size), cut(two, start, size)))
    return pieces


def plane_join(info, pieces):
    return jnp.concatenate(
        [lax.select_n((info[2] - row) % PLANES, *pieces) for row in range(PLANES)], axis=1
    )


def half_join(info, here, there):
    low_first = info[1] == 0
    return jnp.concatenate(
        [jnp.where(low_first, here, there), jnp.where(low_first, there, here)], axis=1
    )


def exchange(terms, orient, info):
    (one,) = yield [(first_split(info, terms), swap_pairs(orient, 1))]
    (two,) = yield [(second_split(info, terms, one), swap_pairs(orient, 2))]
    own, *pieces = third_split(info, terms, one, two)
    return (yield from spreading([own] + pieces, orient, info))


def spreading(pieces, orient, info):
    arrived = yield [(pieces[step], plane_pairs(step)) for step in range(1, PLANES)]
    owned = total(pieces[0], *arrived)
    others = yield [(owned, plane_pairs(step)) for step in range(1, PLANES)]
    level = plane_join(info, [owned] + others)
    (there,) = yield [(level, swap_pairs(orient, 2))]
    level = half_join(info, level, there)
    (there,) = yield [(level, swap_pairs(orient, 1))]
    return level, there


def plane_exchange(terms, info):
    quarter = terms[0].shape[1] // 4
    size = quarter // PLANES
    going = [
        total(*[cut(term, (info[0] ^ away) * quarter, quarter) for term in terms])
        for away in (1, 2, 3)
    ]
    got = yield [(piece, flip_pairs(away)) for away, piece in zip((1, 2, 3), going)]
    parts = []
    for ahead in range(PLANES):
        start = (info[2] + ahead) % PLANES * size
        kept = [cut(term, info[0] * quarter + start, size) for term in terms]
        parts.append(total(*kept, *[cut(piece, start, size) for piece in got]))
    arrived = yield [(parts[step], plane_pairs(step)) for step in range(1, PLANES)]
    owned = total(parts[0], *arrived)
    others = yield [(owned, plane_pairs(step)) for step in range(1, PLANES)]
    level = plane_join(info, [owned] + others)
    there = yield [(level, flip_pairs(away)) for away in (1, 2, 3)]
    return [level] + there


def doubling(array_in):
    cores = [(at, at ^ 1) for at in range(2 * FAST_BATCH)]
    for pairs in [cores] + [flip_pairs(bit) for bit in (1, 2, 4, 8)]:
        (other,) = yield [(array_in, pairs)]
        array_in = array_in + other
    return array_in


class Chain:
    def __init__(self, steps):
        self.steps = steps
        self.result = None
        self.pending = next(steps)

    @property
    def ready(self):
        return [parts for parts, _ in self.pending]

    def take(self, arrived):
        try:
            self.pending = self.steps.send(arrived)
        except StopIteration as stop:
            self.pending, self.result = [], stop.value


def phase(chains=(), swaps=(), work=None):
    ready, swaps = lax.optimization_barrier(([chain.ready for chain in chains], list(swaps)))
    arrived = [
        [send(parts, pairs) for parts, (_, pairs) in zip(given, chain.pending)]
        for given, chain in zip(ready, chains)
    ]
    swapped = [core_swap(array) for array in swaps]
    done = None if work is None else work((ready, swaps))
    arrived, swapped, done = lax.optimization_barrier((arrived, swapped, done))
    for chain, parts in zip(chains, arrived):
        chain.take(parts)
    return swapped, done


def core_swap(array_in):
    return lax.ppermute(array_in, "tensor", [(0, 1), (1, 0)])


def seen_mask():
    key_at = lax.broadcasted_iota(jnp.int32, (2 * LONG, LONG), 0) % LONG // SHORT
    query_at = lax.broadcasted_iota(jnp.int32, (2 * LONG, LONG), 1) // SHORT
    return key_at == query_at


def low_lanes(rows):
    return lax.broadcasted_iota(jnp.int32, (rows, 2 * HD), 1) < HD


def pair_lanes(pair):
    return pl.ds(pl.multiple_of(pair * 2 * HD, 2 * HD), 2 * HD)


def both_heads(array_in):
    low = low_lanes(array_in.shape[0])
    none = jnp.zeros_like(array_in)
    return jnp.concatenate(
        [jnp.where(low, array_in, none), jnp.where(low, none, array_in)], axis=0
    )


def by_head(array_in):
    return array_in.reshape(2, LONG, array_in.shape[1])


def pair_columns(array_in):
    return jnp.where(low_lanes(LONG), array_in[:LONG], array_in[LONG:])


FORWARD_PAIRS = 2
BACKWARD_PAIRS = 1


def attend_pairs(first, short, q_ref, k_ref, v_ref, ctx_ref, lse_ref):
    pairs = range(FORWARD_PAIRS)
    lanes = [pair_lanes(first + pair) for pair in pairs]
    queries = [q_ref[:, at] * BF(HD**-0.5) for at in lanes]
    keys_here = [both_heads(k_ref[:, at]) for at in lanes]
    values_t = [v_ref[:, at].T for at in lanes]
    scores = [dot_nt(keys_here[pair], queries[pair]) for pair in pairs]
    if short:
        scores = [jnp.where(seen_mask(), score, -1e30) for score in scores]
    scores = [by_head(score) for score in scores]
    tops = [jnp.max(score, axis=1, keepdims=True) for score in scores]
    weights = [jnp.exp(score - top) for score, top in zip(scores, tops)]
    norms = [jnp.sum(weight, axis=1, keepdims=True) for weight in weights]
    probs = [(weight * (1.0 / norm)).astype(BF) for weight, norm in zip(weights, norms)]
    for pair in pairs:
        outs = [
            dot(values_t[pair][head * HD : (head + 1) * HD], probs[pair][head])
            for head in range(2)
        ]
        ctx_ref[:, lanes[pair]] = jnp.concatenate(outs, axis=0).T.astype(BF)
        for head in range(2):
            spot = pl.ds((first + pair) * 2 + head, 1)
            lse_ref[0, spot, :] = tops[pair][head] + jnp.log(norms[pair][head])


def forward_kernel(
    info_ref, x_ref, rows_ref, w0_ref, w1_ref, w2_ref, w3_ref,
    q_ref, k_ref, v_ref, ctx_ref, lse_ref, z_ref, xt_ref, w_ref, sem_ref,
):
    width = x_ref.shape[1]
    parts = (w0_ref, w1_ref, w2_ref, w3_ref)
    copies = load_blocks(info_ref, parts, PAIRED, w_ref, sem_ref)
    start_first(copies)
    tokens = x_ref[...]
    xt_ref[...] = tokens.T
    first_time(copies[:2])
    q_ref[...] = (dot(tokens, w_ref[:, :width]) + rows_ref[0:1]).astype(BF)
    first_time(copies[2:4])
    k_ref[...] = dot(tokens, w_ref[:, width : 2 * width]).astype(BF)
    first_time(copies[4:6])
    v_ref[...] = (dot(tokens, w_ref[:, 2 * width : 3 * width]) + rows_ref[1:2]).astype(BF)
    pairs = width // (2 * HD)

    def all_pairs(short):
        @pl.loop(0, pairs, step=FORWARD_PAIRS)
        def _(first):
            attend_pairs(first, short, q_ref, k_ref, v_ref, ctx_ref, lse_ref)

    @pl.when(info_ref[0] == 1)
    def _():
        all_pairs(False)

    @pl.when(info_ref[0] != 1)
    def _():
        all_pairs(True)

    first_time(copies[6:8])
    attended = dot_nt(ctx_ref[...], w_ref[:, 3 * width :])
    z_ref[...] = tokens.astype(F32) + attended + rows_ref[2:3]


def forward(group, info, tokens, rows, weights, kept=None):
    tok = tokens.shape[0] // 2
    width = tokens.shape[1]
    groups = tok // LONG
    tile = pl.BlockSpec((LONG, width), lambda i, *_: (group, 0))
    low = struct((tok, width), BF)
    return call(
        forward_kernel,
        (1,),
        [
            pl.BlockSpec((LONG, width), lambda i, info: (info[1] * groups + group, 0)),
            pl.BlockSpec((8, width), lambda i, *_: (0, 0)),
        ]
        + [ANY] * 4,
        [
            tile, tile, tile, tile,
            pl.BlockSpec((1, 16, LONG), lambda i, *_: (group, 0, 0)),
            tile,
            pl.BlockSpec((width, LONG), lambda i, *_: (0, group)),
        ],
        [
            low, low, low, low,
            struct((groups, 16, LONG), F32),
            struct((tok, width), F32),
            struct((width, tok), BF),
        ],
        [pltpu.VMEM((width, 4 * width), BF), pltpu.SemaphoreType.DMA((16,))],
        1,
        2 * LONG * width * (4 * width + 2 * LONG) * 2,
        12 * 2**20,
        LONG * LONG * 12,
        kept,
    )(info, tokens, rows, *weights, *(kept or ()))


def up_kernel(
    info_ref, z_ref, rows_ref, bias_ref, w0_ref, w1_ref, w2_ref, w3_ref,
    act_ref, slope_ref, ht_ref, hidden_ref, w_ref, sem_ref,
):
    width = z_ref.shape[1]
    parts = (w0_ref, w1_ref, w2_ref, w3_ref)
    copies = load_blocks(info_ref, parts, HALVED, w_ref, sem_ref)
    start_first(copies)
    normal, _ = normalized(z_ref[...])
    hidden = normal * rows_ref[3:4] + rows_ref[4:5]
    hidden_ref[...] = hidden
    low = hidden.astype(BF)
    ht_ref[...] = low.T
    for part in range(FF // width):
        spot = slice(part * width, (part + 1) * width)
        first_time(copies[2 * part : 2 * part + 2])
        upper = dot(low, w_ref[:, spot]) + bias_ref[part : part + 1]
        phi_sum = 0.5 + 0.5 * lax.erf(upper * (0.5**0.5))
        density = jnp.exp(-0.5 * upper * upper) * 0.3989422804014327
        act_ref[:, spot] = (upper * phi_sum).astype(BF)
        slope_ref[:, spot] = (phi_sum + upper * density).astype(BF)


ROWS, COLUMNS, NORM_ROWS = 256, 256, 128
UP_TILE = 256


def feed_up(info, first, rows, bias, weights):
    tok, width = first.shape
    wide = struct((tok, FF), BF)
    return call(
        up_kernel,
        (tok // UP_TILE,),
        [
            pl.BlockSpec((UP_TILE, width), lambda i, *_: (i, 0)),
            pl.BlockSpec((8, width), lambda i, *_: (0, 0)),
            pl.BlockSpec((4, width), lambda i, *_: (0, 0)),
        ]
        + [ANY] * 4,
        [
            pl.BlockSpec((UP_TILE, FF), lambda i, *_: (i, 0)),
            pl.BlockSpec((UP_TILE, FF), lambda i, *_: (i, 0)),
            pl.BlockSpec((width, UP_TILE), lambda i, *_: (0, i)),
            pl.BlockSpec((UP_TILE, width), lambda i, *_: (i, 0)),
        ],
        [wide, wide, struct((width, tok), BF), struct((tok, width), F32)],
        [pltpu.VMEM((width, FF), BF), pltpu.SemaphoreType.DMA((16,))],
        1,
        2 * tok * width * FF,
        20 * 2**20,
        tok * FF * 2,
    )(info, first, rows, bias, *weights)


PARTS = 4


def wait_pairs(copies):
    for pair in copies:
        for copy in pair:
            copy.wait()


def down_kernel(info_ref, h_in_ref, act_ref, cot_in_ref, rows_ref, *refs):
    parts, outs, gt_ref, sum_ref = refs[:4], refs[4:7], refs[7], refs[8]
    w_ref, h_ref, cot_ref, branch_ref = refs[9:13]
    out_ref, dz_ref, dyt_ref, low_ref, sem_ref, own_sem_ref = refs[13:]
    step = pl.program_id(0)
    tok, width = h_ref.shape
    copies = load_blocks(info_ref, parts, HALVED, w_ref, sem_ref)
    start = pl.multiple_of(info_ref[1] * tok, tok)
    h_copy = pltpu.make_async_copy(h_in_ref, h_ref, own_sem_ref.at[0])
    cot_copy = pltpu.make_async_copy(
        cot_in_ref.at[pl.ds(start, tok)], cot_ref, own_sem_ref.at[1]
    )
    out_copies = [
        pltpu.make_async_copy(source, target, own_sem_ref.at[2 + at])
        for at, (source, target) in enumerate(zip((out_ref, dz_ref, dyt_ref), outs))
    ]
    start_first(copies)

    @pl.when(step == 0)
    def _():
        h_copy.start()
        cot_copy.start()
        sum_ref[...] = jnp.zeros_like(sum_ref)

    for part in range(PARTS):
        @pl.when(step == part)
        def _():
            wait_pairs(copies[2 * part : 2 * part + 2])
            lanes = slice(part * width, (part + 1) * width)
            branch = dot_nt(act_ref[...], w_ref[:, lanes])
            branch_ref[...] = branch if part == 0 else branch_ref[...] + branch

    @pl.when(step == PARTS - 1)
    def _():
        h_copy.wait()
        cot_copy.wait()
        gains = rows_ref[6:7]
        sums = [0.0, 0.0, 0.0]
        for row in range(0, tok, NORM_ROWS):
            spot = slice(row, row + NORM_ROWS)
            normal, inverse = normalized(h_ref[spot, :] + branch_ref[spot, :] + rows_ref[5:6])
            out_ref[spot, :] = (normal * gains + rows_ref[7:8]).astype(BF)
            cot = cot_ref[spot, :].astype(F32)
            grad = norm_back(cot * gains, normal, inverse)
            dz_ref[spot, :] = grad
            low_ref[spot, :] = grad.astype(BF)
            for at, value in enumerate((grad, cot * normal, cot)):
                sums[at] = sums[at] + fold_rows(value)
        dyt_ref[...] = low_ref[...].T
        for at in range(3):
            sum_ref[at : at + 1] += row_sum(sums[at])
        for copy in out_copies:
            copy.start()

    @pl.when(step >= PARTS)
    def _():
        put_blocks(gt_ref, dot(dyt_ref[...], act_ref[...]))

    @pl.when(step == PARTS + 1)
    def _():
        for copy in out_copies:
            copy.wait()


def put_blocks(ref, grad):
    cols = ref.shape[2]
    for block in range(ref.shape[0]):
        ref[block] = grad[:, block * cols : (block + 1) * cols].astype(BF)


def feed_down(info, hidden, act, cot, rows, weights):
    tok, width = hidden.shape
    wide = (tok, width)
    return call(
        down_kernel,
        (PARTS + 2,),
        [
            ANY,
            pl.BlockSpec(wide, lambda i, *_: (0, jnp.where(i < PARTS, i, i - 2))),
            ANY,
            pl.BlockSpec((8, width), lambda i, *_: (0, 0)),
        ]
        + [ANY] * 4,
        [
            ANY,
            ANY,
            ANY,
            pl.BlockSpec((2, width, width // 2), lambda i, *_: (jnp.clip(i - PARTS, 0, 1), 0, 0)),
            pl.BlockSpec((8, width), lambda i, *_: (0, 0)),
        ],
        [
            struct(wide, BF),
            struct(wide, F32),
            struct((width, tok), BF),
            struct((4, width, width // 2), BF),
            struct((8, width), F32),
        ],
        [
            pltpu.VMEM((width, FF), BF),
            pltpu.VMEM(wide, F32),
            pltpu.VMEM(wide, BF),
            pltpu.VMEM(wide, F32),
            pltpu.VMEM(wide, BF),
            pltpu.VMEM(wide, F32),
            pltpu.VMEM((width, tok), BF),
            pltpu.VMEM(wide, BF),
            pltpu.SemaphoreType.DMA((16,)),
            pltpu.SemaphoreType.DMA((5,)),
        ],
        1,
        3 * tok * width * FF,
        30 * 2**20,
    )(info, hidden, act, cot, rows, *weights)


def back_kernel(info_ref, z_in_ref, dz2_ref, slope_ref, rows_ref, *refs):
    down, upper, other = refs[:4], refs[4:8], refs[8:12]
    outs, da_ref, sum_ref = refs[12:15], refs[15], refs[16]
    wd_ref, wu_ref, wo_ref, z_ref, hidden_ref, low_ref, held_ref = refs[17:24]
    dz1_ref, dctx_ref, dtt_ref, dsem_ref, usem_ref, osem_ref, own_sem_ref = refs[24:]
    step = pl.program_id(0)
    tok, width = z_ref.shape
    downs = load_blocks(info_ref, down, HALVED, wd_ref, dsem_ref)
    ups = load_blocks(info_ref, upper, HALVED, wu_ref, usem_ref)
    others = load_blocks(info_ref, other, [(0, 3), (1, 3)], wo_ref, osem_ref)
    z_copy = pltpu.make_async_copy(z_in_ref, z_ref, own_sem_ref.at[0])
    for at in range(0, 8, 2):
        start_first(downs[at : at + 2] + ups[at : at + 2])
    start_first(others + [[z_copy]])

    @pl.when(step == 0)
    def _():
        sum_ref[...] = jnp.zeros_like(sum_ref)
        hidden_ref[...] = dz2_ref[...]
        low_ref[...] = dz2_ref[...].astype(BF)

    for part in range(PARTS + 1):
        @pl.when(step == part)
        def _():
            if part < PARTS:
                wait_pairs(downs[2 * part : 2 * part + 2])
            if part > 0:
                wait_pairs(ups[2 * part - 2 : 2 * part])
            place = 4 + (part ^ (2 * info_ref[1]))
            for column in range(0, width, COLUMNS):
                spot = slice(column, column + COLUMNS)
                lanes = slice(part * width + column, part * width + column + COLUMNS)
                if part < PARTS:
                    grad_act = dot(low_ref[...], wd_ref[:, lanes])
                if part > 0:
                    before = slice((part - 1) * width, part * width)
                    hidden_ref[:, spot] += dot_nt(held_ref[(part - 1) % 2], wu_ref[spot, before])
                if part < PARTS:
                    grad_up = (grad_act * slope_ref[:, spot].astype(F32)).astype(BF)
                    da_ref[:, spot] = grad_up
                    held_ref[part % 2, :, spot] = grad_up
                    sum_ref[pl.ds(place, 1), spot] = row_sum(fold_rows(grad_up.astype(F32)))

    @pl.when(step == PARTS)
    def _():
        z_copy.wait()
        gains = rows_ref[3:4]
        sums = [0.0, 0.0, 0.0]
        out_copies = []
        for half in range(2):
            rows = slice(half * (tok // 2), (half + 1) * (tok // 2))
            for row in range(rows.start, rows.stop, NORM_ROWS):
                spot = slice(row, row + NORM_ROWS)
                grad_hidden = hidden_ref[spot, :]
                normal, inverse = normalized(z_ref[spot, :])
                grad_one = norm_back(grad_hidden * gains, normal, inverse)
                dz1_ref[spot, :] = grad_one
                low_ref[spot, :] = grad_one.astype(BF)
                for at, value in enumerate((grad_one, grad_hidden * normal, grad_hidden)):
                    sums[at] = sums[at] + fold_rows(value)
            if half == 0:
                wait_pairs(others)
            dctx_ref[rows, :] = dot(low_ref[rows, :], wo_ref[...]).astype(BF)
            dtt_ref[:, rows] = low_ref[rows, :].T
            spot = pl.ds(rows.start, tok // 2)
            for at, (source, target) in enumerate(zip((dz1_ref, dctx_ref, dtt_ref), outs)):
                source, target = (
                    (source.at[:, spot], target.at[:, spot])
                    if at == 2
                    else (source.at[spot], target.at[spot])
                )
                out_copies.append(
                    pltpu.make_async_copy(source, target, own_sem_ref.at[1 + 3 * half + at])
                )
                out_copies[-1].start()
        for at in range(3):
            sum_ref[at : at + 1] = row_sum(sums[at])
        for copy in out_copies:
            copy.wait()


def feed_back(info, first, dz2, slope, rows, down, upper, other):
    tok, width = first.shape
    wide = (tok, width)
    fixed = pl.BlockSpec((8, width), lambda i, *_: (0, 0))
    part = pl.BlockSpec(wide, lambda i, *_: (0, jnp.minimum(i, PARTS - 1)))
    return call(
        back_kernel,
        (PARTS + 1,),
        [ANY, pl.BlockSpec(wide, lambda i, *_: (0, 0)), part, fixed] + [ANY] * 12,
        [ANY, ANY, ANY, part, fixed],
        [
            struct(wide, F32),
            struct(wide, BF),
            struct((width, tok), BF),
            struct((tok, FF), BF),
            struct((8, width), F32),
        ],
        [
            pltpu.VMEM((width, FF), BF),
            pltpu.VMEM((width, FF), BF),
            pltpu.VMEM((width, width), BF),
            pltpu.VMEM(wide, F32),
            pltpu.VMEM(wide, F32),
            pltpu.VMEM(wide, BF),
            pltpu.VMEM((2, *wide), BF),
            pltpu.VMEM(wide, F32),
            pltpu.VMEM(wide, BF),
            pltpu.VMEM((width, tok), BF),
            pltpu.SemaphoreType.DMA((16,)),
            pltpu.SemaphoreType.DMA((16,)),
            pltpu.SemaphoreType.DMA((4,)),
            pltpu.SemaphoreType.DMA((7,)),
        ],
        1,
        4 * tok * width * FF,
        30 * 2**20,
    )(info, first, dz2, slope, rows, *down, *upper, *other)


def product_kernel(left_ref, right_ref, *outs):
    grad = dot(left_ref[...], right_ref[...])
    step = pl.program_id(0)
    for at, ref in enumerate(outs):
        @pl.when(step // 2 == at)
        def _():
            put_blocks(ref, grad)


def wide_grad(left_t, right, halves, blocks=4):
    width, tok = left_t.shape
    first = halves[0]
    spec = [
        pl.BlockSpec(
            (2, width, width // 2), lambda i, at=at: (jnp.clip(i - 2 * at, 0, 1), 0, 0)
        )
        for at in range(len(halves))
    ]
    return call(
        product_kernel,
        (2 * len(halves),),
        [
            pl.BlockSpec((width, tok), lambda i: (0, 0)),
            pl.BlockSpec((tok, width), lambda i: (0, (i + 2 * first) % 4)),
        ],
        spec,
        [struct((blocks, width, width // 2), BF)] * len(halves),
        [],
        0,
        tok * width * FF * len(halves),
        10 * 2**20 * len(halves),
    )(left_t, right)


def share_kernel(left_ref, right_ref, out_ref):
    put_blocks(out_ref, dot(left_ref[...], right_ref[...]))


def share_grad(left_t, right, half):
    width, tok = left_t.shape
    cols = right.shape[1] // 2
    shape = (3, width, cols // 3)
    return call(
        share_kernel,
        (1,),
        [
            pl.BlockSpec((width, tok), lambda i: (0, 0)),
            pl.BlockSpec((tok, cols), lambda i: (0, half)),
        ],
        [pl.BlockSpec(shape, lambda i: (0, 0, 0))],
        [struct(shape, BF)],
        [],
        0,
        2 * tok * width * cols,
        6 * 2**20,
    )(left_t, right)[0]


def up_grad_kernel(ht_ref, dtt_ref, da_ref, ctx_ref, gm_ref, gt_ref, held_ref, sem_ref):
    step = pl.program_id(0)
    cols = held_ref.shape[3]

    def copies(at):
        targets = (
            [(ref, PARTS) for ref in (gm_ref, gt_ref)]
            if at == PARTS
            else [((gm_ref, gt_ref)[at // 2], at % 2 * 2 + block) for block in range(2)]
        )
        return [
            pltpu.make_async_copy(
                held_ref.at[at % 2, block], ref.at[target], sem_ref.at[at % 2, block]
            )
            for block, (ref, target) in enumerate(targets)
        ]

    for at in range(PARTS + 1):
        @pl.when(step == at)
        def _():
            left, right = (dtt_ref, ctx_ref) if at == PARTS else (ht_ref, da_ref)
            grad = dot(left[...], right[...])
            if at >= 2:
                for copy in copies(at - 2):
                    copy.wait()
            for block in range(2):
                held_ref[at % 2, block] = grad[:, block * cols : (block + 1) * cols].astype(BF)
            for copy in copies(at):
                copy.start()
            if at == PARTS:
                for copy in copies(at - 1) + copies(at):
                    copy.wait()


def up_grad(hidden_t, dt_t, grad_up, ctx):
    width, tok = hidden_t.shape
    cols = width // 2
    whole = pl.BlockSpec((width, tok), lambda i: (0, 0))
    return call(
        up_grad_kernel,
        (PARTS + 1,),
        [
            whole,
            whole,
            pl.BlockSpec((tok, width), lambda i: (0, jnp.minimum(i, PARTS - 1))),
            pl.BlockSpec((tok, width), lambda i: (0, 0)),
        ],
        [ANY, ANY],
        [struct((PARTS + 1, width, cols), BF)] * 2,
        [pltpu.VMEM((2, 2, width, cols), BF), pltpu.SemaphoreType.DMA((2, 2))],
        0,
        2 * tok * width * (FF + width),
        25 * 2**20,
    )(hidden_t, dt_t, grad_up, ctx)


def attend_pairs_back(first, short, q_ref, k_ref, v_ref, dctx_ref, lse_ref, dqkv_ref):
    width = q_ref.shape[1]
    pairs = range(BACKWARD_PAIRS)
    lanes = [pair_lanes(first + pair) for pair in pairs]
    queries = [q_ref[:, at] * BF(HD**-0.5) for at in lanes]
    keys_here = [k_ref[:, at] for at in lanes]
    grads = [dctx_ref[:, at] for at in lanes]
    keys_t = [keys.T for keys in keys_here]
    scores = [dot_nt(both_heads(keys_here[pair]), queries[pair]) for pair in pairs]
    grad_probs = [
        by_head(dot_nt(both_heads(v_ref[:, lanes[pair]]), grads[pair])) for pair in pairs
    ]
    if short:
        scores = [jnp.where(seen_mask(), score, -1e30) for score in scores]
    probs = [
        jnp.exp(
            by_head(scores[pair])
            - jnp.stack(
                [lse_ref[0, pl.ds((first + pair) * 2 + head, 1), :] for head in range(2)]
            )
        )
        for pair in pairs
    ]
    grad_v = [
        dot(prob.astype(BF).reshape(2 * LONG, LONG), grads[pair])
        for pair, prob in enumerate(probs)
    ]
    inners = [
        jnp.sum(prob * grad, axis=1, keepdims=True) for prob, grad in zip(probs, grad_probs)
    ]
    grad_scores = [
        (prob * (grad - inner)).astype(BF)
        for prob, grad, inner in zip(probs, grad_probs, inners)
    ]
    grad_k = [
        dot(grad.reshape(2 * LONG, LONG), queries[pair]) for pair, grad in enumerate(grad_scores)
    ]
    for pair in pairs:
        grad_q = [
            dot(keys_t[pair][head * HD : (head + 1) * HD], grad_scores[pair][head])
            for head in range(2)
        ]

        def store(part, values_in):
            at = first + pair
            half = at // 3
            start = half * (3 * width // 2) + part * (width // 2) + (at - 3 * half) * 2 * HD
            dqkv_ref[:, pl.ds(pl.multiple_of(start, 2 * HD), 2 * HD)] = values_in.astype(BF)

        store(0, jnp.concatenate(grad_q, axis=0).T * HD**-0.5)
        store(1, pair_columns(grad_k[pair]))
        store(2, pair_columns(grad_v[pair]))


def attend_back_kernel(
    info_ref, q_ref, k_ref, v_ref, dctx_ref, lse_ref, dz_ref, w0_ref, w1_ref, w2_ref, w3_ref,
    dqkv_ref, gx_ref, sum_ref, w_ref, sem_ref,
):
    width = q_ref.shape[1]
    parts = (w0_ref, w1_ref, w2_ref, w3_ref)
    copies = load_blocks(info_ref, parts, SHARES, w_ref, sem_ref)
    start_first(copies)

    def all_pairs(short):
        @pl.loop(0, width // (2 * HD), step=BACKWARD_PAIRS)
        def _(first):
            attend_pairs_back(first, short, q_ref, k_ref, v_ref, dctx_ref, lse_ref, dqkv_ref)

    @pl.when(info_ref[0] == 1)
    def _():
        all_pairs(False)

    @pl.when(info_ref[0] != 1)
    def _():
        all_pairs(True)

    sum_ref[...] = jnp.zeros_like(sum_ref)
    cols = width // 2
    for half in range(2):
        core = info_ref[1] if half == 0 else 1 - info_ref[1]
        spot = pl.ds(pl.multiple_of(core * cols, cols), cols)
        for row, part in enumerate((0, 2)):
            start = (3 * half + part) * cols
            sum_ref[row : row + 1, spot] = row_sum(dqkv_ref[:, start : start + cols].astype(F32))
    first_time(copies)
    gx_ref[...] = (dz_ref[...] + dot_nt(dqkv_ref[...], w_ref[...])).astype(BF)


def attend_back(group, info, q, k, v, dctx, lse, dz, weights, kept=None):
    tok, width = q.shape
    tile = pl.BlockSpec((LONG, width), lambda i, *_: (group, 0))
    *results, sums = call(
        attend_back_kernel,
        (1,),
        [
            tile, tile, tile, tile,
            pl.BlockSpec((1, 16, LONG), lambda i, *_: (group, 0, 0)),
            tile,
        ]
        + [ANY] * 4,
        [
            pl.BlockSpec((LONG, 3 * width), lambda i, *_: (group, 0)),
            tile,
            pl.BlockSpec((8, width), lambda i, *_: (0, 0)),
        ],
        [struct((tok, 3 * width), BF), struct((tok, width), BF), struct((8, width), F32)],
        [pltpu.VMEM((width, 3 * width), BF), pltpu.SemaphoreType.DMA((12,))],
        1,
        2 * LONG * width * (3 * width + 10 * LONG),
        15 * 2**20,
        LONG * LONG * 12,
        kept,
    )(info, q, k, v, dctx, lse, dz, *weights, *(kept or ()))
    return results, sums


def adamw_update(weights_in, moment, square, average_in, gradient, rate, scalars):
    beta_one, beta_two, ema_decay, scale_one, scale_two = scalars
    moment_new = beta_one * moment + (1.0 - beta_one) * gradient
    square_new = beta_two * square + (1.0 - beta_two) * gradient * gradient
    moment_hat = moment_new * scale_one
    square_hat = square_new * scale_two
    weights_new = weights_in - rate * (
        moment_hat / (jnp.sqrt(square_hat) + 1e-08) + 0.01 * weights_in
    )
    average_new = ema_decay * average_in + (1.0 - ema_decay) * weights_new
    return weights_new, moment_new, square_new, average_new


SLOT_STEPS = 3
LATE = 4


def fetch_gradient(ref, table_ref, slot, held_ref, sem_ref, rows):
    spot = pl.ds(pl.multiple_of(table_ref[2, slot] * rows, rows), rows)
    return pltpu.make_async_copy(
        ref.at[table_ref[1, slot], spot], held_ref.at[slot], sem_ref.at[slot]
    )


def adamw_kernel(table_ref, scale_ref, w_ref, m_ref, s_ref, a_ref, *refs):
    grads, outs, (held_ref, sem_ref) = refs[:4], refs[4:8], refs[8:]
    step = pl.program_id(0)
    count, rows, _ = w_ref.shape

    @pl.when(step == 0)
    def _():
        @pl.loop(0, held_ref.shape[0])
        def _(slot):
            for at, ref in enumerate(grads):
                chosen = table_ref[0, slot] == at + LATE
                if at == 0:
                    chosen = table_ref[0, slot] <= LATE

                @pl.when(chosen)
                def _():
                    fetch_gradient(ref, table_ref, slot, held_ref, sem_ref, rows).start()

    scalars = [scale_ref[at] for at in range(5)]

    @pl.loop(0, count)
    def _(at):
        slot = step * count + at
        fetch_gradient(grads[0], table_ref, slot, held_ref, sem_ref, rows).wait()
        gradient = held_ref[slot].astype(F32) * scale_ref[8 + 2 * slot]
        results = adamw_update(
            w_ref[at], m_ref[at], s_ref[at], a_ref[at], gradient,
            scale_ref[9 + 2 * slot], scalars,
        )
        for ref, value in zip(outs, results):
            ref[at] = value


def adamw_slots(table, scales, states, grads):
    cap, rows, cols = states[0].shape
    steps = SLOT_STEPS if cap % SLOT_STEPS == 0 else 1
    own = pl.BlockSpec((cap // steps, rows, cols), lambda i, *_: (i, 0, 0))
    return call(
        adamw_kernel,
        (steps,),
        [own] * 4 + [ANY] * 4,
        [own] * 4,
        [struct(states[0].shape, F32)] * 4,
        [pltpu.VMEM((cap, rows, cols), BF), pltpu.SemaphoreType.DMA((cap,))],
        2,
        20 * cap * rows * cols,
        40 * cap * rows * cols,
    )(table, scales, *states, *grads)


def late_kernel(table_ref, scale_ref, *refs):
    states, grads, outs, scratch = refs[:4], refs[4:8], refs[8:12], refs[12:]
    state_ref, result_ref, held_ref, sem_ref, state_sem_ref, out_sem_ref = scratch
    cap, rows, _ = held_ref.shape
    scalars = [scale_ref[at] for at in range(5)]

    def loads(slot):
        return [
            pltpu.make_async_copy(ref.at[slot], state_ref.at[slot, at], state_sem_ref.at[slot, at])
            for at, ref in enumerate(states)
        ]

    def stores(slot):
        return [
            pltpu.make_async_copy(result_ref.at[slot, at], ref.at[slot], out_sem_ref.at[slot, at])
            for at, ref in enumerate(outs)
        ]

    def each(work):
        @pl.loop(0, cap)
        def _(slot):
            @pl.when(table_ref[0, slot] < LATE)
            def _():
                work(slot)

    def begin(slot):
        for at, ref in enumerate(grads):
            @pl.when(table_ref[0, slot] == at)
            def _():
                fetch_gradient(ref, table_ref, slot, held_ref, sem_ref, rows).start()
        for copy in loads(slot):
            copy.start()

    def update(slot):
        fetch_gradient(grads[0], table_ref, slot, held_ref, sem_ref, rows).wait()
        for copy in loads(slot):
            copy.wait()
        gradient = held_ref[slot].astype(F32) * scale_ref[8 + 2 * slot]
        results = adamw_update(
            *[state_ref[slot, at] for at in range(4)], gradient, scale_ref[9 + 2 * slot], scalars
        )
        for at, value in enumerate(results):
            result_ref[slot, at] = value
        for copy in stores(slot):
            copy.start()

    def finish(slot):
        for copy in stores(slot):
            copy.wait()

    each(begin)
    each(update)
    each(finish)


def adamw_late(table, scales, states, grads, kept):
    cap, rows, cols = states[0].shape
    return call(
        late_kernel,
        (1,),
        [ANY] * 8,
        [ANY] * 4,
        [struct(states[0].shape, F32)] * 4,
        [
            pltpu.VMEM((cap, 4, rows, cols), F32),
            pltpu.VMEM((cap, 4, rows, cols), F32),
            pltpu.VMEM((cap, rows, cols), BF),
            pltpu.SemaphoreType.DMA((cap,)),
            pltpu.SemaphoreType.DMA((cap, 4)),
            pltpu.SemaphoreType.DMA((cap, 4)),
        ],
        2,
        20 * cap * rows * cols,
        40 * cap * rows * cols,
        0,
        kept,
    )(table, scales, *states, *grads, *kept)


def on_device(
    tokens,
    cotangent,
    phase_of,
    unit_slot,
    step_count,
    learn_rates,
    decay_rates,
    master,
    first_moment,
    second_moment,
    average,
    vector_state,
):
    cap, unit_rows, cols = master.shape
    tok_rows, width = tokens.shape
    batch_count = lax.axis_size("batch")
    row_blocks = width // unit_rows
    col_blocks = FF // width
    core = lax.axis_index("tensor")
    place = lax.axis_index("batch")
    fast = batch_count == FAST_BATCH
    plane, y_at, x_at = place // 4, (place // 2) % 2, place % 2
    up_base = 4 * row_blocks
    down_base = up_base + row_blocks * col_blocks
    chunks = [(0, 1, row_blocks), (up_base, col_blocks, 1), (down_base, col_blocks, 1)]
    corner = jnp.stack([place % 4, place % 4, plane]).astype(jnp.int32)

    def coords(orient):
        y_first = (core + orient) % 2 == 0
        first = jnp.where(y_first, y_at, x_at)
        second = jnp.where(y_first, x_at, y_at)
        return jnp.stack([first, second, plane]).astype(jnp.int32)

    places = [coords(orient) for orient in range(2)]

    def chunk_units(chunk):
        base, row_step, block_step = chunk
        return base + jnp.arange(4)[:, None] * block_step + jnp.arange(row_blocks)[None] * row_step

    def spreads(sources, which):
        first_bit = jnp.where(core == 0, 2, 1)
        inner = place % 4
        numbers = jnp.stack(
            [
                places[0][0] * 2 + places[0][1], plane, place,
                inner, inner ^ first_bit, inner ^ (3 - first_bit), inner ^ 3,
            ]
        ).astype(jnp.int32)
        return [spread(sources, unit_slot, numbers, chunks[at]) for at in which]

    def weights_chain(pieces):
        return Chain(spreading(pieces, 0, places[0]))

    def weights_plain(at):
        local = unit_slot[chunk_units(chunks[at])] - place * cap
        own = (local >= 0) & (local < cap)
        blocks = jnp.take(master, jnp.clip(local, 0, cap - 1), axis=0)
        blocks = jnp.where(own[..., None, None], blocks, 0.0).astype(BF)
        return lax.psum(blocks.reshape(4, width, cols), "batch")

    def grads_chain(terms, orient):
        return Chain(exchange(terms, orient, places[orient]))

    def shared(array_in):
        half = array_in.shape[1] // 2
        parts = [array_in[:, :half], array_in[:, half:]]
        return parts + [core_swap(part) for part in parts]

    def halves_of(array_in):
        other = lax.dynamic_slice_in_dim(array_in, (1 - core) * cols, cols, array_in.ndim - 1)
        return lax.dynamic_slice_in_dim(array_in, core * cols, cols, array_in.ndim - 1), other

    def swapped(array_in):
        return jnp.concatenate(halves_of(array_in), axis=-1)

    def both(here, there):
        low_first = core == 0
        return jnp.concatenate(
            [jnp.where(low_first, here, there), jnp.where(low_first, there, here)], axis=0
        )

    count_f = step_count[0].astype(F32)
    scalars = [
        decay_rates[0],
        decay_rates[1],
        decay_rates[2],
        1.0 / (1.0 - decay_rates[0] ** count_f),
        1.0 / (1.0 - decay_rates[1] ** count_f),
    ]

    def vec_update(sums):
        vector_grads = jnp.concatenate(
            [sums[0:2], sums[8:11], sums[12:16], sums[16:19]], axis=0
        )
        grads_scaled = vector_grads * float(tok_rows * batch_count) ** (-0.5)
        vec_weights, vec_first, vec_second, vec_average = adamw_update(
            vector_state[0], vector_state[1], vector_state[2], vector_state[3],
            grads_scaled, learn_rates[4], scalars,
        )
        return (
            jnp.stack([vec_weights, vec_average]),
            jnp.stack([grads_scaled, vec_first]),
            vec_second,
        )

    my_ids = place * cap + jnp.arange(cap, dtype=jnp.int32)
    matches = unit_slot[None, :] == my_ids[:, None]
    unit_ids = jnp.arange(unit_slot.shape[0], dtype=jnp.int32)
    unit = jnp.sum(jnp.where(matches, unit_ids[None, :], 0), axis=1)
    occupied = jnp.any(matches, axis=1)
    is_up = (unit >= up_base) & (unit < down_base)
    is_down = unit >= down_base
    is_other = (unit >= 3 * row_blocks) & (unit < up_base)
    is_wide = is_up | is_down
    chunk_at = jnp.where(is_down, 2, jnp.where(is_up | is_other, 1, 0))
    local = unit - jnp.where(is_down, down_base, up_base)
    block_at = jnp.where(
        is_wide, local % col_blocks, jnp.where(is_other, col_blocks, unit // row_blocks)
    )
    row_at = jnp.where(is_wide, local // col_blocks, unit % row_blocks)
    kind = jnp.where(
        occupied,
        (unit >= 3 * row_blocks).astype(jnp.int32) + is_up.astype(jnp.int32) + 2 * is_down,
        0,
    )
    rates = jnp.sum(
        jnp.where(kind[:, None] == jnp.arange(4)[None, :], learn_rates[None, :4], 0.0), axis=1
    )
    quarter_rows, half_rows = row_blocks // 4, row_blocks // 2
    first_quarter = corner[0] if fast else 0
    first_half = jnp.where(chunk_at == 1, places[1][0], places[0][0]) if fast else 0
    array_at = jnp.where(
        chunk_at == 0,
        (row_at // quarter_rows) ^ first_quarter,
        2 + 2 * chunk_at + ((row_at // half_rows) ^ first_half),
    )
    row_at = jnp.where(chunk_at == 0, row_at % quarter_rows, row_at % half_rows)
    table = jnp.stack([array_at, block_at, row_at]).astype(jnp.int32)
    states = (master, first_moment, second_moment, average)
    scales = jnp.concatenate(
        [
            jnp.stack(scalars),
            jnp.zeros((3,), F32),
            jnp.stack([occupied.astype(F32), rates], axis=1).reshape(-1),
        ]
    )
    firsts = [places[0][0], places[1][0]] if fast else [0, 0]
    info = jnp.stack([phase_of[0], core, *firsts]).astype(jnp.int32)
    vectors = vector_state[0]
    rows = jnp.concatenate([swapped(vectors[0:2]), vectors[2:5], vectors[9:12]], axis=0)
    upper = vectors[5:9].reshape(2, FF // 2)
    turned = jnp.concatenate([upper[1:], upper[:1]], axis=0)
    bias_up = jnp.where(core == 0, upper, turned).reshape(4, width)

    if fast:
        low_master = master.astype(BF)
        beside = lax.ppermute(low_master, BOTH, swap_pairs(0, 1))
        across = lax.ppermute(low_master, BOTH, swap_pairs(0, 2))
        diagonal = lax.ppermute(beside, BOTH, swap_pairs(0, 2))
        sources = (low_master, beside, across, diagonal)
        io = weights_chain(spreads(sources, (0,))[0])
        _, (up, down) = phase([io], work=lambda _: spreads(sources, (1, 2)))
        up, down = weights_chain(up), weights_chain(down)
        _, (info, rows, bias_up, table, scales) = phase(
            [io], work=lambda _: (info, rows, bias_up, table, scales)
        )
        phase([io, up])
        theirs_first, _ = phase([io, up], io.ready)
        theirs_last, _ = phase([up, down], io.result[1:])
        weights_io = [*io.result, *theirs_first, *theirs_last]
        theirs_first, stage = phase(
            [up, down],
            up.ready,
            lambda late: forward(0, after(info, late), tokens, rows, weights_io),
        )
        theirs_last, stage = phase(
            [down],
            up.result[1:],
            lambda late: forward(1, after(info, late), tokens, rows, weights_io, kept=stage),
        )
        weights_up = [*up.result, *theirs_first, *theirs_last]
        q, k, v, ctx, lse, first, x_t = stage
        theirs_first, (act, slope, hidden_t, hidden) = phase(
            [down],
            down.ready,
            lambda late: feed_up(after(info, late), first, rows, bias_up, weights_up),
        )
        theirs_last, _ = phase(swaps=down.result[1:])
        weights_down = [*down.result, *theirs_first, *theirs_last]
    else:
        weights_io, weights_up, weights_down = [shared(weights_plain(at)) for at in range(3)]
        stage = None
        for group in range(tok_rows // 2 // LONG):
            stage = forward(group, info, tokens, rows, weights_io, kept=stage)
        q, k, v, ctx, lse, first, x_t = stage
        act, slope, hidden_t, hidden = feed_up(info, first, rows, bias_up, weights_up)

    out_half, dz2, grad_two_t, down_theirs, sums_two = feed_down(
        info, hidden, act, cotangent, rows, weights_down
    )
    heads = (q, k, v)

    def back(info):
        return feed_back(
            info, first, dz2, slope, rows, weights_down, weights_up, weights_io
        )

    def heads_back(group, info, dctx, dz1, kept=None):
        return attend_back(group, info, *heads, dctx, lse, dz1, weights_io, kept=kept)

    if fast:
        (other,), (down_mine,) = phase(
            swaps=[down_theirs], work=lambda late: wide_grad(after(grad_two_t, late), act, (0,))
        )
        down = grads_chain([down_mine, other], 0)
        (out_other,), (dz1, dctx, dt_t, grad_up, sums_one) = phase(
            [down], [out_half], lambda late: back(after(info, late))
        )
        _, (up_mine, up_theirs) = phase(
            [down],
            work=lambda late: up_grad(after(hidden_t, late), dt_t, grad_up, ctx),
        )
        (other,), (kept, sums_zero) = phase(
            [down], [up_theirs], lambda late: heads_back(0, after(info, late), dctx, dz1)
        )
        up = grads_chain([up_mine, other], 1)
        _, (kept, sums_extra) = phase(
            [down, up],
            work=lambda late: heads_back(1, after(info, late), dctx, dz1, kept),
        )
        dqkv, grad_x = kept
        vec = Chain(doubling(jnp.concatenate([sums_zero + sums_extra, sums_one, sums_two])))
        _, io_theirs = phase(
            [down, up, vec], work=lambda late: share_grad(after(x_t, late), dqkv, 1)
        )
        (other,), io_mine = phase(
            [down, up, vec], [io_theirs], lambda late: share_grad(after(x_t, late), dqkv, 0)
        )
        io = Chain(plane_exchange([io_mine, other], corner))
        (grad_x_other,), out = phase(
            [io, up, vec], [grad_x], lambda late: both(after(out_half, late), out_other)
        )
        _, input_grad = phase(
            [io, up, vec],
            work=lambda late: both(after(grad_x, late), grad_x_other).astype(F32),
        )
        phase([io, up, vec])
        _, (new_states, vec_outs) = phase(
            [io],
            work=lambda late: (
                adamw_slots(after(table, late), scales, states, [*up.result, *down.result]),
                vec_update(after(vec.result, late)),
            ),
        )
        grads = io.result
    else:
        dz1, dctx, dt_t, grad_up, sums_one = back(info)
        kept, sums_zero = None, 0.0
        for group in range(tok_rows // 2 // LONG):
            kept, sums_extra = heads_back(group, info, dctx, dz1, kept)
            sums_zero = sums_zero + sums_extra
        dqkv, grad_x = kept
        up_mine, up_theirs = up_grad(hidden_t, dt_t, grad_up, ctx)
        (down_mine,) = wide_grad(grad_two_t, act, (0,))
        grads = []
        for mine, theirs, parts in (
            (share_grad(x_t, dqkv, 0), share_grad(x_t, dqkv, 1), 4),
            (up_mine, up_theirs, 2),
            (down_mine, down_theirs, 2),
        ):
            grad = lax.psum(total(mine, core_swap(theirs)), "batch")
            grads += jnp.split(grad, parts, axis=1)
        new_states = adamw_slots(table, scales, states, grads[4:])
        grads = grads[:4]
        vec_outs = vec_update(
            lax.psum(jnp.concatenate([sums_zero, sums_one, sums_two]), BOTH)
        )
        out = both(out_half, core_swap(out_half))
        input_grad = both(grad_x, core_swap(grad_x)).astype(F32)

    new_states = adamw_late(table, scales, states, grads, new_states)
    return (out, input_grad, *new_states, *vec_outs)


def solution(mesh):
    return jax.shard_map(
        on_device,
        mesh=mesh,
        in_specs=(
            P("batch", None),
            P("batch", None),
            P("batch"),
            P(),
            P(),
            P(),
            P(),
            P("batch", None, "tensor"),
            P("batch", None, "tensor"),
            P("batch", None, "tensor"),
            P("batch", None, "tensor"),
            P(),
        ),
        out_specs=(
            P("batch", None),
            P("batch", None),
            P("batch", None, "tensor"),
            P("batch", None, "tensor"),
            P("batch", None, "tensor"),
            P("batch", None, "tensor"),
            P(),
            P(),
            P(),
        ),
        check_vma=False,
    )
```

```python
import functools

import jax
import jax.numpy as jnp
from jax import lax
from jax.experimental import pallas as pl
from jax.experimental.pallas import tpu as pltpu
from jax.sharding import PartitionSpec as P

HD = 64
FF = 3072
SHORT = 128
LONG = 512
EPS = 1e-12
BF = jnp.bfloat16
F32 = jnp.float32
VMEM_BYTES = 60 * 2**20
BOTH = ("batch", "tensor")
ANY = pl.BlockSpec(memory_space=pl.ANY)
PLANES = 4
FAST_BATCH = 16


def dot(first_mat, second_mat):
    return lax.dot_general(
        first_mat, second_mat, (((1,), (0,)), ((), ())), preferred_element_type=F32
    )


def dot_nt(first_mat, second_mat):
    return lax.dot_general(
        first_mat, second_mat, (((1,), (1,)), ((), ())), preferred_element_type=F32
    )


def normalized(rows):
    centred = rows - jnp.mean(rows, axis=-1, keepdims=True)
    inverse = lax.rsqrt(jnp.mean(centred * centred, axis=-1, keepdims=True) + EPS)
    return centred * inverse, inverse


def norm_back(grad_scaled, normal, inverse):
    mean_grad = jnp.mean(grad_scaled, axis=-1, keepdims=True)
    mean_both = jnp.mean(grad_scaled * normal, axis=-1, keepdims=True)
    return inverse * (grad_scaled - mean_grad - normal * mean_both)


def fold_rows(array_in):
    rows, cols = array_in.shape
    return jnp.sum(array_in.reshape(rows // 8, 8, cols), axis=0)


def row_sum(array_in):
    return jnp.sum(array_in, axis=0, keepdims=True)


def load_blocks(info_ref, parts, blocks, weight_ref, sem_ref):
    _, half_rows, cols = parts[0].shape
    copies = []
    for spot, (half, block) in enumerate(blocks):
        first = info_ref[2 + half]
        pair = []
        for at in range(2):
            start = pl.multiple_of((first if at == 0 else 1 - first) * half_rows, half_rows)
            pair.append(
                pltpu.make_async_copy(
                    parts[2 * half + at].at[block],
                    weight_ref.at[pl.ds(start, half_rows), pl.ds(spot * cols, cols)],
                    sem_ref.at[2 * spot + at],
                )
            )
        copies.append(pair)
    return copies


def after(array_in, *others):
    return lax.optimization_barrier((array_in, others))[0]


def first_time(copies):
    @pl.when(pl.program_id(0) == 0)
    def _():
        for pair in copies:
            for copy in pair:
                copy.wait()


def start_first(copies):
    @pl.when(pl.program_id(0) == 0)
    def _():
        for pair in copies:
            for copy in pair:
                copy.start()


PAIRED = [(half, block) for block in range(4) for half in range(2)]
SHARES = [(half, block) for half in range(2) for block in range(3)]
HALVED = [(half, block) for half in range(2) for block in range(4)]


def call(
    kernel, grid, in_specs, out_specs, out_shape, scratch, prefetch, flops, moved, exps=0, kept=None
):
    aliases = {}
    if kept is not None:
        given = prefetch + len(in_specs)
        count = len(kept)
        in_specs = in_specs + [ANY] * count
        aliases = {given + at: at for at in range(count)}
        inner = kernel

        def kernel(*refs):
            inner(*refs[:given], *refs[given + count :])

    return pl.pallas_call(
        kernel,
        input_output_aliases=aliases,
        out_shape=out_shape,
        grid_spec=pltpu.PrefetchScalarGridSpec(
            num_scalar_prefetch=prefetch,
            grid=grid,
            in_specs=in_specs,
            out_specs=out_specs,
            scratch_shapes=scratch,
        ),
        compiler_params=pltpu.CompilerParams(vmem_limit_bytes=VMEM_BYTES),
        cost_estimate=pl.CostEstimate(
            flops=30 * flops, bytes_accessed=moved, transcendentals=exps
        ),
    )


def struct(shape, kind):
    return jax.ShapeDtypeStruct(shape, kind)


def spread_kernel(
    base, row_step, block_step, cap, rows, info_ref, slot_ref, *refs
):
    sources, outs, (held_ref, quarter_ref, sem_ref) = refs[:4], refs[4:8], refs[8:]
    block = pl.program_id(0)
    quarter, plane, place = info_ref[0], info_ref[1], info_ref[2]
    copies = [
        [
            pltpu.make_async_copy(
                ref, held_ref.at[pl.ds(info_ref[3 + at] * cap, cap)], sem_ref.at[at]
            )
        ]
        for at, ref in enumerate(sources)
    ]
    start_first(copies)
    first_time(copies)
    total_slots = PLANES * cap
    for step in range(3):
        unit = base + (quarter * 3 + step) * row_step + block * block_step
        local = slot_ref[unit] - plane * total_slots
        here = (local >= 0) & (local < total_slots)
        spot = slice(step * rows, (step + 1) * rows)

        @pl.when(here)
        def _():
            quarter_ref[spot, :] = held_ref[local]

        @pl.when(jnp.logical_not(here))
        def _():
            quarter_ref[spot, :] = jnp.zeros((rows, quarter_ref.shape[1]), BF)

    for ahead, out_ref in enumerate(outs):
        size = out_ref.shape[1]
        start = pl.multiple_of(lax.rem(plane + ahead, PLANES) * size, size)
        out_ref[0] = quarter_ref[pl.ds(start, size), :]


def spread(sources, unit_slot, info, chunk):
    cap, rows, cols = sources[0].shape
    base, row_step, block_step = chunk
    size = 3 * rows // PLANES
    block = pl.BlockSpec((1, size, cols), lambda i, *_: (i, 0, 0))
    return call(
        functools.partial(spread_kernel, base, row_step, block_step, cap, rows),
        (4,),
        [ANY] * 4,
        [block] * 4,
        [struct((4, size, cols), BF)] * 4,
        [
            pltpu.VMEM((PLANES * cap, rows, cols), BF),
            pltpu.VMEM((3 * rows, cols), BF),
            pltpu.SemaphoreType.DMA((4,)),
        ],
        2,
        0,
        5 * 2**20,
    )(info, unit_slot, *sources)


def swap_pairs(orient, stage):
    pairs = []
    for place in range(FAST_BATCH):
        for core in range(2):
            first_bit = 2 if (core + orient) % 2 == 0 else 1
            bit = first_bit if stage == 1 else 3 - first_bit
            pairs.append((place * 2 + core, (place ^ bit) * 2 + core))
    return pairs


def flip_pairs(bit):
    return [
        (place * 2 + core, (place ^ bit) * 2 + core)
        for place in range(FAST_BATCH)
        for core in range(2)
    ]


def plane_pairs(step):
    return [
        (place * 2 + core, (place + 4 * step) % FAST_BATCH * 2 + core)
        for place in range(FAST_BATCH)
        for core in range(2)
    ]


def total(*terms):
    result = terms[0].astype(F32)
    for term in terms[1:]:
        result = result + term.astype(F32)
    return result.astype(BF)


def send(array_in, pairs):
    return lax.ppermute(array_in, BOTH, pairs)


def cut(array_in, start, size):
    return lax.dynamic_slice_in_dim(array_in, start, size, 1)


def first_split(info, terms):
    half = terms[0].shape[1] // 2
    return total(*[cut(term, (1 - info[0]) * half, half) for term in terms])


def second_split(info, terms, got):
    half = got.shape[1] // 2
    start = (1 - info[1]) * half
    kept = [cut(term, info[0] * got.shape[1] + start, half) for term in terms]
    return total(*kept, cut(got, start, half))


def third_split(info, terms, one, two):
    half = two.shape[1]
    size = half // PLANES
    pieces = []
    for ahead in range(PLANES):
        start = (info[2] + ahead) % PLANES * size
        first = info[1] * half + start
        kept = [cut(term, info[0] * one.shape[1] + first, size) for term in terms]
        pieces.append(total(*kept, cut(one, first, size), cut(two, start, size)))
    return pieces


def plane_join(info, pieces):
    return jnp.concatenate(
        [lax.select_n((info[2] - row) % PLANES, *pieces) for row in range(PLANES)], axis=1
    )


def half_join(info, here, there):
    low_first = info[1] == 0
    return jnp.concatenate(
        [jnp.where(low_first, here, there), jnp.where(low_first, there, here)], axis=1
    )


def exchange(terms, orient, info):
    (one,) = yield [(first_split(info, terms), swap_pairs(orient, 1))]
    (two,) = yield [(second_split(info, terms, one), swap_pairs(orient, 2))]
    own, *pieces = third_split(info, terms, one, two)
    return (yield from spreading([own] + pieces, orient, info))


def spreading(pieces, orient, info):
    arrived = yield [(pieces[step], plane_pairs(step)) for step in range(1, PLANES)]
    owned = total(pieces[0], *arrived)
    others = yield [(owned, plane_pairs(step)) for step in range(1, PLANES)]
    level = plane_join(info, [owned] + others)
    (there,) = yield [(level, swap_pairs(orient, 2))]
    level = half_join(info, level, there)
    (there,) = yield [(level, swap_pairs(orient, 1))]
    return level, there


def plane_exchange(terms, info):
    quarter = terms[0].shape[1] // 4
    size = quarter // PLANES
    going = [
        total(*[cut(term, (info[0] ^ away) * quarter, quarter) for term in terms])
        for away in (1, 2, 3)
    ]
    got = yield [(piece, flip_pairs(away)) for away, piece in zip((1, 2, 3), going)]
    parts = []
    for ahead in range(PLANES):
        start = (info[2] + ahead) % PLANES * size
        kept = [cut(term, info[0] * quarter + start, size) for term in terms]
        parts.append(total(*kept, *[cut(piece, start, size) for piece in got]))
    arrived = yield [(parts[step], plane_pairs(step)) for step in range(1, PLANES)]
    owned = total(parts[0], *arrived)
    others = yield [(owned, plane_pairs(step)) for step in range(1, PLANES)]
    level = plane_join(info, [owned] + others)
    there = yield [(level, flip_pairs(away)) for away in (1, 2, 3)]
    return [level] + there


def doubling(array_in):
    cores = [(at, at ^ 1) for at in range(2 * FAST_BATCH)]
    for pairs in [cores] + [flip_pairs(bit) for bit in (1, 2, 4, 8)]:
        (other,) = yield [(array_in, pairs)]
        array_in = array_in + other
    return array_in


class Chain:
    def __init__(self, steps):
        self.steps = steps
        self.result = None
        self.pending = next(steps)

    @property
    def ready(self):
        return [parts for parts, _ in self.pending]

    def take(self, arrived):
        try:
            self.pending = self.steps.send(arrived)
        except StopIteration as stop:
            self.pending, self.result = [], stop.value


def phase(chains=(), swaps=(), work=None):
    ready, swaps = lax.optimization_barrier(([chain.ready for chain in chains], list(swaps)))
    arrived = [
        [send(parts, pairs) for parts, (_, pairs) in zip(given, chain.pending)]
        for given, chain in zip(ready, chains)
    ]
    swapped = [core_swap(array) for array in swaps]
    done = None if work is None else work((ready, swaps))
    arrived, swapped, done = lax.optimization_barrier((arrived, swapped, done))
    for chain, parts in zip(chains, arrived):
        chain.take(parts)
    return swapped, done


def core_swap(array_in):
    return lax.ppermute(array_in, "tensor", [(0, 1), (1, 0)])


def seen_mask():
    key_at = lax.broadcasted_iota(jnp.int32, (2 * LONG, LONG), 0) % LONG // SHORT
    query_at = lax.broadcasted_iota(jnp.int32, (2 * LONG, LONG), 1) // SHORT
    return key_at == query_at


def low_lanes(rows):
    return lax.broadcasted_iota(jnp.int32, (rows, 2 * HD), 1) < HD


def pair_lanes(pair):
    return pl.ds(pl.multiple_of(pair * 2 * HD, 2 * HD), 2 * HD)


def both_heads(array_in):
    low = low_lanes(array_in.shape[0])
    none = jnp.zeros_like(array_in)
    return jnp.concatenate(
        [jnp.where(low, array_in, none), jnp.where(low, none, array_in)], axis=0
    )


def by_head(array_in):
    return array_in.reshape(2, LONG, array_in.shape[1])


def pair_columns(array_in):
    return jnp.where(low_lanes(LONG), array_in[:LONG], array_in[LONG:])


BACKWARD_PAIRS = 1


def attend_pairs(short, q_ref, k_ref, v_ref, ctx_ref, lse_ref):
    pairs = range(q_ref.shape[1] // (2 * HD))
    lanes = [slice(pair * 2 * HD, (pair + 1) * 2 * HD) for pair in pairs]
    queries = [q_ref[:, at] * BF(HD**-0.5) for at in lanes]
    keys_here = [both_heads(k_ref[:, at]) for at in lanes]
    values_t = [v_ref[:, at].T for at in lanes]
    scores = [dot_nt(keys_here[pair], queries[pair]) for pair in pairs]
    if short:
        scores = [jnp.where(seen_mask(), score, -1e30) for score in scores]
    scores = [by_head(score) for score in scores]
    tops = [jnp.max(score, axis=1, keepdims=True) for score in scores]
    weights = [jnp.exp(score - top) for score, top in zip(scores, tops)]
    norms = [jnp.sum(weight, axis=1, keepdims=True) for weight in weights]
    probs = [(weight * (1.0 / norm)).astype(BF) for weight, norm in zip(weights, norms)]
    for pair in pairs:
        outs = [
            dot(values_t[pair][head * HD : (head + 1) * HD], probs[pair][head])
            for head in range(2)
        ]
        ctx_ref[:, lanes[pair]] = jnp.concatenate(outs, axis=0).T.astype(BF)
        for head in range(2):
            spot = slice(pair * 2 + head, pair * 2 + head + 1)
            lse_ref[0, 0, spot, :] = tops[pair][head] + jnp.log(norms[pair][head])


def forward_kernel(half, info_ref, x_ref, rows_ref, first_ref, last_ref, *refs):
    if half == 0:
        before_ref, refs = None, refs
        q_ref, k_ref, v_ref, ctx_ref, lse_ref, z_ref, xt_ref, w_ref, sem_ref = refs
    else:
        before_ref, q_ref, k_ref, v_ref, ctx_ref, lse_ref, z_ref, w_ref, sem_ref = refs
    cols = q_ref.shape[1]
    parts = (first_ref, last_ref) * 2
    copies = load_blocks(info_ref, parts, [(half, block) for block in range(4)], w_ref, sem_ref)
    start_first(copies)
    tokens = x_ref[...]
    if half == 0:
        xt_ref[...] = tokens.T
    first_time(copies[:3])
    projected = dot(tokens, w_ref[:, : 3 * cols])
    spot = slice(half * cols, (half + 1) * cols)
    q_ref[...] = (projected[:, :cols] + rows_ref[0:1, spot]).astype(BF)
    k_ref[...] = projected[:, cols : 2 * cols].astype(BF)
    v_ref[...] = (projected[:, 2 * cols :] + rows_ref[1:2, spot]).astype(BF)

    @pl.when(info_ref[0] == 1)
    def _():
        attend_pairs(False, q_ref, k_ref, v_ref, ctx_ref, lse_ref)

    @pl.when(info_ref[0] != 1)
    def _():
        attend_pairs(True, q_ref, k_ref, v_ref, ctx_ref, lse_ref)

    first_time(copies[3:])
    attended = dot_nt(ctx_ref[...], w_ref[:, 3 * cols :])
    if half == 0:
        z_ref[...] = tokens.astype(F32) + attended + rows_ref[2:3]
    else:
        z_ref[...] = before_ref[...] + attended


def forward(half, info, tokens, rows, weights, before=None):
    tok = tokens.shape[0] // 2
    width = tokens.shape[1]
    cols = width // 2
    groups = tok // LONG
    tile = pl.BlockSpec((LONG, width), lambda i, *_: (i, 0))
    part = pl.BlockSpec((LONG, cols), lambda i, *_: (i, half))
    low = struct((tok, width), BF)
    in_specs = [
        pl.BlockSpec((LONG, width), lambda i, info: (info[1] * groups + i, 0)),
        pl.BlockSpec((8, width), lambda i, *_: (0, 0)),
        ANY,
        ANY,
    ]
    out_specs = [
        part, part, part, part,
        pl.BlockSpec((1, 1, 8, LONG), lambda i, *_: (i, half, 0, 0)),
        tile,
    ]
    outs = [low, low, low, low, struct((groups, 2, 8, LONG), F32), struct((tok, width), F32)]
    inputs, kept = [], None
    if half == 0:
        out_specs.append(pl.BlockSpec((width, LONG), lambda i, *_: (0, i)))
        outs.append(struct((width, tok), BF))
    else:
        *kept, partial_sum = before[:6]
        inputs = [partial_sum]
        in_specs.append(tile)
    return call(
        functools.partial(forward_kernel, half),
        (groups,),
        in_specs,
        out_specs,
        outs,
        [pltpu.VMEM((width, 4 * cols), BF), pltpu.SemaphoreType.DMA((8,))],
        1,
        2 * tok * width * (4 * cols + LONG),
        12 * 2**20,
        tok * LONG * 6,
        kept,
    )(info, tokens, rows, *weights[2 * half : 2 * half + 2], *inputs, *(kept or ()))


def up_kernel(
    info_ref, z_ref, rows_ref, bias_ref, w0_ref, w1_ref, w2_ref, w3_ref,
    act_ref, slope_ref, ht_ref, hidden_ref, w_ref, sem_ref,
):
    width = z_ref.shape[1]
    parts = (w0_ref, w1_ref, w2_ref, w3_ref)
    copies = load_blocks(info_ref, parts, HALVED, w_ref, sem_ref)
    start_first(copies)
    normal, _ = normalized(z_ref[...])
    hidden = normal * rows_ref[3:4] + rows_ref[4:5]
    hidden_ref[...] = hidden
    low = hidden.astype(BF)
    ht_ref[...] = low.T
    for part in range(FF // width):
        spot = slice(part * width, (part + 1) * width)
        first_time(copies[2 * part : 2 * part + 2])
        upper = dot(low, w_ref[:, spot]) + bias_ref[part : part + 1]
        phi_sum = 0.5 + 0.5 * lax.erf(upper * (0.5**0.5))
        density = jnp.exp(-0.5 * upper * upper) * 0.3989422804014327
        act_ref[:, spot] = (upper * phi_sum).astype(BF)
        slope_ref[:, spot] = (phi_sum + upper * density).astype(BF)


ROWS, COLUMNS, NORM_ROWS = 256, 256, 128
UP_TILE = 256


def feed_up(info, first, rows, bias, weights):
    tok, width = first.shape
    wide = struct((tok, FF), BF)
    return call(
        up_kernel,
        (tok // UP_TILE,),
        [
            pl.BlockSpec((UP_TILE, width), lambda i, *_: (i, 0)),
            pl.BlockSpec((8, width), lambda i, *_: (0, 0)),
            pl.BlockSpec((4, width), lambda i, *_: (0, 0)),
        ]
        + [ANY] * 4,
        [
            pl.BlockSpec((UP_TILE, FF), lambda i, *_: (i, 0)),
            pl.BlockSpec((UP_TILE, FF), lambda i, *_: (i, 0)),
            pl.BlockSpec((width, UP_TILE), lambda i, *_: (0, i)),
            pl.BlockSpec((UP_TILE, width), lambda i, *_: (i, 0)),
        ],
        [wide, wide, struct((width, tok), BF), struct((tok, width), F32)],
        [pltpu.VMEM((width, FF), BF), pltpu.SemaphoreType.DMA((16,))],
        1,
        2 * tok * width * FF,
        20 * 2**20,
        tok * FF * 2,
    )(info, first, rows, bias, *weights)


PARTS = 4


def wait_pairs(copies):
    for pair in copies:
        for copy in pair:
            copy.wait()


def down_kernel(info_ref, h_in_ref, act_ref, cot_in_ref, rows_ref, *refs):
    parts, outs, gt_ref, sum_ref = refs[:4], refs[4:7], refs[7], refs[8]
    w_ref, h_ref, cot_ref, branch_ref = refs[9:13]
    out_ref, dz_ref, dyt_ref, low_ref, sem_ref, own_sem_ref = refs[13:]
    step = pl.program_id(0)
    tok, width = h_ref.shape
    copies = load_blocks(info_ref, parts, HALVED, w_ref, sem_ref)
    start = pl.multiple_of(info_ref[1] * tok, tok)
    h_copy = pltpu.make_async_copy(h_in_ref, h_ref, own_sem_ref.at[0])
    cot_copy = pltpu.make_async_copy(
        cot_in_ref.at[pl.ds(start, tok)], cot_ref, own_sem_ref.at[1]
    )
    out_copies = [
        pltpu.make_async_copy(source, target, own_sem_ref.at[2 + at])
        for at, (source, target) in enumerate(zip((out_ref, dz_ref, dyt_ref), outs))
    ]
    start_first(copies)

    @pl.when(step == 0)
    def _():
        h_copy.start()
        cot_copy.start()
        sum_ref[...] = jnp.zeros_like(sum_ref)

    for part in range(PARTS):
        @pl.when(step == part)
        def _():
            wait_pairs(copies[2 * part : 2 * part + 2])
            lanes = slice(part * width, (part + 1) * width)
            branch = dot_nt(act_ref[...], w_ref[:, lanes])
            branch_ref[...] = branch if part == 0 else branch_ref[...] + branch

    @pl.when(step == PARTS - 1)
    def _():
        h_copy.wait()
        cot_copy.wait()
        gains = rows_ref[6:7]
        sums = [0.0, 0.0, 0.0]
        for row in range(0, tok, NORM_ROWS):
            spot = slice(row, row + NORM_ROWS)
            normal, inverse = normalized(h_ref[spot, :] + branch_ref[spot, :] + rows_ref[5:6])
            out_ref[spot, :] = (normal * gains + rows_ref[7:8]).astype(BF)
            cot = cot_ref[spot, :].astype(F32)
            grad = norm_back(cot * gains, normal, inverse)
            dz_ref[spot, :] = grad
            low_ref[spot, :] = grad.astype(BF)
            for at, value in enumerate((grad, cot * normal, cot)):
                sums[at] = sums[at] + fold_rows(value)
        dyt_ref[...] = low_ref[...].T
        for at in range(3):
            sum_ref[at : at + 1] += row_sum(sums[at])
        for copy in out_copies:
            copy.start()

    @pl.when(step >= PARTS)
    def _():
        put_blocks(gt_ref, dot(dyt_ref[...], act_ref[...]))

    @pl.when(step == PARTS + 1)
    def _():
        for copy in out_copies:
            copy.wait()


def put_blocks(ref, grad):
    cols = ref.shape[2]
    for block in range(ref.shape[0]):
        ref[block] = grad[:, block * cols : (block + 1) * cols].astype(BF)


def feed_down(info, hidden, act, cot, rows, weights):
    tok, width = hidden.shape
    wide = (tok, width)
    return call(
        down_kernel,
        (PARTS + 2,),
        [
            ANY,
            pl.BlockSpec(wide, lambda i, *_: (0, jnp.where(i < PARTS, i, i - 2))),
            ANY,
            pl.BlockSpec((8, width), lambda i, *_: (0, 0)),
        ]
        + [ANY] * 4,
        [
            ANY,
            ANY,
            ANY,
            pl.BlockSpec((2, width, width // 2), lambda i, *_: (jnp.clip(i - PARTS, 0, 1), 0, 0)),
            pl.BlockSpec((8, width), lambda i, *_: (0, 0)),
        ],
        [
            struct(wide, BF),
            struct(wide, F32),
            struct((width, tok), BF),
            struct((4, width, width // 2), BF),
            struct((8, width), F32),
        ],
        [
            pltpu.VMEM((width, FF), BF),
            pltpu.VMEM(wide, F32),
            pltpu.VMEM(wide, BF),
            pltpu.VMEM(wide, F32),
            pltpu.VMEM(wide, BF),
            pltpu.VMEM(wide, F32),
            pltpu.VMEM((width, tok), BF),
            pltpu.VMEM(wide, BF),
            pltpu.SemaphoreType.DMA((16,)),
            pltpu.SemaphoreType.DMA((5,)),
        ],
        1,
        3 * tok * width * FF,
        30 * 2**20,
    )(info, hidden, act, cot, rows, *weights)


def back_kernel(info_ref, z_in_ref, dz2_ref, slope_ref, rows_ref, *refs):
    down, upper, other = refs[:4], refs[4:8], refs[8:12]
    outs, da_ref, sum_ref = refs[12:15], refs[15], refs[16]
    wd_ref, wu_ref, wo_ref, z_ref, hidden_ref, low_ref, held_ref = refs[17:24]
    dctx_ref, dtt_ref, dsem_ref, usem_ref, osem_ref, own_sem_ref = refs[24:]
    step = pl.program_id(0)
    tok, width = z_ref.shape
    downs = load_blocks(info_ref, down, HALVED, wd_ref, dsem_ref)
    ups = load_blocks(info_ref, upper, HALVED, wu_ref, usem_ref)
    others = load_blocks(info_ref, other, [(0, 3), (1, 3)], wo_ref, osem_ref)
    z_copy = pltpu.make_async_copy(z_in_ref, z_ref, own_sem_ref.at[0])
    for at in range(0, 8, 2):
        start_first(downs[at : at + 2] + ups[at : at + 2])
    start_first(others + [[z_copy]])

    @pl.when(step == 0)
    def _():
        sum_ref[...] = jnp.zeros_like(sum_ref)
        hidden_ref[...] = dz2_ref[...]
        low_ref[...] = dz2_ref[...].astype(BF)

    for part in range(PARTS + 1):
        @pl.when(step == part)
        def _():
            if part < PARTS:
                wait_pairs(downs[2 * part : 2 * part + 2])
            if part > 0:
                wait_pairs(ups[2 * part - 2 : 2 * part])
            place = 4 + (part ^ (2 * info_ref[1]))
            for column in range(0, width, COLUMNS):
                spot = slice(column, column + COLUMNS)
                lanes = slice(part * width + column, part * width + column + COLUMNS)
                if part < PARTS:
                    grad_act = dot(low_ref[...], wd_ref[:, lanes])
                if part > 0:
                    before = slice((part - 1) * width, part * width)
                    hidden_ref[:, spot] += dot_nt(held_ref[(part - 1) % 2], wu_ref[spot, before])
                if part < PARTS:
                    grad_up = (grad_act * slope_ref[:, spot].astype(F32)).astype(BF)
                    da_ref[:, spot] = grad_up
                    held_ref[part % 2, :, spot] = grad_up
                    sum_ref[pl.ds(place, 1), spot] = row_sum(fold_rows(grad_up.astype(F32)))

    @pl.when(step == PARTS)
    def _():
        z_copy.wait()
        gains = rows_ref[3:4]
        sums = [0.0, 0.0, 0.0]
        out_copies = []
        for half in range(2):
            rows = slice(half * (tok // 2), (half + 1) * (tok // 2))
            for row in range(rows.start, rows.stop, NORM_ROWS):
                spot = slice(row, row + NORM_ROWS)
                grad_hidden = hidden_ref[spot, :]
                normal, inverse = normalized(z_ref[spot, :])
                grad_one = norm_back(grad_hidden * gains, normal, inverse)
                low_ref[spot, :] = grad_one.astype(BF)
                for at, value in enumerate((grad_one, grad_hidden * normal, grad_hidden)):
                    sums[at] = sums[at] + fold_rows(value)
            if half == 0:
                wait_pairs(others)
            dctx_ref[rows, :] = dot(low_ref[rows, :], wo_ref[...]).astype(BF)
            dtt_ref[:, rows] = low_ref[rows, :].T
            spot = pl.ds(rows.start, tok // 2)
            for at, (source, target) in enumerate(zip((low_ref, dctx_ref, dtt_ref), outs)):
                source, target = (
                    (source.at[:, spot], target.at[:, spot])
                    if at == 2
                    else (source.at[spot], target.at[spot])
                )
                out_copies.append(
                    pltpu.make_async_copy(source, target, own_sem_ref.at[1 + 3 * half + at])
                )
                out_copies[-1].start()
        for at in range(3):
            sum_ref[at : at + 1] = row_sum(sums[at])
        for copy in out_copies:
            copy.wait()


def feed_back(info, first, dz2, slope, rows, down, upper, other):
    tok, width = first.shape
    wide = (tok, width)
    fixed = pl.BlockSpec((8, width), lambda i, *_: (0, 0))
    part = pl.BlockSpec(wide, lambda i, *_: (0, jnp.minimum(i, PARTS - 1)))
    return call(
        back_kernel,
        (PARTS + 1,),
        [ANY, pl.BlockSpec(wide, lambda i, *_: (0, 0)), part, fixed] + [ANY] * 12,
        [ANY, ANY, ANY, part, fixed],
        [
            struct(wide, BF),
            struct(wide, BF),
            struct((width, tok), BF),
            struct((tok, FF), BF),
            struct((8, width), F32),
        ],
        [
            pltpu.VMEM((width, FF), BF),
            pltpu.VMEM((width, FF), BF),
            pltpu.VMEM((width, width), BF),
            pltpu.VMEM(wide, F32),
            pltpu.VMEM(wide, F32),
            pltpu.VMEM(wide, BF),
            pltpu.VMEM((2, *wide), BF),
            pltpu.VMEM(wide, BF),
            pltpu.VMEM((width, tok), BF),
            pltpu.SemaphoreType.DMA((16,)),
            pltpu.SemaphoreType.DMA((16,)),
            pltpu.SemaphoreType.DMA((4,)),
            pltpu.SemaphoreType.DMA((7,)),
        ],
        1,
        4 * tok * width * FF,
        30 * 2**20,
    )(info, first, dz2, slope, rows, *down, *upper, *other)


def product_kernel(left_ref, right_ref, *outs):
    grad = dot(left_ref[...], right_ref[...])
    step = pl.program_id(0)
    for at, ref in enumerate(outs):
        @pl.when(step // 2 == at)
        def _():
            put_blocks(ref, grad)


def wide_grad(left_t, right, halves, blocks=4):
    width, tok = left_t.shape
    first = halves[0]
    spec = [
        pl.BlockSpec(
            (2, width, width // 2), lambda i, at=at: (jnp.clip(i - 2 * at, 0, 1), 0, 0)
        )
        for at in range(len(halves))
    ]
    return call(
        product_kernel,
        (2 * len(halves),),
        [
            pl.BlockSpec((width, tok), lambda i: (0, 0)),
            pl.BlockSpec((tok, width), lambda i: (0, (i + 2 * first) % 4)),
        ],
        spec,
        [struct((blocks, width, width // 2), BF)] * len(halves),
        [],
        0,
        tok * width * FF * len(halves),
        10 * 2**20 * len(halves),
    )(left_t, right)


def share_kernel(left_ref, right_ref, out_ref):
    put_blocks(out_ref, dot(left_ref[...], right_ref[...]))


def share_grad(left_t, right, half):
    width, tok = left_t.shape
    cols = right.shape[1] // 2
    shape = (3, width, cols // 3)
    return call(
        share_kernel,
        (1,),
        [
            pl.BlockSpec((width, tok), lambda i: (0, 0)),
            pl.BlockSpec((tok, cols), lambda i: (0, half)),
        ],
        [pl.BlockSpec(shape, lambda i: (0, 0, 0))],
        [struct(shape, BF)],
        [],
        0,
        2 * tok * width * cols,
        6 * 2**20,
    )(left_t, right)[0]


def up_grad_kernel(
    ht_ref, da_ref, dtt_in_ref, ctx_in_ref, gm_ref, gt_ref,
    held_ref, dtt_ref, ctx_ref, sem_ref, in_sem_ref,
):
    step = pl.program_id(0)
    loads = [
        pltpu.make_async_copy(dtt_in_ref, dtt_ref, in_sem_ref.at[0]),
        pltpu.make_async_copy(ctx_in_ref, ctx_ref, in_sem_ref.at[1]),
    ]
    start_first([loads])
    cols = held_ref.shape[3]

    def copies(at):
        targets = (
            [(ref, PARTS) for ref in (gm_ref, gt_ref)]
            if at == PARTS
            else [((gm_ref, gt_ref)[at // 2], at % 2 * 2 + block) for block in range(2)]
        )
        return [
            pltpu.make_async_copy(
                held_ref.at[at % 2, block], ref.at[target], sem_ref.at[at % 2, block]
            )
            for block, (ref, target) in enumerate(targets)
        ]

    for at in range(PARTS + 1):
        @pl.when(step == at)
        def _():
            if at == PARTS:
                wait_pairs([loads])
            left, right = (dtt_ref, ctx_ref) if at == PARTS else (ht_ref, da_ref)
            grad = dot(left[...], right[...])
            if at >= 2:
                for copy in copies(at - 2):
                    copy.wait()
            for block in range(2):
                held_ref[at % 2, block] = grad[:, block * cols : (block + 1) * cols].astype(BF)
            for copy in copies(at):
                copy.start()
            if at == PARTS:
                for copy in copies(at - 1) + copies(at):
                    copy.wait()


def up_grad(hidden_t, dt_t, grad_up, ctx):
    width, tok = hidden_t.shape
    cols = width // 2
    whole = pl.BlockSpec((width, tok), lambda i: (0, 0))
    return call(
        up_grad_kernel,
        (PARTS + 1,),
        [
            whole,
            pl.BlockSpec((tok, width), lambda i: (0, jnp.minimum(i, PARTS - 1))),
            ANY,
            ANY,
        ],
        [ANY, ANY],
        [struct((PARTS + 1, width, cols), BF)] * 2,
        [
            pltpu.VMEM((2, 2, width, cols), BF),
            pltpu.VMEM((width, tok), BF),
            pltpu.VMEM((tok, width), BF),
            pltpu.SemaphoreType.DMA((2, 2)),
            pltpu.SemaphoreType.DMA((2,)),
        ],
        0,
        2 * tok * width * (FF + width),
        25 * 2**20,
    )(hidden_t, grad_up, dt_t, ctx)


def attend_pairs_back(first, short, q_ref, k_ref, v_ref, dctx_ref, lse_ref, dqkv_ref):
    width = q_ref.shape[1]
    pairs = range(BACKWARD_PAIRS)
    lanes = [pair_lanes(first + pair) for pair in pairs]
    queries = [q_ref[:, at] * BF(HD**-0.5) for at in lanes]
    keys_here = [k_ref[:, at] for at in lanes]
    grads = [dctx_ref[:, at] for at in lanes]
    keys_t = [keys.T for keys in keys_here]
    scores = [dot_nt(both_heads(keys_here[pair]), queries[pair]) for pair in pairs]
    grad_probs = [
        by_head(dot_nt(both_heads(v_ref[:, lanes[pair]]), grads[pair])) for pair in pairs
    ]
    if short:
        scores = [jnp.where(seen_mask(), score, -1e30) for score in scores]
    probs = [
        jnp.exp(
            by_head(scores[pair])
            - jnp.stack(
                [
                    lse_ref[0, (first + pair) // 3, pl.ds((first + pair) % 3 * 2 + head, 1), :]
                    for head in range(2)
                ]
            )
        )
        for pair in pairs
    ]
    grad_v = [
        dot(prob.astype(BF).reshape(2 * LONG, LONG), grads[pair])
        for pair, prob in enumerate(probs)
    ]
    inners = [
        jnp.sum(prob * grad, axis=1, keepdims=True) for prob, grad in zip(probs, grad_probs)
    ]
    grad_scores = [
        (prob * (grad - inner)).astype(BF)
        for prob, grad, inner in zip(probs, grad_probs, inners)
    ]
    grad_k = [
        dot(grad.reshape(2 * LONG, LONG), queries[pair]) for pair, grad in enumerate(grad_scores)
    ]
    for pair in pairs:
        grad_q = [
            dot(keys_t[pair][head * HD : (head + 1) * HD], grad_scores[pair][head])
            for head in range(2)
        ]

        def store(part, values_in):
            at = first + pair
            half = at // 3
            start = half * (3 * width // 2) + part * (width // 2) + (at - 3 * half) * 2 * HD
            dqkv_ref[:, pl.ds(pl.multiple_of(start, 2 * HD), 2 * HD)] = values_in.astype(BF)

        store(0, jnp.concatenate(grad_q, axis=0).T * HD**-0.5)
        store(1, pair_columns(grad_k[pair]))
        store(2, pair_columns(grad_v[pair]))


def attend_back_kernel(
    info_ref, q_ref, k_ref, v_ref, dctx_ref, lse_ref, dqkv_ref, sum_ref,
):
    width = q_ref.shape[1]

    def all_pairs(short):
        @pl.loop(0, width // (2 * HD), step=BACKWARD_PAIRS)
        def _(first):
            attend_pairs_back(first, short, q_ref, k_ref, v_ref, dctx_ref, lse_ref, dqkv_ref)

    @pl.when(info_ref[0] == 1)
    def _():
        all_pairs(False)

    @pl.when(info_ref[0] != 1)
    def _():
        all_pairs(True)

    sum_ref[...] = jnp.zeros_like(sum_ref)
    cols = width // 2
    for half in range(2):
        core = info_ref[1] if half == 0 else 1 - info_ref[1]
        spot = pl.ds(pl.multiple_of(core * cols, cols), cols)
        for row, part in enumerate((0, 2)):
            start = (3 * half + part) * cols
            sum_ref[row : row + 1, spot] = row_sum(dqkv_ref[:, start : start + cols].astype(F32))


def attend_back(group, info, q, k, v, dctx, lse, kept=None):
    tok, width = q.shape
    tile = pl.BlockSpec((LONG, width), lambda i, *_: (group, 0))
    dqkv, sums = call(
        attend_back_kernel,
        (1,),
        [
            tile, tile, tile, tile,
            pl.BlockSpec((1, 2, 8, LONG), lambda i, *_: (group, 0, 0, 0)),
        ],
        [
            pl.BlockSpec((LONG, 3 * width), lambda i, *_: (group, 0)),
            pl.BlockSpec((8, width), lambda i, *_: (0, 0)),
        ],
        [struct((tok, 3 * width), BF), struct((8, width), F32)],
        [],
        1,
        2 * LONG * width * 10 * LONG,
        12 * 2**20,
        LONG * LONG * 12,
        kept,
    )(info, q, k, v, dctx, lse, *(kept or ()))
    return dqkv, sums


def token_grad_kernel(info_ref, dqkv_ref, dz_ref, *refs):
    parts, (gx_ref, w_ref, sem_ref) = refs[:4], refs[4:]
    copies = load_blocks(info_ref, parts, SHARES, w_ref, sem_ref)
    start_first(copies)
    first_time(copies)
    gx_ref[...] = (dz_ref[...].astype(F32) + dot_nt(dqkv_ref[...], w_ref[...])).astype(BF)


def token_grad(info, dqkv, dz, weights):
    tok, width = dz.shape
    tile = pl.BlockSpec((LONG, width), lambda i, *_: (i, 0))
    return call(
        token_grad_kernel,
        (tok // LONG,),
        [pl.BlockSpec((LONG, 3 * width), lambda i, *_: (i, 0)), tile] + [ANY] * 4,
        [tile],
        [struct((tok, width), BF)],
        [pltpu.VMEM((width, 3 * width), BF), pltpu.SemaphoreType.DMA((12,))],
        1,
        6 * tok * width * width,
        15 * 2**20,
    )(info, dqkv, dz, *weights)[0]


def adamw_update(weights_in, moment, square, average_in, gradient, rate, scalars):
    beta_one, beta_two, ema_decay, scale_one, scale_two = scalars
    moment_new = beta_one * moment + (1.0 - beta_one) * gradient
    square_new = beta_two * square + (1.0 - beta_two) * gradient * gradient
    moment_hat = moment_new * scale_one
    square_hat = square_new * scale_two
    weights_new = weights_in - rate * (
        moment_hat / (jnp.sqrt(square_hat) + 1e-08) + 0.01 * weights_in
    )
    average_new = ema_decay * average_in + (1.0 - ema_decay) * weights_new
    return weights_new, moment_new, square_new, average_new


SLOT_STEPS = 3
LATE = 4


def fetch_gradient(ref, table_ref, slot, held_ref, sem_ref, rows):
    spot = pl.ds(pl.multiple_of(table_ref[2, slot] * rows, rows), rows)
    return pltpu.make_async_copy(
        ref.at[table_ref[1, slot], spot], held_ref.at[slot], sem_ref.at[slot]
    )


def adamw_kernel(table_ref, scale_ref, w_ref, m_ref, s_ref, a_ref, *refs):
    grads, outs, (held_ref, sem_ref) = refs[:4], refs[4:8], refs[8:]
    step = pl.program_id(0)
    count, rows, _ = w_ref.shape

    @pl.when(step == 0)
    def _():
        @pl.loop(0, held_ref.shape[0])
        def _(slot):
            for at, ref in enumerate(grads):
                chosen = table_ref[0, slot] == at + LATE
                if at == 0:
                    chosen = table_ref[0, slot] <= LATE

                @pl.when(chosen)
                def _():
                    fetch_gradient(ref, table_ref, slot, held_ref, sem_ref, rows).start()

    scalars = [scale_ref[at] for at in range(5)]

    @pl.loop(0, count)
    def _(at):
        slot = step * count + at
        fetch_gradient(grads[0], table_ref, slot, held_ref, sem_ref, rows).wait()
        gradient = held_ref[slot].astype(F32) * scale_ref[8 + 2 * slot]
        results = adamw_update(
            w_ref[at], m_ref[at], s_ref[at], a_ref[at], gradient,
            scale_ref[9 + 2 * slot], scalars,
        )
        for ref, value in zip(outs, results):
            ref[at] = value


def adamw_slots(table, scales, states, grads):
    cap, rows, cols = states[0].shape
    steps = SLOT_STEPS if cap % SLOT_STEPS == 0 else 1
    own = pl.BlockSpec((cap // steps, rows, cols), lambda i, *_: (i, 0, 0))
    return call(
        adamw_kernel,
        (steps,),
        [own] * 4 + [ANY] * 4,
        [own] * 4,
        [struct(states[0].shape, F32)] * 4,
        [pltpu.VMEM((cap, rows, cols), BF), pltpu.SemaphoreType.DMA((cap,))],
        2,
        20 * cap * rows * cols,
        40 * cap * rows * cols,
    )(table, scales, *states, *grads)


def late_kernel(table_ref, scale_ref, *refs):
    states, grads, outs, scratch = refs[:4], refs[4:8], refs[8:12], refs[12:]
    state_ref, result_ref, held_ref, sem_ref, state_sem_ref, out_sem_ref = scratch
    cap, rows, _ = held_ref.shape
    scalars = [scale_ref[at] for at in range(5)]

    def loads(slot):
        return [
            pltpu.make_async_copy(ref.at[slot], state_ref.at[slot, at], state_sem_ref.at[slot, at])
            for at, ref in enumerate(states)
        ]

    def stores(slot):
        return [
            pltpu.make_async_copy(result_ref.at[slot, at], ref.at[slot], out_sem_ref.at[slot, at])
            for at, ref in enumerate(outs)
        ]

    def each(work):
        @pl.loop(0, cap)
        def _(slot):
            @pl.when(table_ref[0, slot] < LATE)
            def _():
                work(slot)

    def begin(slot):
        for at, ref in enumerate(grads):
            @pl.when(table_ref[0, slot] == at)
            def _():
                fetch_gradient(ref, table_ref, slot, held_ref, sem_ref, rows).start()
        for copy in loads(slot):
            copy.start()

    def update(slot):
        fetch_gradient(grads[0], table_ref, slot, held_ref, sem_ref, rows).wait()
        for copy in loads(slot):
            copy.wait()
        gradient = held_ref[slot].astype(F32) * scale_ref[8 + 2 * slot]
        results = adamw_update(
            *[state_ref[slot, at] for at in range(4)], gradient, scale_ref[9 + 2 * slot], scalars
        )
        for at, value in enumerate(results):
            result_ref[slot, at] = value
        for copy in stores(slot):
            copy.start()

    def finish(slot):
        for copy in stores(slot):
            copy.wait()

    each(begin)
    each(update)
    each(finish)


def adamw_late(table, scales, states, grads, kept):
    cap, rows, cols = states[0].shape
    return call(
        late_kernel,
        (1,),
        [ANY] * 8,
        [ANY] * 4,
        [struct(states[0].shape, F32)] * 4,
        [
            pltpu.VMEM((cap, 4, rows, cols), F32),
            pltpu.VMEM((cap, 4, rows, cols), F32),
            pltpu.VMEM((cap, rows, cols), BF),
            pltpu.SemaphoreType.DMA((cap,)),
            pltpu.SemaphoreType.DMA((cap, 4)),
            pltpu.SemaphoreType.DMA((cap, 4)),
        ],
        2,
        20 * cap * rows * cols,
        40 * cap * rows * cols,
        0,
        kept,
    )(table, scales, *states, *grads, *kept)


def on_device(
    tokens,
    cotangent,
    phase_of,
    unit_slot,
    step_count,
    learn_rates,
    decay_rates,
    master,
    first_moment,
    second_moment,
    average,
    vector_state,
):
    cap, unit_rows, cols = master.shape
    tok_rows, width = tokens.shape
    batch_count = lax.axis_size("batch")
    row_blocks = width // unit_rows
    col_blocks = FF // width
    core = lax.axis_index("tensor")
    place = lax.axis_index("batch")
    fast = batch_count == FAST_BATCH
    plane, y_at, x_at = place // 4, (place // 2) % 2, place % 2
    up_base = 4 * row_blocks
    down_base = up_base + row_blocks * col_blocks
    chunks = [(0, 1, row_blocks), (up_base, col_blocks, 1), (down_base, col_blocks, 1)]
    corner = jnp.stack([place % 4, place % 4, plane]).astype(jnp.int32)

    def coords(orient):
        y_first = (core + orient) % 2 == 0
        first = jnp.where(y_first, y_at, x_at)
        second = jnp.where(y_first, x_at, y_at)
        return jnp.stack([first, second, plane]).astype(jnp.int32)

    places = [coords(orient) for orient in range(2)]

    def chunk_units(chunk):
        base, row_step, block_step = chunk
        return base + jnp.arange(4)[:, None] * block_step + jnp.arange(row_blocks)[None] * row_step

    def spreads(sources, which):
        first_bit = jnp.where(core == 0, 2, 1)
        inner = place % 4
        numbers = jnp.stack(
            [
                places[0][0] * 2 + places[0][1], plane, place,
                inner, inner ^ first_bit, inner ^ (3 - first_bit), inner ^ 3,
            ]
        ).astype(jnp.int32)
        return [spread(sources, unit_slot, numbers, chunks[at]) for at in which]

    def weights_chain(pieces):
        return Chain(spreading(pieces, 0, places[0]))

    def weights_plain(at):
        local = unit_slot[chunk_units(chunks[at])] - place * cap
        own = (local >= 0) & (local < cap)
        blocks = jnp.take(master, jnp.clip(local, 0, cap - 1), axis=0)
        blocks = jnp.where(own[..., None, None], blocks, 0.0).astype(BF)
        return lax.psum(blocks.reshape(4, width, cols), "batch")

    def grads_chain(terms, orient):
        return Chain(exchange(terms, orient, places[orient]))

    def shared(array_in):
        half = array_in.shape[1] // 2
        parts = [array_in[:, :half], array_in[:, half:]]
        return parts + [core_swap(part) for part in parts]

    def halves_of(array_in):
        other = lax.dynamic_slice_in_dim(array_in, (1 - core) * cols, cols, array_in.ndim - 1)
        return lax.dynamic_slice_in_dim(array_in, core * cols, cols, array_in.ndim - 1), other

    def swapped(array_in):
        return jnp.concatenate(halves_of(array_in), axis=-1)

    def both(here, there):
        low_first = core == 0
        return jnp.concatenate(
            [jnp.where(low_first, here, there), jnp.where(low_first, there, here)], axis=0
        )

    count_f = step_count[0].astype(F32)
    scalars = [
        decay_rates[0],
        decay_rates[1],
        decay_rates[2],
        1.0 / (1.0 - decay_rates[0] ** count_f),
        1.0 / (1.0 - decay_rates[1] ** count_f),
    ]

    def vec_update(sums):
        vector_grads = jnp.concatenate(
            [sums[0:2], sums[8:11], sums[12:16], sums[16:19]], axis=0
        )
        grads_scaled = vector_grads * float(tok_rows * batch_count) ** (-0.5)
        vec_weights, vec_first, vec_second, vec_average = adamw_update(
            vector_state[0], vector_state[1], vector_state[2], vector_state[3],
            grads_scaled, learn_rates[4], scalars,
        )
        return (
            jnp.stack([vec_weights, vec_average]),
            jnp.stack([grads_scaled, vec_first]),
            vec_second,
        )

    my_ids = place * cap + jnp.arange(cap, dtype=jnp.int32)
    matches = unit_slot[None, :] == my_ids[:, None]
    unit_ids = jnp.arange(unit_slot.shape[0], dtype=jnp.int32)
    unit = jnp.sum(jnp.where(matches, unit_ids[None, :], 0), axis=1)
    occupied = jnp.any(matches, axis=1)
    is_up = (unit >= up_base) & (unit < down_base)
    is_down = unit >= down_base
    is_other = (unit >= 3 * row_blocks) & (unit < up_base)
    is_wide = is_up | is_down
    chunk_at = jnp.where(is_down, 2, jnp.where(is_up | is_other, 1, 0))
    local = unit - jnp.where(is_down, down_base, up_base)
    block_at = jnp.where(
        is_wide, local % col_blocks, jnp.where(is_other, col_blocks, unit // row_blocks)
    )
    row_at = jnp.where(is_wide, local // col_blocks, unit % row_blocks)
    kind = jnp.where(
        occupied,
        (unit >= 3 * row_blocks).astype(jnp.int32) + is_up.astype(jnp.int32) + 2 * is_down,
        0,
    )
    rates = jnp.sum(
        jnp.where(kind[:, None] == jnp.arange(4)[None, :], learn_rates[None, :4], 0.0), axis=1
    )
    quarter_rows, half_rows = row_blocks // 4, row_blocks // 2
    first_quarter = corner[0] if fast else 0
    first_half = jnp.where(chunk_at == 1, places[1][0], places[0][0]) if fast else 0
    array_at = jnp.where(
        chunk_at == 0,
        (row_at // quarter_rows) ^ first_quarter,
        2 + 2 * chunk_at + ((row_at // half_rows) ^ first_half),
    )
    row_at = jnp.where(chunk_at == 0, row_at % quarter_rows, row_at % half_rows)
    table = jnp.stack([array_at, block_at, row_at]).astype(jnp.int32)
    states = (master, first_moment, second_moment, average)
    scales = jnp.concatenate(
        [
            jnp.stack(scalars),
            jnp.zeros((3,), F32),
            jnp.stack([occupied.astype(F32), rates], axis=1).reshape(-1),
        ]
    )
    firsts = [places[0][0], places[1][0]] if fast else [0, 0]
    info = jnp.stack([phase_of[0], core, *firsts]).astype(jnp.int32)
    vectors = vector_state[0]
    rows = jnp.concatenate([swapped(vectors[0:2]), vectors[2:5], vectors[9:12]], axis=0)
    upper = vectors[5:9].reshape(2, FF // 2)
    turned = jnp.concatenate([upper[1:], upper[:1]], axis=0)
    bias_up = jnp.where(core == 0, upper, turned).reshape(4, width)

    if fast:
        low_master = master.astype(BF)
        beside = lax.ppermute(low_master, BOTH, swap_pairs(0, 1))
        across = lax.ppermute(low_master, BOTH, swap_pairs(0, 2))
        diagonal = lax.ppermute(beside, BOTH, swap_pairs(0, 2))
        sources = (low_master, beside, across, diagonal)
        io = weights_chain(spreads(sources, (0,))[0])
        _, (up, down) = phase([io], work=lambda _: spreads(sources, (1, 2)))
        up, down = weights_chain(up), weights_chain(down)
        _, (info, rows, bias_up, table, scales) = phase(
            [io], work=lambda _: (info, rows, bias_up, table, scales)
        )
        phase([io, up])
        theirs_first, _ = phase([io, up], io.ready)
        theirs_last, begun = phase(
            [up, down],
            io.result[1:],
            lambda late: forward(0, after(info, late), tokens, rows, io.result),
        )
        weights_io = [*io.result, *theirs_first, *theirs_last]
        theirs_first, stage = phase(
            [up, down],
            up.ready,
            lambda late: forward(1, after(info, late), tokens, rows, weights_io, begun),
        )
        theirs_last, _ = phase([down], up.result[1:])
        weights_up = [*up.result, *theirs_first, *theirs_last]
        q, k, v, ctx, lse, first = stage
        x_t = begun[6]
        theirs_first, (act, slope, hidden_t, hidden) = phase(
            [down],
            down.ready,
            lambda late: feed_up(after(info, late), first, rows, bias_up, weights_up),
        )
        theirs_last, _ = phase(swaps=down.result[1:])
        weights_down = [*down.result, *theirs_first, *theirs_last]
    else:
        weights_io, weights_up, weights_down = [shared(weights_plain(at)) for at in range(3)]
        begun = forward(0, info, tokens, rows, weights_io)
        q, k, v, ctx, lse, first = forward(1, info, tokens, rows, weights_io, begun)
        x_t = begun[6]
        act, slope, hidden_t, hidden = feed_up(info, first, rows, bias_up, weights_up)

    out_half, dz2, grad_two_t, down_theirs, sums_two = feed_down(
        info, hidden, act, cotangent, rows, weights_down
    )
    heads = (q, k, v)

    def back(info):
        return feed_back(
            info, first, dz2, slope, rows, weights_down, weights_up, weights_io
        )

    def heads_back(group, info, dctx, kept=None):
        return attend_back(group, info, *heads, dctx, lse, kept)

    if fast:
        (other,), (down_mine,) = phase(
            swaps=[down_theirs], work=lambda late: wide_grad(after(grad_two_t, late), act, (0,))
        )
        down = grads_chain([down_mine, other], 0)
        (out_other,), (dz1, dctx, dt_t, grad_up, sums_one) = phase(
            [down], [out_half], lambda late: back(after(info, late))
        )
        _, (up_mine, up_theirs) = phase(
            [down],
            work=lambda late: up_grad(after(hidden_t, late), dt_t, grad_up, ctx),
        )
        (other,), (dqkv, sums_zero) = phase(
            [down], [up_theirs], lambda late: heads_back(0, after(info, late), dctx)
        )
        up = grads_chain([up_mine, other], 1)
        _, (dqkv, sums_extra) = phase(
            [down, up],
            work=lambda late: heads_back(1, after(info, late), dctx, [dqkv]),
        )
        vec = Chain(doubling(jnp.concatenate([sums_zero + sums_extra, sums_one, sums_two])))
        _, (io_theirs, grad_x) = phase(
            [down, up, vec],
            work=lambda late: (
                share_grad(after(x_t, late), dqkv, 1),
                token_grad(info, dqkv, dz1, weights_io),
            ),
        )
        (other,), io_mine = phase(
            [down, up, vec], [io_theirs], lambda late: share_grad(after(x_t, late), dqkv, 0)
        )
        io = Chain(plane_exchange([io_mine, other], corner))
        (grad_x_other,), out = phase(
            [io, up, vec], [grad_x], lambda late: both(after(out_half, late), out_other)
        )
        _, input_grad = phase(
            [io, up, vec],
            work=lambda late: both(after(grad_x, late), grad_x_other).astype(F32),
        )
        phase([io, up, vec])
        _, (new_states, vec_outs) = phase(
            [io],
            work=lambda late: (
                adamw_slots(after(table, late), scales, states, [*up.result, *down.result]),
                vec_update(after(vec.result, late)),
            ),
        )
        grads = io.result
    else:
        dz1, dctx, dt_t, grad_up, sums_one = back(info)
        dqkv, sums_zero = heads_back(0, info, dctx)
        for group in range(1, tok_rows // 2 // LONG):
            dqkv, sums_extra = heads_back(group, info, dctx, [dqkv])
            sums_zero = sums_zero + sums_extra
        grad_x = token_grad(info, dqkv, dz1, weights_io)
        up_mine, up_theirs = up_grad(hidden_t, dt_t, grad_up, ctx)
        (down_mine,) = wide_grad(grad_two_t, act, (0,))
        grads = []
        for mine, theirs, parts in (
            (share_grad(x_t, dqkv, 0), share_grad(x_t, dqkv, 1), 4),
            (up_mine, up_theirs, 2),
            (down_mine, down_theirs, 2),
        ):
            grad = lax.psum(total(mine, core_swap(theirs)), "batch")
            grads += jnp.split(grad, parts, axis=1)
        new_states = adamw_slots(table, scales, states, grads[4:])
        grads = grads[:4]
        vec_outs = vec_update(
            lax.psum(jnp.concatenate([sums_zero, sums_one, sums_two]), BOTH)
        )
        out = both(out_half, core_swap(out_half))
        input_grad = both(grad_x, core_swap(grad_x)).astype(F32)

    new_states = adamw_late(table, scales, states, grads, new_states)
    return (out, input_grad, *new_states, *vec_outs)


def solution(mesh):
    return jax.shard_map(
        on_device,
        mesh=mesh,
        in_specs=(
            P("batch", None),
            P("batch", None),
            P("batch"),
            P(),
            P(),
            P(),
            P(),
            P("batch", None, "tensor"),
            P("batch", None, "tensor"),
            P("batch", None, "tensor"),
            P("batch", None, "tensor"),
            P(),
        ),
        out_specs=(
            P("batch", None),
            P("batch", None),
            P("batch", None, "tensor"),
            P("batch", None, "tensor"),
            P("batch", None, "tensor"),
            P("batch", None, "tensor"),
            P(),
            P(),
            P(),
        ),
        check_vma=False,
    )
```

```python
import functools

import jax
import jax.numpy as jnp
from jax import lax
from jax.experimental import pallas as pl
from jax.experimental.pallas import tpu as pltpu
from jax.sharding import PartitionSpec as P

HD = 64
FF = 3072
SHORT = 128
LONG = 512
EPS = 1e-12
BF = jnp.bfloat16
F32 = jnp.float32
VMEM_BYTES = 60 * 2**20
BOTH = ("batch", "tensor")
ANY = pl.BlockSpec(memory_space=pl.ANY)
PLANES = 4
FAST_BATCH = 16


def dot(first_mat, second_mat):
    return lax.dot_general(
        first_mat, second_mat, (((1,), (0,)), ((), ())), preferred_element_type=F32
    )


def dot_nt(first_mat, second_mat):
    return lax.dot_general(
        first_mat, second_mat, (((1,), (1,)), ((), ())), preferred_element_type=F32
    )


def normalized(rows):
    centred = rows - jnp.mean(rows, axis=-1, keepdims=True)
    inverse = lax.rsqrt(jnp.mean(centred * centred, axis=-1, keepdims=True) + EPS)
    return centred * inverse, inverse


def norm_back(grad_scaled, normal, inverse):
    mean_grad = jnp.mean(grad_scaled, axis=-1, keepdims=True)
    mean_both = jnp.mean(grad_scaled * normal, axis=-1, keepdims=True)
    return inverse * (grad_scaled - mean_grad - normal * mean_both)


def fold_rows(array_in):
    rows, cols = array_in.shape
    return jnp.sum(array_in.reshape(rows // 8, 8, cols), axis=0)


def row_sum(array_in):
    return jnp.sum(array_in, axis=0, keepdims=True)


def load_blocks(info_ref, parts, blocks, weight_ref, sem_ref):
    _, half_rows, cols = parts[0].shape
    copies = []
    for spot, (half, block) in enumerate(blocks):
        first = info_ref[2 + half]
        pair = []
        for at in range(2):
            start = pl.multiple_of((first if at == 0 else 1 - first) * half_rows, half_rows)
            pair.append(
                pltpu.make_async_copy(
                    parts[2 * half + at].at[block],
                    weight_ref.at[pl.ds(start, half_rows), pl.ds(spot * cols, cols)],
                    sem_ref.at[2 * spot + at],
                )
            )
        copies.append(pair)
    return copies


def after(array_in, *others):
    return lax.optimization_barrier((array_in, others))[0]


def first_time(copies):
    @pl.when(pl.program_id(0) == 0)
    def _():
        for pair in copies:
            for copy in pair:
                copy.wait()


def start_first(copies):
    @pl.when(pl.program_id(0) == 0)
    def _():
        for pair in copies:
            for copy in pair:
                copy.start()


PAIRED = [(half, block) for block in range(4) for half in range(2)]
SHARES = [(half, block) for half in range(2) for block in range(3)]
HALVED = [(half, block) for half in range(2) for block in range(4)]


def call(
    kernel, grid, in_specs, out_specs, out_shape, scratch, prefetch, flops, moved, exps=0, kept=None
):
    aliases = {}
    if kept is not None:
        given = prefetch + len(in_specs)
        count = len(kept)
        in_specs = in_specs + [ANY] * count
        aliases = {given + at: at for at in range(count)}
        inner = kernel

        def kernel(*refs):
            inner(*refs[:given], *refs[given + count :])

    return pl.pallas_call(
        kernel,
        input_output_aliases=aliases,
        out_shape=out_shape,
        grid_spec=pltpu.PrefetchScalarGridSpec(
            num_scalar_prefetch=prefetch,
            grid=grid,
            in_specs=in_specs,
            out_specs=out_specs,
            scratch_shapes=scratch,
        ),
        compiler_params=pltpu.CompilerParams(vmem_limit_bytes=VMEM_BYTES),
        cost_estimate=pl.CostEstimate(
            flops=10 * flops, bytes_accessed=moved, transcendentals=exps
        ),
    )


def struct(shape, kind):
    return jax.ShapeDtypeStruct(shape, kind)


def spread_kernel(
    base, row_step, block_step, cap, rows, info_ref, slot_ref, *refs
):
    sources, outs, (held_ref, quarter_ref, sem_ref) = refs[:4], refs[4:8], refs[8:]
    quarter, plane = info_ref[0], info_ref[1]
    copies = [
        [
            pltpu.make_async_copy(
                ref, held_ref.at[pl.ds(info_ref[3 + at] * cap, cap)], sem_ref.at[at]
            )
        ]
        for at, ref in enumerate(sources)
    ]
    start_first(copies)
    first_time(copies)
    total_slots = PLANES * cap
    for block in range(quarter_ref.shape[0]):
        for step in range(3):
            unit = base + (quarter * 3 + step) * row_step + block * block_step
            local = slot_ref[unit] - plane * total_slots
            here = (local >= 0) & (local < total_slots)
            spot = slice(step * rows, (step + 1) * rows)

            @pl.when(here)
            def _():
                quarter_ref[block, spot, :] = held_ref[local]

            @pl.when(jnp.logical_not(here))
            def _():
                quarter_ref[block, spot, :] = jnp.zeros((rows, quarter_ref.shape[2]), BF)

    for ahead, out_ref in enumerate(outs):
        size = out_ref.shape[1]
        start = pl.multiple_of(lax.rem(plane + ahead, PLANES) * size, size)
        out_ref[...] = quarter_ref[:, pl.ds(start, size), :]


def spread(sources, unit_slot, info, chunk):
    cap, rows, cols = sources[0].shape
    base, row_step, block_step = chunk
    size = 3 * rows // PLANES
    block = pl.BlockSpec((4, size, cols), lambda i, *_: (0, 0, 0))
    return call(
        functools.partial(spread_kernel, base, row_step, block_step, cap, rows),
        (1,),
        [ANY] * 4,
        [block] * 4,
        [struct((4, size, cols), BF)] * 4,
        [
            pltpu.VMEM((PLANES * cap, rows, cols), BF),
            pltpu.VMEM((4, 3 * rows, cols), BF),
            pltpu.SemaphoreType.DMA((4,)),
        ],
        2,
        0,
        5 * 2**20,
    )(info, unit_slot, *sources)


def swap_pairs(orient, stage):
    pairs = []
    for place in range(FAST_BATCH):
        for core in range(2):
            first_bit = 2 if (core + orient) % 2 == 0 else 1
            bit = first_bit if stage == 1 else 3 - first_bit
            pairs.append((place * 2 + core, (place ^ bit) * 2 + core))
    return pairs


def flip_pairs(bit):
    return [
        (place * 2 + core, (place ^ bit) * 2 + core)
        for place in range(FAST_BATCH)
        for core in range(2)
    ]


def plane_pairs(step):
    return [
        (place * 2 + core, (place + 4 * step) % FAST_BATCH * 2 + core)
        for place in range(FAST_BATCH)
        for core in range(2)
    ]


def total(*terms):
    result = terms[0].astype(F32)
    for term in terms[1:]:
        result = result + term.astype(F32)
    return result.astype(BF)


def send(array_in, pairs):
    return lax.ppermute(array_in, BOTH, pairs)


def cut(array_in, start, size):
    return lax.dynamic_slice_in_dim(array_in, start, size, 1)


def first_split(info, terms):
    half = terms[0].shape[1] // 2
    return total(*[cut(term, (1 - info[0]) * half, half) for term in terms])


def second_split(info, terms, got):
    half = got.shape[1] // 2
    start = (1 - info[1]) * half
    kept = [cut(term, info[0] * got.shape[1] + start, half) for term in terms]
    return total(*kept, cut(got, start, half))


def third_split(info, terms, one, two):
    half = two.shape[1]
    size = half // PLANES
    pieces = []
    for ahead in range(PLANES):
        start = (info[2] + ahead) % PLANES * size
        first = info[1] * half + start
        kept = [cut(term, info[0] * one.shape[1] + first, size) for term in terms]
        pieces.append(total(*kept, cut(one, first, size), cut(two, start, size)))
    return pieces


def plane_join(info, pieces):
    return jnp.concatenate(
        [lax.select_n((info[2] - row) % PLANES, *pieces) for row in range(PLANES)], axis=1
    )


def half_join(info, here, there):
    low_first = info[1] == 0
    return jnp.concatenate(
        [jnp.where(low_first, here, there), jnp.where(low_first, there, here)], axis=1
    )


def exchange(terms, orient, info):
    (one,) = yield [(first_split(info, terms), swap_pairs(orient, 1))]
    (two,) = yield [(second_split(info, terms, one), swap_pairs(orient, 2))]
    own, *pieces = third_split(info, terms, one, two)
    return (yield from spreading([own] + pieces, orient, info))


def spreading(pieces, orient, info):
    arrived = yield [(pieces[step], plane_pairs(step)) for step in range(1, PLANES)]
    owned = total(pieces[0], *arrived)
    others = yield [(owned, plane_pairs(step)) for step in range(1, PLANES)]
    level = plane_join(info, [owned] + others)
    (there,) = yield [(level, swap_pairs(orient, 2))]
    level = half_join(info, level, there)
    (there,) = yield [(level, swap_pairs(orient, 1))]
    return level, there


def plane_exchange(terms, info):
    quarter = terms[0].shape[1] // 4
    size = quarter // PLANES
    going = [
        total(*[cut(term, (info[0] ^ away) * quarter, quarter) for term in terms])
        for away in (1, 2, 3)
    ]
    got = yield [(piece, flip_pairs(away)) for away, piece in zip((1, 2, 3), going)]
    parts = []
    for ahead in range(PLANES):
        start = (info[2] + ahead) % PLANES * size
        kept = [cut(term, info[0] * quarter + start, size) for term in terms]
        parts.append(total(*kept, *[cut(piece, start, size) for piece in got]))
    arrived = yield [(parts[step], plane_pairs(step)) for step in range(1, PLANES)]
    owned = total(parts[0], *arrived)
    others = yield [(owned, plane_pairs(step)) for step in range(1, PLANES)]
    level = plane_join(info, [owned] + others)
    there = yield [(level, flip_pairs(away)) for away in (1, 2, 3)]
    return [level] + there


def doubling(array_in):
    cores = [(at, at ^ 1) for at in range(2 * FAST_BATCH)]
    for pairs in [cores] + [flip_pairs(bit) for bit in (1, 2, 4, 8)]:
        (other,) = yield [(array_in, pairs)]
        array_in = array_in + other
    return array_in


class Chain:
    def __init__(self, steps):
        self.steps = steps
        self.result = None
        self.pending = next(steps)

    @property
    def ready(self):
        return [parts for parts, _ in self.pending]

    def begin(self):
        return [send(parts, pairs) for parts, pairs in self.pending]

    def take(self, arrived):
        try:
            self.pending = self.steps.send(arrived)
        except StopIteration as stop:
            self.pending, self.result = [], stop.value


def phase(chains=(), swaps=(), work=None):
    ready, swaps = lax.optimization_barrier(([chain.ready for chain in chains], list(swaps)))
    arrived = [
        [send(parts, pairs) for parts, (_, pairs) in zip(given, chain.pending)]
        for given, chain in zip(ready, chains)
    ]
    swapped = [core_swap(array) for array in swaps]
    done = None if work is None else work((ready, swaps))
    arrived, swapped, done = lax.optimization_barrier((arrived, swapped, done))
    for chain, parts in zip(chains, arrived):
        chain.take(parts)
    return swapped, done


def core_swap(array_in):
    return lax.ppermute(array_in, "tensor", [(0, 1), (1, 0)])


def seen_mask():
    key_at = lax.broadcasted_iota(jnp.int32, (2 * LONG, LONG), 0) % LONG // SHORT
    query_at = lax.broadcasted_iota(jnp.int32, (2 * LONG, LONG), 1) // SHORT
    return key_at == query_at


def low_lanes(rows):
    return lax.broadcasted_iota(jnp.int32, (rows, 2 * HD), 1) < HD


def pair_lanes(pair):
    return pl.ds(pl.multiple_of(pair * 2 * HD, 2 * HD), 2 * HD)


def both_heads(array_in):
    low = low_lanes(array_in.shape[0])
    none = jnp.zeros_like(array_in)
    return jnp.concatenate(
        [jnp.where(low, array_in, none), jnp.where(low, none, array_in)], axis=0
    )


def by_head(array_in):
    return array_in.reshape(2, LONG, array_in.shape[1])


def pair_columns(array_in):
    return jnp.where(low_lanes(LONG), array_in[:LONG], array_in[LONG:])


BACKWARD_PAIRS = 1


def attend_pairs(short, q_ref, k_ref, v_ref, ctx_ref, lse_ref):
    pairs = range(q_ref.shape[1] // (2 * HD))
    lanes = [slice(pair * 2 * HD, (pair + 1) * 2 * HD) for pair in pairs]
    queries = [q_ref[:, at] * BF(HD**-0.5) for at in lanes]
    keys_here = [both_heads(k_ref[:, at]) for at in lanes]
    values_t = [v_ref[:, at].T for at in lanes]
    scores = [dot_nt(keys_here[pair], queries[pair]) for pair in pairs]
    if short:
        scores = [jnp.where(seen_mask(), score, -1e30) for score in scores]
    scores = [by_head(score) for score in scores]
    tops = [jnp.max(score, axis=1, keepdims=True) for score in scores]
    weights = [jnp.exp(score - top) for score, top in zip(scores, tops)]
    norms = [jnp.sum(weight, axis=1, keepdims=True) for weight in weights]
    probs = [(weight * (1.0 / norm)).astype(BF) for weight, norm in zip(weights, norms)]
    for pair in pairs:
        outs = [
            dot(values_t[pair][head * HD : (head + 1) * HD], probs[pair][head])
            for head in range(2)
        ]
        ctx_ref[:, lanes[pair]] = jnp.concatenate(outs, axis=0).T.astype(BF)
        for head in range(2):
            spot = slice(pair * 2 + head, pair * 2 + head + 1)
            lse_ref[0, 0, spot, :] = tops[pair][head] + jnp.log(norms[pair][head])


def forward_kernel(half, info_ref, x_ref, rows_ref, first_ref, last_ref, *refs):
    if half == 0:
        before_ref, refs = None, refs
        q_ref, k_ref, v_ref, ctx_ref, lse_ref, z_ref, xt_ref, w_ref, sem_ref = refs
    else:
        before_ref, q_ref, k_ref, v_ref, ctx_ref, lse_ref, z_ref, w_ref, sem_ref = refs
    cols = q_ref.shape[1]
    parts = (first_ref, last_ref) * 2
    copies = load_blocks(info_ref, parts, [(half, block) for block in range(4)], w_ref, sem_ref)
    start_first(copies)
    tokens = x_ref[...]
    if half == 0:
        xt_ref[...] = tokens.T
    first_time(copies[:3])
    projected = dot(tokens, w_ref[:, : 3 * cols])
    spot = slice(half * cols, (half + 1) * cols)
    q_ref[...] = (projected[:, :cols] + rows_ref[0:1, spot]).astype(BF)
    k_ref[...] = projected[:, cols : 2 * cols].astype(BF)
    v_ref[...] = (projected[:, 2 * cols :] + rows_ref[1:2, spot]).astype(BF)

    @pl.when(info_ref[0] == 1)
    def _():
        attend_pairs(False, q_ref, k_ref, v_ref, ctx_ref, lse_ref)

    @pl.when(info_ref[0] != 1)
    def _():
        attend_pairs(True, q_ref, k_ref, v_ref, ctx_ref, lse_ref)

    first_time(copies[3:])
    attended = dot_nt(ctx_ref[...], w_ref[:, 3 * cols :])
    if half == 0:
        z_ref[...] = tokens.astype(F32) + attended + rows_ref[2:3]
    else:
        z_ref[...] = before_ref[...] + attended


def forward(half, info, tokens, rows, weights, before=None):
    tok = tokens.shape[0] // 2
    width = tokens.shape[1]
    cols = width // 2
    groups = tok // LONG
    tile = pl.BlockSpec((LONG, width), lambda i, *_: (i, 0))
    part = pl.BlockSpec((LONG, cols), lambda i, *_: (i, half))
    low = struct((tok, width), BF)
    in_specs = [
        pl.BlockSpec((LONG, width), lambda i, info: (info[1] * groups + i, 0)),
        pl.BlockSpec((8, width), lambda i, *_: (0, 0)),
        ANY,
        ANY,
    ]
    out_specs = [
        part, part, part, part,
        pl.BlockSpec((1, 1, 8, LONG), lambda i, *_: (i, half, 0, 0)),
        tile,
    ]
    outs = [low, low, low, low, struct((groups, 2, 8, LONG), F32), struct((tok, width), F32)]
    inputs, kept = [], None
    if half == 0:
        out_specs.append(pl.BlockSpec((width, LONG), lambda i, *_: (0, i)))
        outs.append(struct((width, tok), BF))
    else:
        *kept, partial_sum = before[:6]
        inputs = [partial_sum]
        in_specs.append(tile)
    return call(
        functools.partial(forward_kernel, half),
        (groups,),
        in_specs,
        out_specs,
        outs,
        [pltpu.VMEM((width, 4 * cols), BF), pltpu.SemaphoreType.DMA((8,))],
        1,
        2 * tok * width * (4 * cols + LONG),
        12 * 2**20,
        tok * LONG * 6,
        kept,
    )(info, tokens, rows, *weights[2 * half : 2 * half + 2], *inputs, *(kept or ()))


def up_kernel(
    info_ref, z_ref, rows_ref, bias_ref, w0_ref, w1_ref, w2_ref, w3_ref,
    act_ref, slope_ref, ht_ref, hidden_ref, w_ref, sem_ref,
):
    width = z_ref.shape[1]
    parts = (w0_ref, w1_ref, w2_ref, w3_ref)
    copies = load_blocks(info_ref, parts, HALVED, w_ref, sem_ref)
    start_first(copies)
    normal, _ = normalized(z_ref[...])
    hidden = normal * rows_ref[3:4] + rows_ref[4:5]
    hidden_ref[...] = hidden
    low = hidden.astype(BF)
    ht_ref[...] = low.T
    for part in range(FF // width):
        spot = slice(part * width, (part + 1) * width)
        first_time(copies[2 * part : 2 * part + 2])
        upper = dot(low, w_ref[:, spot]) + bias_ref[part : part + 1]
        phi_sum = 0.5 + 0.5 * lax.erf(upper * (0.5**0.5))
        density = jnp.exp(-0.5 * upper * upper) * 0.3989422804014327
        act_ref[:, spot] = (upper * phi_sum).astype(BF)
        slope_ref[:, spot] = (phi_sum + upper * density).astype(BF)


ROWS, COLUMNS, NORM_ROWS = 256, 256, 128
UP_TILE = 256


def feed_up(info, first, rows, bias, weights):
    tok, width = first.shape
    wide = struct((tok, FF), BF)
    return call(
        up_kernel,
        (tok // UP_TILE,),
        [
            pl.BlockSpec((UP_TILE, width), lambda i, *_: (i, 0)),
            pl.BlockSpec((8, width), lambda i, *_: (0, 0)),
            pl.BlockSpec((4, width), lambda i, *_: (0, 0)),
        ]
        + [ANY] * 4,
        [
            pl.BlockSpec((UP_TILE, FF), lambda i, *_: (i, 0)),
            pl.BlockSpec((UP_TILE, FF), lambda i, *_: (i, 0)),
            pl.BlockSpec((width, UP_TILE), lambda i, *_: (0, i)),
            pl.BlockSpec((UP_TILE, width), lambda i, *_: (i, 0)),
        ],
        [wide, wide, struct((width, tok), BF), struct((tok, width), F32)],
        [pltpu.VMEM((width, FF), BF), pltpu.SemaphoreType.DMA((16,))],
        1,
        2 * tok * width * FF,
        20 * 2**20,
        tok * FF * 2,
    )(info, first, rows, bias, *weights)


PARTS = 4


def wait_pairs(copies):
    for pair in copies:
        for copy in pair:
            copy.wait()


def down_kernel(info_ref, h_in_ref, act_ref, cot_in_ref, rows_ref, *refs):
    parts, outs, gt_ref, sum_ref = refs[:4], refs[4:7], refs[7], refs[8]
    w_ref, h_ref, cot_ref, branch_ref = refs[9:13]
    out_ref, dz_ref, dyt_ref, low_ref, sem_ref, own_sem_ref = refs[13:]
    step = pl.program_id(0)
    tok, width = h_ref.shape
    copies = load_blocks(info_ref, parts, HALVED, w_ref, sem_ref)
    start = pl.multiple_of(info_ref[1] * tok, tok)
    h_copy = pltpu.make_async_copy(h_in_ref, h_ref, own_sem_ref.at[0])
    cot_copy = pltpu.make_async_copy(
        cot_in_ref.at[pl.ds(start, tok)], cot_ref, own_sem_ref.at[1]
    )
    out_copies = [
        pltpu.make_async_copy(source, target, own_sem_ref.at[2 + at])
        for at, (source, target) in enumerate(zip((out_ref, dz_ref, dyt_ref), outs))
    ]
    start_first(copies)

    @pl.when(step == 0)
    def _():
        h_copy.start()
        cot_copy.start()
        sum_ref[...] = jnp.zeros_like(sum_ref)

    for part in range(PARTS):
        @pl.when(step == part)
        def _():
            wait_pairs(copies[2 * part : 2 * part + 2])
            lanes = slice(part * width, (part + 1) * width)
            branch = dot_nt(act_ref[...], w_ref[:, lanes])
            branch_ref[...] = branch if part == 0 else branch_ref[...] + branch

    @pl.when(step == PARTS - 1)
    def _():
        h_copy.wait()
        cot_copy.wait()
        gains = rows_ref[6:7]
        sums = [0.0, 0.0, 0.0]
        for row in range(0, tok, NORM_ROWS):
            spot = slice(row, row + NORM_ROWS)
            normal, inverse = normalized(h_ref[spot, :] + branch_ref[spot, :] + rows_ref[5:6])
            out_ref[spot, :] = (normal * gains + rows_ref[7:8]).astype(BF)
            cot = cot_ref[spot, :].astype(F32)
            grad = norm_back(cot * gains, normal, inverse)
            dz_ref[spot, :] = grad
            low_ref[spot, :] = grad.astype(BF)
            for at, value in enumerate((grad, cot * normal, cot)):
                sums[at] = sums[at] + fold_rows(value)
        dyt_ref[...] = low_ref[...].T
        for at in range(3):
            sum_ref[at : at + 1] += row_sum(sums[at])
        for copy in out_copies:
            copy.start()

    @pl.when(step >= PARTS)
    def _():
        put_blocks(gt_ref, dot(dyt_ref[...], act_ref[...]))

    @pl.when(step == PARTS + 1)
    def _():
        for copy in out_copies:
            copy.wait()


def put_blocks(ref, grad):
    cols = ref.shape[2]
    for block in range(ref.shape[0]):
        ref[block] = grad[:, block * cols : (block + 1) * cols].astype(BF)


def feed_down(info, hidden, act, cot, rows, weights):
    tok, width = hidden.shape
    wide = (tok, width)
    return call(
        down_kernel,
        (PARTS + 2,),
        [
            ANY,
            pl.BlockSpec(wide, lambda i, *_: (0, jnp.where(i < PARTS, i, i - 2))),
            ANY,
            pl.BlockSpec((8, width), lambda i, *_: (0, 0)),
        ]
        + [ANY] * 4,
        [
            ANY,
            ANY,
            ANY,
            pl.BlockSpec((2, width, width // 2), lambda i, *_: (jnp.clip(i - PARTS, 0, 1), 0, 0)),
            pl.BlockSpec((8, width), lambda i, *_: (0, 0)),
        ],
        [
            struct(wide, BF),
            struct(wide, F32),
            struct((width, tok), BF),
            struct((4, width, width // 2), BF),
            struct((8, width), F32),
        ],
        [
            pltpu.VMEM((width, FF), BF),
            pltpu.VMEM(wide, F32),
            pltpu.VMEM(wide, BF),
            pltpu.VMEM(wide, F32),
            pltpu.VMEM(wide, BF),
            pltpu.VMEM(wide, F32),
            pltpu.VMEM((width, tok), BF),
            pltpu.VMEM(wide, BF),
            pltpu.SemaphoreType.DMA((16,)),
            pltpu.SemaphoreType.DMA((5,)),
        ],
        1,
        3 * tok * width * FF,
        30 * 2**20,
    )(info, hidden, act, cot, rows, *weights)


def back_kernel(info_ref, z_in_ref, dz2_ref, slope_ref, rows_ref, *refs):
    down, upper, other = refs[:4], refs[4:8], refs[8:12]
    outs, da_ref, sum_ref = refs[12:15], refs[15], refs[16]
    wd_ref, wu_ref, wo_ref, z_ref, hidden_ref, low_ref, held_ref = refs[17:24]
    dctx_ref, dtt_ref, dsem_ref, usem_ref, osem_ref, own_sem_ref = refs[24:]
    step = pl.program_id(0)
    tok, width = z_ref.shape
    downs = load_blocks(info_ref, down, HALVED, wd_ref, dsem_ref)
    ups = load_blocks(info_ref, upper, HALVED, wu_ref, usem_ref)
    others = load_blocks(info_ref, other, [(0, 3), (1, 3)], wo_ref, osem_ref)
    z_copy = pltpu.make_async_copy(z_in_ref, z_ref, own_sem_ref.at[0])
    for at in range(0, 8, 2):
        start_first(downs[at : at + 2] + ups[at : at + 2])
    start_first(others + [[z_copy]])

    @pl.when(step == 0)
    def _():
        sum_ref[...] = jnp.zeros_like(sum_ref)
        hidden_ref[...] = dz2_ref[...]
        low_ref[...] = dz2_ref[...].astype(BF)

    for part in range(PARTS + 1):
        @pl.when(step == part)
        def _():
            if part < PARTS:
                wait_pairs(downs[2 * part : 2 * part + 2])
            if part > 0:
                wait_pairs(ups[2 * part - 2 : 2 * part])
            place = 4 + (part ^ (2 * info_ref[1]))
            for column in range(0, width, COLUMNS):
                spot = slice(column, column + COLUMNS)
                lanes = slice(part * width + column, part * width + column + COLUMNS)
                if part < PARTS:
                    grad_act = dot(low_ref[...], wd_ref[:, lanes])
                if part > 0:
                    before = slice((part - 1) * width, part * width)
                    hidden_ref[:, spot] += dot_nt(held_ref[(part - 1) % 2], wu_ref[spot, before])
                if part < PARTS:
                    grad_up = (grad_act * slope_ref[:, spot].astype(F32)).astype(BF)
                    da_ref[:, spot] = grad_up
                    held_ref[part % 2, :, spot] = grad_up
                    sum_ref[pl.ds(place, 1), spot] = row_sum(fold_rows(grad_up.astype(F32)))

    @pl.when(step == PARTS)
    def _():
        z_copy.wait()
        gains = rows_ref[3:4]
        sums = [0.0, 0.0, 0.0]
        out_copies = []
        for half in range(2):
            rows = slice(half * (tok // 2), (half + 1) * (tok // 2))
            for row in range(rows.start, rows.stop, NORM_ROWS):
                spot = slice(row, row + NORM_ROWS)
                grad_hidden = hidden_ref[spot, :]
                normal, inverse = normalized(z_ref[spot, :])
                grad_one = norm_back(grad_hidden * gains, normal, inverse)
                low_ref[spot, :] = grad_one.astype(BF)
                for at, value in enumerate((grad_one, grad_hidden * normal, grad_hidden)):
                    sums[at] = sums[at] + fold_rows(value)
            if half == 0:
                wait_pairs(others)
            dctx_ref[rows, :] = dot(low_ref[rows, :], wo_ref[...]).astype(BF)
            dtt_ref[:, rows] = low_ref[rows, :].T
            spot = pl.ds(rows.start, tok // 2)
            for at, (source, target) in enumerate(zip((low_ref, dctx_ref, dtt_ref), outs)):
                source, target = (
                    (source.at[:, spot], target.at[:, spot])
                    if at == 2
                    else (source.at[spot], target.at[spot])
                )
                out_copies.append(
                    pltpu.make_async_copy(source, target, own_sem_ref.at[1 + 3 * half + at])
                )
                out_copies[-1].start()
        for at in range(3):
            sum_ref[at : at + 1] = row_sum(sums[at])
        for copy in out_copies:
            copy.wait()


def feed_back(info, first, dz2, slope, rows, down, upper, other):
    tok, width = first.shape
    wide = (tok, width)
    fixed = pl.BlockSpec((8, width), lambda i, *_: (0, 0))
    part = pl.BlockSpec(wide, lambda i, *_: (0, jnp.minimum(i, PARTS - 1)))
    return call(
        back_kernel,
        (PARTS + 1,),
        [ANY, pl.BlockSpec(wide, lambda i, *_: (0, 0)), part, fixed] + [ANY] * 12,
        [ANY, ANY, ANY, part, fixed],
        [
            struct(wide, BF),
            struct(wide, BF),
            struct((width, tok), BF),
            struct((tok, FF), BF),
            struct((8, width), F32),
        ],
        [
            pltpu.VMEM((width, FF), BF),
            pltpu.VMEM((width, FF), BF),
            pltpu.VMEM((width, width), BF),
            pltpu.VMEM(wide, F32),
            pltpu.VMEM(wide, F32),
            pltpu.VMEM(wide, BF),
            pltpu.VMEM((2, *wide), BF),
            pltpu.VMEM(wide, BF),
            pltpu.VMEM((width, tok), BF),
            pltpu.SemaphoreType.DMA((16,)),
            pltpu.SemaphoreType.DMA((16,)),
            pltpu.SemaphoreType.DMA((4,)),
            pltpu.SemaphoreType.DMA((7,)),
        ],
        1,
        4 * tok * width * FF,
        30 * 2**20,
    )(info, first, dz2, slope, rows, *down, *upper, *other)


def product_kernel(left_ref, right_ref, *outs):
    grad = dot(left_ref[...], right_ref[...])
    step = pl.program_id(0)
    for at, ref in enumerate(outs):
        @pl.when(step // 2 == at)
        def _():
            put_blocks(ref, grad)


def wide_grad(left_t, right, halves, blocks=4):
    width, tok = left_t.shape
    first = halves[0]
    spec = [
        pl.BlockSpec(
            (2, width, width // 2), lambda i, at=at: (jnp.clip(i - 2 * at, 0, 1), 0, 0)
        )
        for at in range(len(halves))
    ]
    return call(
        product_kernel,
        (2 * len(halves),),
        [
            pl.BlockSpec((width, tok), lambda i: (0, 0)),
            pl.BlockSpec((tok, width), lambda i: (0, (i + 2 * first) % 4)),
        ],
        spec,
        [struct((blocks, width, width // 2), BF)] * len(halves),
        [],
        0,
        tok * width * FF * len(halves),
        10 * 2**20 * len(halves),
    )(left_t, right)


def share_kernel(left_ref, right_ref, out_ref):
    put_blocks(out_ref, dot(left_ref[...], right_ref[...]))


def share_grad(left_t, right, half):
    width, tok = left_t.shape
    cols = right.shape[1] // 2
    shape = (3, width, cols // 3)
    return call(
        share_kernel,
        (1,),
        [
            pl.BlockSpec((width, tok), lambda i: (0, 0)),
            pl.BlockSpec((tok, cols), lambda i: (0, half)),
        ],
        [pl.BlockSpec(shape, lambda i: (0, 0, 0))],
        [struct(shape, BF)],
        [],
        0,
        2 * tok * width * cols,
        6 * 2**20,
    )(left_t, right)[0]


def up_grad_kernel(
    ht_ref, da_ref, dtt_in_ref, ctx_in_ref, gm_ref, gt_ref,
    held_ref, dtt_ref, ctx_ref, sem_ref, in_sem_ref,
):
    step = pl.program_id(0)
    loads = [
        pltpu.make_async_copy(dtt_in_ref, dtt_ref, in_sem_ref.at[0]),
        pltpu.make_async_copy(ctx_in_ref, ctx_ref, in_sem_ref.at[1]),
    ]
    start_first([loads])
    cols = held_ref.shape[3]

    def copies(at):
        targets = (
            [(ref, PARTS) for ref in (gm_ref, gt_ref)]
            if at == PARTS
            else [((gm_ref, gt_ref)[at // 2], at % 2 * 2 + block) for block in range(2)]
        )
        return [
            pltpu.make_async_copy(
                held_ref.at[at % 2, block], ref.at[target], sem_ref.at[at % 2, block]
            )
            for block, (ref, target) in enumerate(targets)
        ]

    for at in range(PARTS + 1):
        @pl.when(step == at)
        def _():
            if at == PARTS:
                wait_pairs([loads])
            left, right = (dtt_ref, ctx_ref) if at == PARTS else (ht_ref, da_ref)
            grad = dot(left[...], right[...])
            if at >= 2:
                for copy in copies(at - 2):
                    copy.wait()
            for block in range(2):
                held_ref[at % 2, block] = grad[:, block * cols : (block + 1) * cols].astype(BF)
            for copy in copies(at):
                copy.start()
            if at == PARTS:
                for copy in copies(at - 1) + copies(at):
                    copy.wait()


def up_grad(hidden_t, dt_t, grad_up, ctx):
    width, tok = hidden_t.shape
    cols = width // 2
    whole = pl.BlockSpec((width, tok), lambda i: (0, 0))
    return call(
        up_grad_kernel,
        (PARTS + 1,),
        [
            whole,
            pl.BlockSpec((tok, width), lambda i: (0, jnp.minimum(i, PARTS - 1))),
            ANY,
            ANY,
        ],
        [ANY, ANY],
        [struct((PARTS + 1, width, cols), BF)] * 2,
        [
            pltpu.VMEM((2, 2, width, cols), BF),
            pltpu.VMEM((width, tok), BF),
            pltpu.VMEM((tok, width), BF),
            pltpu.SemaphoreType.DMA((2, 2)),
            pltpu.SemaphoreType.DMA((2,)),
        ],
        0,
        2 * tok * width * (FF + width),
        25 * 2**20,
    )(hidden_t, grad_up, dt_t, ctx)


def attend_pairs_back(first, short, q_ref, k_ref, v_ref, dctx_ref, lse_ref, dqkv_ref):
    width = q_ref.shape[1]
    pairs = range(BACKWARD_PAIRS)
    lanes = [pair_lanes(first + pair) for pair in pairs]
    queries = [q_ref[:, at] * BF(HD**-0.5) for at in lanes]
    keys_here = [k_ref[:, at] for at in lanes]
    grads = [dctx_ref[:, at] for at in lanes]
    keys_t = [keys.T for keys in keys_here]
    scores = [dot_nt(both_heads(keys_here[pair]), queries[pair]) for pair in pairs]
    grad_probs = [
        by_head(dot_nt(both_heads(v_ref[:, lanes[pair]]), grads[pair])) for pair in pairs
    ]
    if short:
        scores = [jnp.where(seen_mask(), score, -1e30) for score in scores]
    probs = [
        jnp.exp(
            by_head(scores[pair])
            - jnp.stack(
                [
                    lse_ref[0, (first + pair) // 3, pl.ds((first + pair) % 3 * 2 + head, 1), :]
                    for head in range(2)
                ]
            )
        )
        for pair in pairs
    ]
    grad_v = [
        dot(prob.astype(BF).reshape(2 * LONG, LONG), grads[pair])
        for pair, prob in enumerate(probs)
    ]
    inners = [
        jnp.sum(prob * grad, axis=1, keepdims=True) for prob, grad in zip(probs, grad_probs)
    ]
    grad_scores = [
        (prob * (grad - inner)).astype(BF)
        for prob, grad, inner in zip(probs, grad_probs, inners)
    ]
    grad_k = [
        dot(grad.reshape(2 * LONG, LONG), queries[pair]) for pair, grad in enumerate(grad_scores)
    ]
    for pair in pairs:
        grad_q = [
            dot(keys_t[pair][head * HD : (head + 1) * HD], grad_scores[pair][head])
            for head in range(2)
        ]

        def store(part, values_in):
            at = first + pair
            half = at // 3
            start = half * (3 * width // 2) + part * (width // 2) + (at - 3 * half) * 2 * HD
            dqkv_ref[:, pl.ds(pl.multiple_of(start, 2 * HD), 2 * HD)] = values_in.astype(BF)

        store(0, jnp.concatenate(grad_q, axis=0).T * HD**-0.5)
        store(1, pair_columns(grad_k[pair]))
        store(2, pair_columns(grad_v[pair]))


def attend_back_kernel(
    info_ref, q_ref, k_ref, v_ref, dctx_ref, lse_ref, dqkv_ref, sum_ref,
):
    width = q_ref.shape[1]

    def all_pairs(short):
        @pl.loop(0, width // (2 * HD), step=BACKWARD_PAIRS)
        def _(first):
            attend_pairs_back(first, short, q_ref, k_ref, v_ref, dctx_ref, lse_ref, dqkv_ref)

    @pl.when(info_ref[0] == 1)
    def _():
        all_pairs(False)

    @pl.when(info_ref[0] != 1)
    def _():
        all_pairs(True)

    sum_ref[...] = jnp.zeros_like(sum_ref)
    cols = width // 2
    for half in range(2):
        core = info_ref[1] if half == 0 else 1 - info_ref[1]
        spot = pl.ds(pl.multiple_of(core * cols, cols), cols)
        for row, part in enumerate((0, 2)):
            start = (3 * half + part) * cols
            sum_ref[row : row + 1, spot] = row_sum(dqkv_ref[:, start : start + cols].astype(F32))


def attend_back(group, info, q, k, v, dctx, lse, kept=None):
    tok, width = q.shape
    tile = pl.BlockSpec((LONG, width), lambda i, *_: (group, 0))
    dqkv, sums = call(
        attend_back_kernel,
        (1,),
        [
            tile, tile, tile, tile,
            pl.BlockSpec((1, 2, 8, LONG), lambda i, *_: (group, 0, 0, 0)),
        ],
        [
            pl.BlockSpec((LONG, 3 * width), lambda i, *_: (group, 0)),
            pl.BlockSpec((8, width), lambda i, *_: (0, 0)),
        ],
        [struct((tok, 3 * width), BF), struct((8, width), F32)],
        [],
        1,
        2 * LONG * width * 10 * LONG,
        12 * 2**20,
        LONG * LONG * 12,
        kept,
    )(info, q, k, v, dctx, lse, *(kept or ()))
    return dqkv, sums


def token_grad_kernel(info_ref, dqkv_ref, dz_ref, *refs):
    parts, (gx_ref, w_ref, sem_ref) = refs[:4], refs[4:]
    copies = load_blocks(info_ref, parts, SHARES, w_ref, sem_ref)
    start_first(copies)
    first_time(copies)
    gx_ref[...] = (dz_ref[...].astype(F32) + dot_nt(dqkv_ref[...], w_ref[...])).astype(BF)


def token_grad(info, dqkv, dz, weights):
    tok, width = dz.shape
    tile = pl.BlockSpec((LONG, width), lambda i, *_: (i, 0))
    return call(
        token_grad_kernel,
        (tok // LONG,),
        [pl.BlockSpec((LONG, 3 * width), lambda i, *_: (i, 0)), tile] + [ANY] * 4,
        [tile],
        [struct((tok, width), BF)],
        [pltpu.VMEM((width, 3 * width), BF), pltpu.SemaphoreType.DMA((12,))],
        1,
        6 * tok * width * width,
        15 * 2**20,
    )(info, dqkv, dz, *weights)[0]


def adamw_update(weights_in, moment, square, average_in, gradient, rate, scalars):
    beta_one, beta_two, ema_decay, scale_one, scale_two = scalars
    moment_new = beta_one * moment + (1.0 - beta_one) * gradient
    square_new = beta_two * square + (1.0 - beta_two) * gradient * gradient
    moment_hat = moment_new * scale_one
    square_hat = square_new * scale_two
    weights_new = weights_in - rate * (
        moment_hat / (jnp.sqrt(square_hat) + 1e-08) + 0.01 * weights_in
    )
    average_new = ema_decay * average_in + (1.0 - ema_decay) * weights_new
    return weights_new, moment_new, square_new, average_new


SLOT_STEPS = 3
LATE = 3


def fetch_gradient(ref, table_ref, slot, held_ref, sem_ref, rows):
    spot = pl.ds(pl.multiple_of(table_ref[2, slot] * rows, rows), rows)
    return pltpu.make_async_copy(
        ref.at[table_ref[1, slot], spot], held_ref.at[slot], sem_ref.at[slot]
    )


def await_gradient(ref, slot, held_ref, sem_ref, rows):
    pltpu.make_async_copy(
        ref.at[0, pl.ds(0, rows)], held_ref.at[slot], sem_ref.at[slot]
    ).wait()


def adamw_kernel(table_ref, scale_ref, w_ref, m_ref, s_ref, a_ref, *refs):
    grads, outs, (held_ref, sem_ref) = refs[:5], refs[5:9], refs[9:]
    step = pl.program_id(0)
    count, rows, _ = w_ref.shape

    @pl.when(step == 0)
    def _():
        @pl.loop(0, held_ref.shape[0])
        def _(slot):
            for at, ref in enumerate(grads):
                chosen = table_ref[0, slot] == at + LATE
                if at == 0:
                    chosen = table_ref[0, slot] <= LATE

                @pl.when(chosen)
                def _():
                    fetch_gradient(ref, table_ref, slot, held_ref, sem_ref, rows).start()

    scalars = [scale_ref[at] for at in range(5)]

    @pl.loop(0, count)
    def _(at):
        slot = step * count + at
        await_gradient(grads[0], slot, held_ref, sem_ref, rows)
        gradient = held_ref[slot].astype(F32) * scale_ref[8 + 2 * slot]
        results = adamw_update(
            w_ref[at], m_ref[at], s_ref[at], a_ref[at], gradient,
            scale_ref[9 + 2 * slot], scalars,
        )
        for ref, value in zip(outs, results):
            ref[at] = value


def adamw_slots(table, scales, states, grads):
    cap, rows, cols = states[0].shape
    steps = SLOT_STEPS if cap % SLOT_STEPS == 0 else 1
    own = pl.BlockSpec((cap // steps, rows, cols), lambda i, *_: (i, 0, 0))
    return call(
        adamw_kernel,
        (steps,),
        [own] * 4 + [ANY] * 5,
        [own] * 4,
        [struct(states[0].shape, F32)] * 4,
        [pltpu.VMEM((cap, rows, cols), BF), pltpu.SemaphoreType.DMA((cap,))],
        2,
        20 * cap * rows * cols,
        40 * cap * rows * cols,
    )(table, scales, *states, *grads)


def late_kernel(table_ref, scale_ref, *refs):
    states, grads, outs, scratch = refs[:4], refs[4:7], refs[7:11], refs[11:]
    state_ref, result_ref, held_ref, sem_ref, state_sem_ref, out_sem_ref = scratch
    cap, rows, _ = held_ref.shape
    scalars = [scale_ref[at] for at in range(5)]

    def loads(slot):
        return [
            pltpu.make_async_copy(ref.at[slot], state_ref.at[slot, at], state_sem_ref.at[slot, at])
            for at, ref in enumerate(states)
        ]

    def stores(slot):
        return [
            pltpu.make_async_copy(result_ref.at[slot, at], ref.at[slot], out_sem_ref.at[slot, at])
            for at, ref in enumerate(outs)
        ]

    def each(work):
        @pl.loop(0, cap)
        def _(slot):
            @pl.when(table_ref[0, slot] < LATE)
            def _():
                work(slot)

    def begin(slot):
        for at, ref in enumerate(grads):
            @pl.when(table_ref[0, slot] == at)
            def _():
                fetch_gradient(ref, table_ref, slot, held_ref, sem_ref, rows).start()
        for copy in loads(slot):
            copy.start()

    def update(slot):
        await_gradient(grads[0], slot, held_ref, sem_ref, rows)
        for copy in loads(slot):
            copy.wait()
        gradient = held_ref[slot].astype(F32) * scale_ref[8 + 2 * slot]
        results = adamw_update(
            *[state_ref[slot, at] for at in range(4)], gradient, scale_ref[9 + 2 * slot], scalars
        )
        for at, value in enumerate(results):
            result_ref[slot, at] = value
        for copy in stores(slot):
            copy.start()

    def finish(slot):
        for copy in stores(slot):
            copy.wait()

    each(begin)
    each(update)
    each(finish)


def adamw_late(table, scales, states, grads, kept):
    cap, rows, cols = states[0].shape
    return call(
        late_kernel,
        (1,),
        [ANY] * 7,
        [ANY] * 4,
        [struct(states[0].shape, F32)] * 4,
        [
            pltpu.VMEM((cap, 4, rows, cols), F32),
            pltpu.VMEM((cap, 4, rows, cols), F32),
            pltpu.VMEM((cap, rows, cols), BF),
            pltpu.SemaphoreType.DMA((cap,)),
            pltpu.SemaphoreType.DMA((cap, 4)),
            pltpu.SemaphoreType.DMA((cap, 4)),
        ],
        2,
        20 * cap * rows * cols,
        40 * cap * rows * cols,
        0,
        kept,
    )(table, scales, *states, *grads, *kept)


def on_device(
    tokens,
    cotangent,
    phase_of,
    unit_slot,
    step_count,
    learn_rates,
    decay_rates,
    master,
    first_moment,
    second_moment,
    average,
    vector_state,
):
    cap, unit_rows, cols = master.shape
    tok_rows, width = tokens.shape
    batch_count = lax.axis_size("batch")
    row_blocks = width // unit_rows
    col_blocks = FF // width
    core = lax.axis_index("tensor")
    place = lax.axis_index("batch")
    fast = batch_count == FAST_BATCH
    plane, y_at, x_at = place // 4, (place // 2) % 2, place % 2
    up_base = 4 * row_blocks
    down_base = up_base + row_blocks * col_blocks
    chunks = [(0, 1, row_blocks), (up_base, col_blocks, 1), (down_base, col_blocks, 1)]
    corner = jnp.stack([place % 4, place % 4, plane]).astype(jnp.int32)

    def coords(orient):
        y_first = (core + orient) % 2 == 0
        first = jnp.where(y_first, y_at, x_at)
        second = jnp.where(y_first, x_at, y_at)
        return jnp.stack([first, second, plane]).astype(jnp.int32)

    places = [coords(orient) for orient in range(2)]

    def chunk_units(chunk):
        base, row_step, block_step = chunk
        return base + jnp.arange(4)[:, None] * block_step + jnp.arange(row_blocks)[None] * row_step

    def spreads(sources, which):
        first_bit = jnp.where(core == 0, 2, 1)
        inner = place % 4
        numbers = jnp.stack(
            [
                places[0][0] * 2 + places[0][1], plane, place,
                inner, inner ^ first_bit, inner ^ (3 - first_bit), inner ^ 3,
            ]
        ).astype(jnp.int32)
        return [spread(sources, unit_slot, numbers, chunks[at]) for at in which]

    def weights_chain(pieces):
        return Chain(spreading(pieces, 0, places[0]))

    def weights_plain(at):
        local = unit_slot[chunk_units(chunks[at])] - place * cap
        own = (local >= 0) & (local < cap)
        blocks = jnp.take(master, jnp.clip(local, 0, cap - 1), axis=0)
        blocks = jnp.where(own[..., None, None], blocks, 0.0).astype(BF)
        return lax.psum(blocks.reshape(4, width, cols), "batch")

    def grads_chain(terms, orient):
        return Chain(exchange(terms, orient, places[orient]))

    def shared(array_in):
        half = array_in.shape[1] // 2
        parts = [array_in[:, :half], array_in[:, half:]]
        return parts + [core_swap(part) for part in parts]

    def halves_of(array_in):
        other = lax.dynamic_slice_in_dim(array_in, (1 - core) * cols, cols, array_in.ndim - 1)
        return lax.dynamic_slice_in_dim(array_in, core * cols, cols, array_in.ndim - 1), other

    def swapped(array_in):
        return jnp.concatenate(halves_of(array_in), axis=-1)

    def both(here, there):
        low_first = core == 0
        return jnp.concatenate(
            [jnp.where(low_first, here, there), jnp.where(low_first, there, here)], axis=0
        )

    count_f = step_count[0].astype(F32)
    scalars = [
        decay_rates[0],
        decay_rates[1],
        decay_rates[2],
        1.0 / (1.0 - decay_rates[0] ** count_f),
        1.0 / (1.0 - decay_rates[1] ** count_f),
    ]

    def vec_update(sums):
        vector_grads = jnp.concatenate(
            [sums[0:2], sums[8:11], sums[12:16], sums[16:19]], axis=0
        )
        grads_scaled = vector_grads * float(tok_rows * batch_count) ** (-0.5)
        vec_weights, vec_first, vec_second, vec_average = adamw_update(
            vector_state[0], vector_state[1], vector_state[2], vector_state[3],
            grads_scaled, learn_rates[4], scalars,
        )
        return (
            jnp.stack([vec_weights, vec_average]),
            jnp.stack([grads_scaled, vec_first]),
            vec_second,
        )

    my_ids = place * cap + jnp.arange(cap, dtype=jnp.int32)
    matches = unit_slot[None, :] == my_ids[:, None]
    unit_ids = jnp.arange(unit_slot.shape[0], dtype=jnp.int32)
    unit = jnp.sum(jnp.where(matches, unit_ids[None, :], 0), axis=1)
    occupied = jnp.any(matches, axis=1)
    is_up = (unit >= up_base) & (unit < down_base)
    is_down = unit >= down_base
    is_other = (unit >= 3 * row_blocks) & (unit < up_base)
    is_wide = is_up | is_down
    chunk_at = jnp.where(is_down, 2, jnp.where(is_up | is_other, 1, 0))
    local = unit - jnp.where(is_down, down_base, up_base)
    block_at = jnp.where(
        is_wide, local % col_blocks, jnp.where(is_other, col_blocks, unit // row_blocks)
    )
    row_at = jnp.where(is_wide, local // col_blocks, unit % row_blocks)
    kind = jnp.where(
        occupied,
        (unit >= 3 * row_blocks).astype(jnp.int32) + is_up.astype(jnp.int32) + 2 * is_down,
        0,
    )
    rates = jnp.sum(
        jnp.where(kind[:, None] == jnp.arange(4)[None, :], learn_rates[None, :4], 0.0), axis=1
    )
    quarter_rows, half_rows = row_blocks // 4, row_blocks // 2
    first_quarter = corner[0] if fast else 0
    first_half = jnp.where(chunk_at == 1, places[1][0], places[0][0]) if fast else 0
    array_at = jnp.where(
        chunk_at == 0,
        (((row_at // quarter_rows) ^ first_quarter) + 3) % 4,
        2 + 2 * chunk_at + ((row_at // half_rows) ^ first_half),
    )
    row_at = jnp.where(chunk_at == 0, row_at % quarter_rows, row_at % half_rows)
    table = jnp.stack([array_at, block_at, row_at]).astype(jnp.int32)
    states = (master, first_moment, second_moment, average)
    scales = jnp.concatenate(
        [
            jnp.stack(scalars),
            jnp.zeros((3,), F32),
            jnp.stack([occupied.astype(F32), rates], axis=1).reshape(-1),
        ]
    )
    firsts = [places[0][0], places[1][0]] if fast else [0, 0]
    info = jnp.stack([phase_of[0], core, *firsts]).astype(jnp.int32)
    vectors = vector_state[0]
    rows = jnp.concatenate([swapped(vectors[0:2]), vectors[2:5], vectors[9:12]], axis=0)
    upper = vectors[5:9].reshape(2, FF // 2)
    turned = jnp.concatenate([upper[1:], upper[:1]], axis=0)
    bias_up = jnp.where(core == 0, upper, turned).reshape(4, width)

    if fast:
        low_master = master.astype(BF)
        beside = lax.ppermute(low_master, BOTH, swap_pairs(0, 1))
        across = lax.ppermute(low_master, BOTH, swap_pairs(0, 2))
        diagonal = lax.ppermute(beside, BOTH, swap_pairs(0, 2))
        sources = (low_master, beside, across, diagonal)
        io = weights_chain(spreads(sources, (0,))[0])
        _, (up, down) = phase([io], work=lambda _: spreads(sources, (1, 2)))
        up, down = weights_chain(up), weights_chain(down)
        _, (info, rows, bias_up, table, scales) = phase(
            [io], work=lambda _: (info, rows, bias_up, table, scales)
        )
        phase([io, up])
        theirs_first, _ = phase([io, up], io.ready)
        theirs_last, begun = phase(
            [up, down],
            io.result[1:],
            lambda late: forward(0, after(info, late), tokens, rows, io.result),
        )
        weights_io = [*io.result, *theirs_first, *theirs_last]
        theirs_first, stage = phase(
            [up, down],
            up.ready,
            lambda late: forward(1, after(info, late), tokens, rows, weights_io, begun),
        )
        theirs_last, _ = phase([down], up.result[1:])
        weights_up = [*up.result, *theirs_first, *theirs_last]
        q, k, v, ctx, lse, first = stage
        x_t = begun[6]
        theirs_first, (act, slope, hidden_t, hidden) = phase(
            [down],
            down.ready,
            lambda late: feed_up(after(info, late), first, rows, bias_up, weights_up),
        )
        theirs_last, _ = phase(swaps=down.result[1:])
        weights_down = [*down.result, *theirs_first, *theirs_last]
    else:
        weights_io, weights_up, weights_down = [shared(weights_plain(at)) for at in range(3)]
        begun = forward(0, info, tokens, rows, weights_io)
        q, k, v, ctx, lse, first = forward(1, info, tokens, rows, weights_io, begun)
        x_t = begun[6]
        act, slope, hidden_t, hidden = feed_up(info, first, rows, bias_up, weights_up)

    out_half, dz2, grad_two_t, down_theirs, sums_two = feed_down(
        info, hidden, act, cotangent, rows, weights_down
    )
    heads = (q, k, v)

    def back(info):
        return feed_back(
            info, first, dz2, slope, rows, weights_down, weights_up, weights_io
        )

    def heads_back(group, info, dctx, kept=None):
        return attend_back(group, info, *heads, dctx, lse, kept)

    if fast:
        (other,), (down_mine,) = phase(
            swaps=[down_theirs], work=lambda late: wide_grad(after(grad_two_t, late), act, (0,))
        )
        down = grads_chain([down_mine, other], 0)
        (out_other,), (dz1, dctx, dt_t, grad_up, sums_one) = phase(
            [down], [out_half], lambda late: back(after(info, late))
        )
        _, (up_mine, up_theirs) = phase(
            [down],
            work=lambda late: up_grad(after(hidden_t, late), dt_t, grad_up, ctx),
        )
        (other,), (dqkv, sums_zero) = phase(
            [down], [up_theirs], lambda late: heads_back(0, after(info, late), dctx)
        )
        up = grads_chain([up_mine, other], 1)
        _, (dqkv, sums_extra) = phase(
            [down, up],
            work=lambda late: heads_back(1, after(info, late), dctx, [dqkv]),
        )
        vec = Chain(doubling(jnp.concatenate([sums_zero + sums_extra, sums_one, sums_two])))
        _, (io_theirs, grad_x) = phase(
            [down, up, vec],
            work=lambda late: (
                share_grad(after(x_t, late), dqkv, 1),
                token_grad(info, dqkv, dz1, weights_io),
            ),
        )
        (other,), io_mine = phase(
            [down, up, vec], [io_theirs], lambda late: share_grad(after(x_t, late), dqkv, 0)
        )
        io = Chain(plane_exchange([io_mine, other], corner))
        (grad_x_other,), out = phase(
            [io, up, vec], [grad_x], lambda late: both(after(out_half, late), out_other)
        )
        _, input_grad = phase(
            [io, up, vec],
            work=lambda late: both(after(grad_x, late), grad_x_other).astype(F32),
        )
        phase([io, up, vec])
        nearest = io.ready[0]
        _, (new_states, vec_outs) = phase(
            [io],
            work=lambda late: (
                adamw_slots(
                    after(table, late), scales, states, [nearest, *up.result, *down.result]
                ),
                vec_update(after(vec.result, late)),
            ),
        )
        grads = io.result[1:]
    else:
        dz1, dctx, dt_t, grad_up, sums_one = back(info)
        dqkv, sums_zero = heads_back(0, info, dctx)
        for group in range(1, tok_rows // 2 // LONG):
            dqkv, sums_extra = heads_back(group, info, dctx, [dqkv])
            sums_zero = sums_zero + sums_extra
        grad_x = token_grad(info, dqkv, dz1, weights_io)
        up_mine, up_theirs = up_grad(hidden_t, dt_t, grad_up, ctx)
        (down_mine,) = wide_grad(grad_two_t, act, (0,))
        grads = []
        for mine, theirs, parts in (
            (share_grad(x_t, dqkv, 0), share_grad(x_t, dqkv, 1), 4),
            (up_mine, up_theirs, 2),
            (down_mine, down_theirs, 2),
        ):
            grad = lax.psum(total(mine, core_swap(theirs)), "batch")
            grads += jnp.split(grad, parts, axis=1)
        new_states = adamw_slots(table, scales, states, [grads[0], *grads[4:]])
        grads = grads[1:4]
        vec_outs = vec_update(
            lax.psum(jnp.concatenate([sums_zero, sums_one, sums_two]), BOTH)
        )
        out = both(out_half, core_swap(out_half))
        input_grad = both(grad_x, core_swap(grad_x)).astype(F32)

    new_states = adamw_late(table, scales, states, grads, new_states)
    return (out, input_grad, *new_states, *vec_outs)


def solution(mesh):
    return jax.shard_map(
        on_device,
        mesh=mesh,
        in_specs=(
            P("batch", None),
            P("batch", None),
            P("batch"),
            P(),
            P(),
            P(),
            P(),
            P("batch", None, "tensor"),
            P("batch", None, "tensor"),
            P("batch", None, "tensor"),
            P("batch", None, "tensor"),
            P(),
        ),
        out_specs=(
            P("batch", None),
            P("batch", None),
            P("batch", None, "tensor"),
            P("batch", None, "tensor"),
            P("batch", None, "tensor"),
            P("batch", None, "tensor"),
            P(),
            P(),
            P(),
        ),
        check_vma=False,
    )
```

```python
import functools

import jax
import jax.numpy as jnp
from jax import lax
from jax.experimental import pallas as pl
from jax.experimental.pallas import tpu as pltpu
from jax.sharding import PartitionSpec as P

HD = 64
FF = 3072
SHORT = 128
LONG = 512
EPS = 1e-12
BF = jnp.bfloat16
F32 = jnp.float32
VMEM_BYTES = 60 * 2**20
BOTH = ("batch", "tensor")
ANY = pl.BlockSpec(memory_space=pl.ANY)
PLANES = 4
FAST_BATCH = 16


def dot(first_mat, second_mat):
    return lax.dot_general(
        first_mat, second_mat, (((1,), (0,)), ((), ())), preferred_element_type=F32
    )


def dot_nt(first_mat, second_mat):
    return lax.dot_general(
        first_mat, second_mat, (((1,), (1,)), ((), ())), preferred_element_type=F32
    )


def normalized(rows):
    centred = rows - jnp.mean(rows, axis=-1, keepdims=True)
    inverse = lax.rsqrt(jnp.mean(centred * centred, axis=-1, keepdims=True) + EPS)
    return centred * inverse, inverse


def norm_back(grad_scaled, normal, inverse):
    mean_grad = jnp.mean(grad_scaled, axis=-1, keepdims=True)
    mean_both = jnp.mean(grad_scaled * normal, axis=-1, keepdims=True)
    return inverse * (grad_scaled - mean_grad - normal * mean_both)


def fold_rows(array_in):
    rows, cols = array_in.shape
    return jnp.sum(array_in.reshape(rows // 8, 8, cols), axis=0)


def row_sum(array_in):
    return jnp.sum(array_in, axis=0, keepdims=True)


def load_blocks(info_ref, parts, blocks, weight_ref, sem_ref):
    _, half_rows, cols = parts[0].shape
    copies = []
    for spot, (half, block) in enumerate(blocks):
        first = info_ref[2 + half]
        pair = []
        for at in range(2):
            start = pl.multiple_of((first if at == 0 else 1 - first) * half_rows, half_rows)
            pair.append(
                pltpu.make_async_copy(
                    parts[2 * half + at].at[block],
                    weight_ref.at[pl.ds(start, half_rows), pl.ds(spot * cols, cols)],
                    sem_ref.at[2 * spot + at],
                )
            )
        copies.append(pair)
    return copies


def after(array_in, *others):
    return lax.optimization_barrier((array_in, others))[0]


def first_time(copies):
    @pl.when(pl.program_id(0) == 0)
    def _():
        for pair in copies:
            for copy in pair:
                copy.wait()


def start_first(copies):
    @pl.when(pl.program_id(0) == 0)
    def _():
        for pair in copies:
            for copy in pair:
                copy.start()


PAIRED = [(half, block) for block in range(4) for half in range(2)]
SHARES = [(half, block) for half in range(2) for block in range(3)]
HALVED = [(half, block) for half in range(2) for block in range(4)]


def call(
    kernel, grid, in_specs, out_specs, out_shape, scratch, prefetch, flops, moved, exps=0, kept=None
):
    aliases = {}
    if kept is not None:
        given = prefetch + len(in_specs)
        count = len(kept)
        in_specs = in_specs + [ANY] * count
        aliases = {given + at: at for at in range(count)}
        inner = kernel

        def kernel(*refs):
            inner(*refs[:given], *refs[given + count :])

    return pl.pallas_call(
        kernel,
        input_output_aliases=aliases,
        out_shape=out_shape,
        grid_spec=pltpu.PrefetchScalarGridSpec(
            num_scalar_prefetch=prefetch,
            grid=grid,
            in_specs=in_specs,
            out_specs=out_specs,
            scratch_shapes=scratch,
        ),
        compiler_params=pltpu.CompilerParams(vmem_limit_bytes=VMEM_BYTES),
        cost_estimate=pl.CostEstimate(
            flops=10 * flops, bytes_accessed=moved, transcendentals=exps
        ),
    )


def struct(shape, kind):
    return jax.ShapeDtypeStruct(shape, kind)


def spread_kernel(
    base, row_step, block_step, cap, rows, info_ref, slot_ref, *refs
):
    sources, outs, (held_ref, quarter_ref, sem_ref) = refs[:4], refs[4:8], refs[8:]
    quarter, plane = info_ref[0], info_ref[1]
    copies = [
        [
            pltpu.make_async_copy(
                ref, held_ref.at[pl.ds(info_ref[3 + at] * cap, cap)], sem_ref.at[at]
            )
        ]
        for at, ref in enumerate(sources)
    ]
    start_first(copies)
    first_time(copies)
    total_slots = PLANES * cap
    for block in range(quarter_ref.shape[0]):
        for step in range(3):
            unit = base + (quarter * 3 + step) * row_step + block * block_step
            local = slot_ref[unit] - plane * total_slots
            here = (local >= 0) & (local < total_slots)
            spot = slice(step * rows, (step + 1) * rows)

            @pl.when(here)
            def _():
                quarter_ref[block, spot, :] = held_ref[local]

            @pl.when(jnp.logical_not(here))
            def _():
                quarter_ref[block, spot, :] = jnp.zeros((rows, quarter_ref.shape[2]), BF)

    for ahead, out_ref in enumerate(outs):
        size = out_ref.shape[1]
        start = pl.multiple_of(lax.rem(plane + ahead, PLANES) * size, size)
        out_ref[...] = quarter_ref[:, pl.ds(start, size), :]


def spread(sources, unit_slot, info, chunk):
    cap, rows, cols = sources[0].shape
    base, row_step, block_step = chunk
    size = 3 * rows // PLANES
    block = pl.BlockSpec((4, size, cols), lambda i, *_: (0, 0, 0))
    return call(
        functools.partial(spread_kernel, base, row_step, block_step, cap, rows),
        (1,),
        [ANY] * 4,
        [block] * 4,
        [struct((4, size, cols), BF)] * 4,
        [
            pltpu.VMEM((PLANES * cap, rows, cols), BF),
            pltpu.VMEM((4, 3 * rows, cols), BF),
            pltpu.SemaphoreType.DMA((4,)),
        ],
        2,
        0,
        5 * 2**20,
    )(info, unit_slot, *sources)


def swap_pairs(orient, stage):
    pairs = []
    for place in range(FAST_BATCH):
        for core in range(2):
            first_bit = 2 if (core + orient) % 2 == 0 else 1
            bit = first_bit if stage == 1 else 3 - first_bit
            pairs.append((place * 2 + core, (place ^ bit) * 2 + core))
    return pairs


def flip_pairs(bit):
    return [
        (place * 2 + core, (place ^ bit) * 2 + core)
        for place in range(FAST_BATCH)
        for core in range(2)
    ]


def plane_pairs(step):
    return [
        (place * 2 + core, (place + 4 * step) % FAST_BATCH * 2 + core)
        for place in range(FAST_BATCH)
        for core in range(2)
    ]


def total(*terms):
    result = terms[0].astype(F32)
    for term in terms[1:]:
        result = result + term.astype(F32)
    return result.astype(BF)


def send(array_in, pairs):
    return lax.ppermute(array_in, BOTH, pairs)


def cut(array_in, start, size):
    return lax.dynamic_slice_in_dim(array_in, start, size, 1)


def first_split(info, terms):
    half = terms[0].shape[1] // 2
    return total(*[cut(term, (1 - info[0]) * half, half) for term in terms])


def second_split(info, terms, got):
    half = got.shape[1] // 2
    start = (1 - info[1]) * half
    kept = [cut(term, info[0] * got.shape[1] + start, half) for term in terms]
    return total(*kept, cut(got, start, half))


def third_split(info, terms, one, two):
    half = two.shape[1]
    size = half // PLANES
    pieces = []
    for ahead in range(PLANES):
        start = (info[2] + ahead) % PLANES * size
        first = info[1] * half + start
        kept = [cut(term, info[0] * one.shape[1] + first, size) for term in terms]
        pieces.append(total(*kept, cut(one, first, size), cut(two, start, size)))
    return pieces


def plane_join(info, pieces):
    return jnp.concatenate(
        [lax.select_n((info[2] - row) % PLANES, *pieces) for row in range(PLANES)], axis=1
    )


def half_join(info, here, there):
    low_first = info[1] == 0
    return jnp.concatenate(
        [jnp.where(low_first, here, there), jnp.where(low_first, there, here)], axis=1
    )


def exchange(terms, orient, info):
    (one,) = yield [(first_split(info, terms), swap_pairs(orient, 1))]
    (two,) = yield [(second_split(info, terms, one), swap_pairs(orient, 2))]
    own, *pieces = third_split(info, terms, one, two)
    return (yield from spreading([own] + pieces, orient, info))


def spreading(pieces, orient, info):
    arrived = yield [(pieces[step], plane_pairs(step)) for step in range(1, PLANES)]
    owned = total(pieces[0], *arrived)
    others = yield [(owned, plane_pairs(step)) for step in range(1, PLANES)]
    level = plane_join(info, [owned] + others)
    (there,) = yield [(level, swap_pairs(orient, 2))]
    level = half_join(info, level, there)
    (there,) = yield [(level, swap_pairs(orient, 1))]
    return level, there


def plane_exchange(terms, info):
    quarter = terms[0].shape[1] // 4
    size = quarter // PLANES
    going = [
        total(*[cut(term, (info[0] ^ away) * quarter, quarter) for term in terms])
        for away in (1, 2, 3)
    ]
    got = yield [(piece, flip_pairs(away)) for away, piece in zip((1, 2, 3), going)]
    parts = []
    for ahead in range(PLANES):
        start = (info[2] + ahead) % PLANES * size
        kept = [cut(term, info[0] * quarter + start, size) for term in terms]
        parts.append(total(*kept, *[cut(piece, start, size) for piece in got]))
    arrived = yield [(parts[step], plane_pairs(step)) for step in range(1, PLANES)]
    owned = total(parts[0], *arrived)
    others = yield [(owned, plane_pairs(step)) for step in range(1, PLANES)]
    level = plane_join(info, [owned] + others)
    there = yield [(level, flip_pairs(away)) for away in (1, 2, 3)]
    return [level] + there


def doubling(array_in):
    cores = [(at, at ^ 1) for at in range(2 * FAST_BATCH)]
    for pairs in [cores] + [flip_pairs(bit) for bit in (1, 2, 4, 8)]:
        (other,) = yield [(array_in, pairs)]
        array_in = array_in + other
    return array_in


class Chain:
    def __init__(self, steps):
        self.steps = steps
        self.result = None
        self.pending = next(steps)

    @property
    def ready(self):
        return [parts for parts, _ in self.pending]

    def begin(self):
        return [send(parts, pairs) for parts, pairs in self.pending]

    def take(self, arrived):
        try:
            self.pending = self.steps.send(arrived)
        except StopIteration as stop:
            self.pending, self.result = [], stop.value


def phase(chains=(), swaps=(), work=None):
    ready, swaps = lax.optimization_barrier(([chain.ready for chain in chains], list(swaps)))
    arrived = [
        [send(parts, pairs) for parts, (_, pairs) in zip(given, chain.pending)]
        for given, chain in zip(ready, chains)
    ]
    swapped = [core_swap(array) for array in swaps]
    done = None if work is None else work((ready, swaps))
    arrived, swapped, done = lax.optimization_barrier((arrived, swapped, done))
    for chain, parts in zip(chains, arrived):
        chain.take(parts)
    return swapped, done


def core_swap(array_in):
    return lax.ppermute(array_in, "tensor", [(0, 1), (1, 0)])


def seen_mask():
    key_at = lax.broadcasted_iota(jnp.int32, (2 * LONG, LONG), 0) % LONG // SHORT
    query_at = lax.broadcasted_iota(jnp.int32, (2 * LONG, LONG), 1) // SHORT
    return key_at == query_at


def low_lanes(rows):
    return lax.broadcasted_iota(jnp.int32, (rows, 2 * HD), 1) < HD


def pair_lanes(pair):
    return pl.ds(pl.multiple_of(pair * 2 * HD, 2 * HD), 2 * HD)


def both_heads(array_in):
    low = low_lanes(array_in.shape[0])
    none = jnp.zeros_like(array_in)
    return jnp.concatenate(
        [jnp.where(low, array_in, none), jnp.where(low, none, array_in)], axis=0
    )


def by_head(array_in):
    return array_in.reshape(2, LONG, array_in.shape[1])


def pair_columns(array_in):
    return jnp.where(low_lanes(LONG), array_in[:LONG], array_in[LONG:])


BACKWARD_PAIRS = 1


def attend_pairs(short, q_ref, k_ref, v_ref, ctx_ref, lse_ref):
    pairs = range(q_ref.shape[1] // (2 * HD))
    lanes = [slice(pair * 2 * HD, (pair + 1) * 2 * HD) for pair in pairs]
    queries = [q_ref[:, at] * BF(HD**-0.5) for at in lanes]
    keys_here = [both_heads(k_ref[:, at]) for at in lanes]
    values_t = [v_ref[:, at].T for at in lanes]
    scores = [dot_nt(keys_here[pair], queries[pair]) for pair in pairs]
    if short:
        scores = [jnp.where(seen_mask(), score, -1e30) for score in scores]
    scores = [by_head(score) for score in scores]
    tops = [jnp.max(score, axis=1, keepdims=True) for score in scores]
    weights = [jnp.exp(score - top) for score, top in zip(scores, tops)]
    norms = [jnp.sum(weight, axis=1, keepdims=True) for weight in weights]
    probs = [(weight * (1.0 / norm)).astype(BF) for weight, norm in zip(weights, norms)]
    for pair in pairs:
        outs = [
            dot(values_t[pair][head * HD : (head + 1) * HD], probs[pair][head])
            for head in range(2)
        ]
        ctx_ref[:, lanes[pair]] = jnp.concatenate(outs, axis=0).T.astype(BF)
        for head in range(2):
            spot = slice(pair * 2 + head, pair * 2 + head + 1)
            lse_ref[0, 0, spot, :] = tops[pair][head] + jnp.log(norms[pair][head])


def forward_kernel(half, info_ref, x_ref, rows_ref, first_ref, last_ref, *refs):
    if half == 0:
        before_ref, refs = None, refs
        q_ref, k_ref, v_ref, ctx_ref, lse_ref, z_ref, xt_ref, w_ref, sem_ref = refs
    else:
        before_ref, q_ref, k_ref, v_ref, ctx_ref, lse_ref, z_ref, w_ref, sem_ref = refs
    cols = q_ref.shape[1]
    parts = (first_ref, last_ref) * 2
    copies = load_blocks(info_ref, parts, [(half, block) for block in range(4)], w_ref, sem_ref)
    start_first(copies)
    tokens = x_ref[...]
    if half == 0:
        xt_ref[...] = tokens.T
    first_time(copies[:3])
    projected = dot(tokens, w_ref[:, : 3 * cols])
    spot = slice(half * cols, (half + 1) * cols)
    q_ref[...] = (projected[:, :cols] + rows_ref[0:1, spot]).astype(BF)
    k_ref[...] = projected[:, cols : 2 * cols].astype(BF)
    v_ref[...] = (projected[:, 2 * cols :] + rows_ref[1:2, spot]).astype(BF)

    @pl.when(info_ref[0] == 1)
    def _():
        attend_pairs(False, q_ref, k_ref, v_ref, ctx_ref, lse_ref)

    @pl.when(info_ref[0] != 1)
    def _():
        attend_pairs(True, q_ref, k_ref, v_ref, ctx_ref, lse_ref)

    first_time(copies[3:])
    attended = dot_nt(ctx_ref[...], w_ref[:, 3 * cols :])
    if half == 0:
        z_ref[...] = tokens.astype(F32) + attended + rows_ref[2:3]
    else:
        z_ref[...] = before_ref[...] + attended


def forward(half, info, tokens, rows, weights, before=None):
    tok = tokens.shape[0] // 2
    width = tokens.shape[1]
    cols = width // 2
    groups = tok // LONG
    tile = pl.BlockSpec((LONG, width), lambda i, *_: (i, 0))
    part = pl.BlockSpec((LONG, cols), lambda i, *_: (i, half))
    low = struct((tok, width), BF)
    in_specs = [
        pl.BlockSpec((LONG, width), lambda i, info: (info[1] * groups + i, 0)),
        pl.BlockSpec((8, width), lambda i, *_: (0, 0)),
        ANY,
        ANY,
    ]
    out_specs = [
        part, part, part, part,
        pl.BlockSpec((1, 1, 8, LONG), lambda i, *_: (i, half, 0, 0)),
        tile,
    ]
    outs = [low, low, low, low, struct((groups, 2, 8, LONG), F32), struct((tok, width), F32)]
    inputs, kept = [], None
    if half == 0:
        out_specs.append(pl.BlockSpec((width, LONG), lambda i, *_: (0, i)))
        outs.append(struct((width, tok), BF))
    else:
        *kept, partial_sum = before[:6]
        inputs = [partial_sum]
        in_specs.append(tile)
    return call(
        functools.partial(forward_kernel, half),
        (groups,),
        in_specs,
        out_specs,
        outs,
        [pltpu.VMEM((width, 4 * cols), BF), pltpu.SemaphoreType.DMA((8,))],
        1,
        2 * tok * width * (4 * cols + LONG),
        12 * 2**20,
        tok * LONG * 6,
        kept,
    )(info, tokens, rows, *weights[2 * half : 2 * half + 2], *inputs, *(kept or ()))


def up_kernel(
    info_ref, z_ref, rows_ref, bias_ref, w0_ref, w1_ref, w2_ref, w3_ref,
    act_ref, slope_ref, ht_ref, hidden_ref, w_ref, sem_ref,
):
    width = z_ref.shape[1]
    parts = (w0_ref, w1_ref, w2_ref, w3_ref)
    copies = load_blocks(info_ref, parts, HALVED, w_ref, sem_ref)
    start_first(copies)
    normal, _ = normalized(z_ref[...])
    hidden = normal * rows_ref[3:4] + rows_ref[4:5]
    hidden_ref[...] = hidden
    low = hidden.astype(BF)
    ht_ref[...] = low.T
    for part in range(FF // width):
        spot = slice(part * width, (part + 1) * width)
        first_time(copies[2 * part : 2 * part + 2])
        upper = dot(low, w_ref[:, spot]) + bias_ref[part : part + 1]
        phi_sum = 0.5 + 0.5 * lax.erf(upper * (0.5**0.5))
        density = jnp.exp(-0.5 * upper * upper) * 0.3989422804014327
        act_ref[:, spot] = (upper * phi_sum).astype(BF)
        slope_ref[:, spot] = (phi_sum + upper * density).astype(BF)


ROWS, COLUMNS, NORM_ROWS = 256, 256, 128
UP_TILE = 256


def feed_up(info, first, rows, bias, weights):
    tok, width = first.shape
    wide = struct((tok, FF), BF)
    return call(
        up_kernel,
        (tok // UP_TILE,),
        [
            pl.BlockSpec((UP_TILE, width), lambda i, *_: (i, 0)),
            pl.BlockSpec((8, width), lambda i, *_: (0, 0)),
            pl.BlockSpec((4, width), lambda i, *_: (0, 0)),
        ]
        + [ANY] * 4,
        [
            pl.BlockSpec((UP_TILE, FF), lambda i, *_: (i, 0)),
            pl.BlockSpec((UP_TILE, FF), lambda i, *_: (i, 0)),
            pl.BlockSpec((width, UP_TILE), lambda i, *_: (0, i)),
            pl.BlockSpec((UP_TILE, width), lambda i, *_: (i, 0)),
        ],
        [wide, wide, struct((width, tok), BF), struct((tok, width), F32)],
        [pltpu.VMEM((width, FF), BF), pltpu.SemaphoreType.DMA((16,))],
        1,
        2 * tok * width * FF,
        20 * 2**20,
        tok * FF * 2,
    )(info, first, rows, bias, *weights)


PARTS = 4


def wait_pairs(copies):
    for pair in copies:
        for copy in pair:
            copy.wait()


def down_kernel(info_ref, h_in_ref, act_ref, cot_in_ref, rows_ref, *refs):
    parts, outs, gt_ref, sum_ref = refs[:4], refs[4:7], refs[7], refs[8]
    w_ref, h_ref, cot_ref, branch_ref = refs[9:13]
    out_ref, dz_ref, dyt_ref, low_ref, sem_ref, own_sem_ref = refs[13:]
    step = pl.program_id(0)
    tok, width = h_ref.shape
    copies = load_blocks(info_ref, parts, HALVED, w_ref, sem_ref)
    start = pl.multiple_of(info_ref[1] * tok, tok)
    h_copy = pltpu.make_async_copy(h_in_ref, h_ref, own_sem_ref.at[0])
    cot_copy = pltpu.make_async_copy(
        cot_in_ref.at[pl.ds(start, tok)], cot_ref, own_sem_ref.at[1]
    )
    out_copies = [
        pltpu.make_async_copy(source, target, own_sem_ref.at[2 + at])
        for at, (source, target) in enumerate(zip((out_ref, dz_ref, dyt_ref), outs))
    ]
    start_first(copies)

    @pl.when(step == 0)
    def _():
        h_copy.start()
        cot_copy.start()
        sum_ref[...] = jnp.zeros_like(sum_ref)

    for part in range(PARTS):
        @pl.when(step == part)
        def _():
            wait_pairs(copies[2 * part : 2 * part + 2])
            lanes = slice(part * width, (part + 1) * width)
            branch = dot_nt(act_ref[...], w_ref[:, lanes])
            branch_ref[...] = branch if part == 0 else branch_ref[...] + branch

    @pl.when(step == PARTS - 1)
    def _():
        h_copy.wait()
        cot_copy.wait()
        gains = rows_ref[6:7]
        sums = [0.0, 0.0, 0.0]
        for row in range(0, tok, NORM_ROWS):
            spot = slice(row, row + NORM_ROWS)
            normal, inverse = normalized(h_ref[spot, :] + branch_ref[spot, :] + rows_ref[5:6])
            out_ref[spot, :] = (normal * gains + rows_ref[7:8]).astype(BF)
            cot = cot_ref[spot, :].astype(F32)
            grad = norm_back(cot * gains, normal, inverse)
            dz_ref[spot, :] = grad
            low_ref[spot, :] = grad.astype(BF)
            for at, value in enumerate((grad, cot * normal, cot)):
                sums[at] = sums[at] + fold_rows(value)
        dyt_ref[...] = low_ref[...].T
        for at in range(3):
            sum_ref[at : at + 1] += row_sum(sums[at])
        for copy in out_copies:
            copy.start()

    @pl.when(step >= PARTS)
    def _():
        put_blocks(gt_ref, dot(dyt_ref[...], act_ref[...]))

    @pl.when(step == PARTS + 1)
    def _():
        for copy in out_copies:
            copy.wait()


def put_blocks(ref, grad):
    cols = ref.shape[2]
    for block in range(ref.shape[0]):
        ref[block] = grad[:, block * cols : (block + 1) * cols].astype(BF)


def feed_down(info, hidden, act, cot, rows, weights):
    tok, width = hidden.shape
    wide = (tok, width)
    return call(
        down_kernel,
        (PARTS + 2,),
        [
            ANY,
            pl.BlockSpec(wide, lambda i, *_: (0, jnp.where(i < PARTS, i, i - 2))),
            ANY,
            pl.BlockSpec((8, width), lambda i, *_: (0, 0)),
        ]
        + [ANY] * 4,
        [
            ANY,
            ANY,
            ANY,
            pl.BlockSpec((2, width, width // 2), lambda i, *_: (jnp.clip(i - PARTS, 0, 1), 0, 0)),
            pl.BlockSpec((8, width), lambda i, *_: (0, 0)),
        ],
        [
            struct(wide, BF),
            struct(wide, F32),
            struct((width, tok), BF),
            struct((4, width, width // 2), BF),
            struct((8, width), F32),
        ],
        [
            pltpu.VMEM((width, FF), BF),
            pltpu.VMEM(wide, F32),
            pltpu.VMEM(wide, BF),
            pltpu.VMEM(wide, F32),
            pltpu.VMEM(wide, BF),
            pltpu.VMEM(wide, F32),
            pltpu.VMEM((width, tok), BF),
            pltpu.VMEM(wide, BF),
            pltpu.SemaphoreType.DMA((16,)),
            pltpu.SemaphoreType.DMA((5,)),
        ],
        1,
        3 * tok * width * FF,
        30 * 2**20,
    )(info, hidden, act, cot, rows, *weights)


def back_kernel(info_ref, z_in_ref, dz2_ref, slope_ref, rows_ref, *refs):
    down, upper, other = refs[:4], refs[4:8], refs[8:12]
    outs, da_ref, sum_ref = refs[12:15], refs[15], refs[16]
    wd_ref, wu_ref, wo_ref, z_ref, hidden_ref, low_ref, held_ref = refs[17:24]
    dctx_ref, dtt_ref, dsem_ref, usem_ref, osem_ref, own_sem_ref = refs[24:]
    step = pl.program_id(0)
    tok, width = z_ref.shape
    downs = load_blocks(info_ref, down, HALVED, wd_ref, dsem_ref)
    ups = load_blocks(info_ref, upper, HALVED, wu_ref, usem_ref)
    others = load_blocks(info_ref, other, [(0, 3), (1, 3)], wo_ref, osem_ref)
    z_copy = pltpu.make_async_copy(z_in_ref, z_ref, own_sem_ref.at[0])
    for at in range(0, 8, 2):
        start_first(downs[at : at + 2] + ups[at : at + 2])
    start_first(others + [[z_copy]])

    @pl.when(step == 0)
    def _():
        sum_ref[...] = jnp.zeros_like(sum_ref)
        hidden_ref[...] = dz2_ref[...]
        low_ref[...] = dz2_ref[...].astype(BF)

    for part in range(PARTS + 1):
        @pl.when(step == part)
        def _():
            if part < PARTS:
                wait_pairs(downs[2 * part : 2 * part + 2])
            if part > 0:
                wait_pairs(ups[2 * part - 2 : 2 * part])
            place = 4 + (part ^ (2 * info_ref[1]))
            for column in range(0, width, COLUMNS):
                spot = slice(column, column + COLUMNS)
                lanes = slice(part * width + column, part * width + column + COLUMNS)
                if part < PARTS:
                    grad_act = dot(low_ref[...], wd_ref[:, lanes])
                if part > 0:
                    before = slice((part - 1) * width, part * width)
                    hidden_ref[:, spot] += dot_nt(held_ref[(part - 1) % 2], wu_ref[spot, before])
                if part < PARTS:
                    grad_up = (grad_act * slope_ref[:, spot].astype(F32)).astype(BF)
                    da_ref[:, spot] = grad_up
                    held_ref[part % 2, :, spot] = grad_up
                    sum_ref[pl.ds(place, 1), spot] = row_sum(fold_rows(grad_up.astype(F32)))

    @pl.when(step == PARTS)
    def _():
        z_copy.wait()
        gains = rows_ref[3:4]
        sums = [0.0, 0.0, 0.0]
        out_copies = []
        for half in range(2):
            rows = slice(half * (tok // 2), (half + 1) * (tok // 2))
            for row in range(rows.start, rows.stop, NORM_ROWS):
                spot = slice(row, row + NORM_ROWS)
                grad_hidden = hidden_ref[spot, :]
                normal, inverse = normalized(z_ref[spot, :])
                grad_one = norm_back(grad_hidden * gains, normal, inverse)
                low_ref[spot, :] = grad_one.astype(BF)
                for at, value in enumerate((grad_one, grad_hidden * normal, grad_hidden)):
                    sums[at] = sums[at] + fold_rows(value)
            if half == 0:
                wait_pairs(others)
            dctx_ref[rows, :] = dot(low_ref[rows, :], wo_ref[...]).astype(BF)
            dtt_ref[:, rows] = low_ref[rows, :].T
            spot = pl.ds(rows.start, tok // 2)
            for at, (source, target) in enumerate(zip((low_ref, dctx_ref, dtt_ref), outs)):
                source, target = (
                    (source.at[:, spot], target.at[:, spot])
                    if at == 2
                    else (source.at[spot], target.at[spot])
                )
                out_copies.append(
                    pltpu.make_async_copy(source, target, own_sem_ref.at[1 + 3 * half + at])
                )
                out_copies[-1].start()
        for at in range(3):
            sum_ref[at : at + 1] = row_sum(sums[at])
        for copy in out_copies:
            copy.wait()


def feed_back(info, first, dz2, slope, rows, down, upper, other):
    tok, width = first.shape
    wide = (tok, width)
    fixed = pl.BlockSpec((8, width), lambda i, *_: (0, 0))
    part = pl.BlockSpec(wide, lambda i, *_: (0, jnp.minimum(i, PARTS - 1)))
    return call(
        back_kernel,
        (PARTS + 1,),
        [ANY, pl.BlockSpec(wide, lambda i, *_: (0, 0)), part, fixed] + [ANY] * 12,
        [ANY, ANY, ANY, part, fixed],
        [
            struct(wide, BF),
            struct(wide, BF),
            struct((width, tok), BF),
            struct((tok, FF), BF),
            struct((8, width), F32),
        ],
        [
            pltpu.VMEM((width, FF), BF),
            pltpu.VMEM((width, FF), BF),
            pltpu.VMEM((width, width), BF),
            pltpu.VMEM(wide, F32),
            pltpu.VMEM(wide, F32),
            pltpu.VMEM(wide, BF),
            pltpu.VMEM((2, *wide), BF),
            pltpu.VMEM(wide, BF),
            pltpu.VMEM((width, tok), BF),
            pltpu.SemaphoreType.DMA((16,)),
            pltpu.SemaphoreType.DMA((16,)),
            pltpu.SemaphoreType.DMA((4,)),
            pltpu.SemaphoreType.DMA((7,)),
        ],
        1,
        4 * tok * width * FF,
        30 * 2**20,
    )(info, first, dz2, slope, rows, *down, *upper, *other)


def product_kernel(left_ref, right_ref, *outs):
    grad = dot(left_ref[...], right_ref[...])
    step = pl.program_id(0)
    for at, ref in enumerate(outs):
        @pl.when(step // 2 == at)
        def _():
            put_blocks(ref, grad)


def wide_grad(left_t, right, halves, blocks=4):
    width, tok = left_t.shape
    first = halves[0]
    spec = [
        pl.BlockSpec(
            (2, width, width // 2), lambda i, at=at: (jnp.clip(i - 2 * at, 0, 1), 0, 0)
        )
        for at in range(len(halves))
    ]
    return call(
        product_kernel,
        (2 * len(halves),),
        [
            pl.BlockSpec((width, tok), lambda i: (0, 0)),
            pl.BlockSpec((tok, width), lambda i: (0, (i + 2 * first) % 4)),
        ],
        spec,
        [struct((blocks, width, width // 2), BF)] * len(halves),
        [],
        0,
        tok * width * FF * len(halves),
        10 * 2**20 * len(halves),
    )(left_t, right)


def share_kernel(left_ref, right_ref, out_ref):
    put_blocks(out_ref, dot(left_ref[...], right_ref[...]))


def share_grad(left_t, right, half):
    width, tok = left_t.shape
    cols = right.shape[1] // 2
    shape = (3, width, cols // 3)
    return call(
        share_kernel,
        (1,),
        [
            pl.BlockSpec((width, tok), lambda i: (0, 0)),
            pl.BlockSpec((tok, cols), lambda i: (0, half)),
        ],
        [pl.BlockSpec(shape, lambda i: (0, 0, 0))],
        [struct(shape, BF)],
        [],
        0,
        2 * tok * width * cols,
        6 * 2**20,
    )(left_t, right)[0]


def up_grad_kernel(
    ht_ref, da_ref, dtt_in_ref, ctx_in_ref, gm_ref, gt_ref,
    held_ref, dtt_ref, ctx_ref, sem_ref, in_sem_ref,
):
    step = pl.program_id(0)
    loads = [
        pltpu.make_async_copy(dtt_in_ref, dtt_ref, in_sem_ref.at[0]),
        pltpu.make_async_copy(ctx_in_ref, ctx_ref, in_sem_ref.at[1]),
    ]
    start_first([loads])
    cols = held_ref.shape[3]

    def copies(at):
        targets = (
            [(ref, PARTS) for ref in (gm_ref, gt_ref)]
            if at == PARTS
            else [((gm_ref, gt_ref)[at // 2], at % 2 * 2 + block) for block in range(2)]
        )
        return [
            pltpu.make_async_copy(
                held_ref.at[at % 2, block], ref.at[target], sem_ref.at[at % 2, block]
            )
            for block, (ref, target) in enumerate(targets)
        ]

    for at in range(PARTS + 1):
        @pl.when(step == at)
        def _():
            if at == PARTS:
                wait_pairs([loads])
            left, right = (dtt_ref, ctx_ref) if at == PARTS else (ht_ref, da_ref)
            grad = dot(left[...], right[...])
            if at >= 2:
                for copy in copies(at - 2):
                    copy.wait()
            for block in range(2):
                held_ref[at % 2, block] = grad[:, block * cols : (block + 1) * cols].astype(BF)
            for copy in copies(at):
                copy.start()
            if at == PARTS:
                for copy in copies(at - 1) + copies(at):
                    copy.wait()


def up_grad(hidden_t, dt_t, grad_up, ctx):
    width, tok = hidden_t.shape
    cols = width // 2
    whole = pl.BlockSpec((width, tok), lambda i: (0, 0))
    return call(
        up_grad_kernel,
        (PARTS + 1,),
        [
            whole,
            pl.BlockSpec((tok, width), lambda i: (0, jnp.minimum(i, PARTS - 1))),
            ANY,
            ANY,
        ],
        [ANY, ANY],
        [struct((PARTS + 1, width, cols), BF)] * 2,
        [
            pltpu.VMEM((2, 2, width, cols), BF),
            pltpu.VMEM((width, tok), BF),
            pltpu.VMEM((tok, width), BF),
            pltpu.SemaphoreType.DMA((2, 2)),
            pltpu.SemaphoreType.DMA((2,)),
        ],
        0,
        2 * tok * width * (FF + width),
        25 * 2**20,
    )(hidden_t, grad_up, dt_t, ctx)


def attend_pairs_back(first, short, q_ref, k_ref, v_ref, dctx_ref, lse_ref, dqkv_ref):
    width = q_ref.shape[1]
    pairs = range(BACKWARD_PAIRS)
    lanes = [pair_lanes(first + pair) for pair in pairs]
    queries = [q_ref[:, at] * BF(HD**-0.5) for at in lanes]
    keys_here = [k_ref[:, at] for at in lanes]
    grads = [dctx_ref[:, at] for at in lanes]
    keys_t = [keys.T for keys in keys_here]
    scores = [dot_nt(both_heads(keys_here[pair]), queries[pair]) for pair in pairs]
    grad_probs = [
        by_head(dot_nt(both_heads(v_ref[:, lanes[pair]]), grads[pair])) for pair in pairs
    ]
    if short:
        scores = [jnp.where(seen_mask(), score, -1e30) for score in scores]
    probs = [
        jnp.exp(
            by_head(scores[pair])
            - jnp.stack(
                [
                    lse_ref[0, (first + pair) // 3, pl.ds((first + pair) % 3 * 2 + head, 1), :]
                    for head in range(2)
                ]
            )
        )
        for pair in pairs
    ]
    grad_v = [
        dot(prob.astype(BF).reshape(2 * LONG, LONG), grads[pair])
        for pair, prob in enumerate(probs)
    ]
    inners = [
        jnp.sum(prob * grad, axis=1, keepdims=True) for prob, grad in zip(probs, grad_probs)
    ]
    grad_scores = [
        (prob * (grad - inner)).astype(BF)
        for prob, grad, inner in zip(probs, grad_probs, inners)
    ]
    grad_k = [
        dot(grad.reshape(2 * LONG, LONG), queries[pair]) for pair, grad in enumerate(grad_scores)
    ]
    for pair in pairs:
        grad_q = [
            dot(keys_t[pair][head * HD : (head + 1) * HD], grad_scores[pair][head])
            for head in range(2)
        ]

        def store(part, values_in):
            at = first + pair
            half = at // 3
            start = half * (3 * width // 2) + part * (width // 2) + (at - 3 * half) * 2 * HD
            dqkv_ref[:, pl.ds(pl.multiple_of(start, 2 * HD), 2 * HD)] = values_in.astype(BF)

        store(0, jnp.concatenate(grad_q, axis=0).T * HD**-0.5)
        store(1, pair_columns(grad_k[pair]))
        store(2, pair_columns(grad_v[pair]))


def attend_back_kernel(
    info_ref, q_ref, k_ref, v_ref, dctx_ref, lse_ref, dqkv_ref, sum_ref,
):
    width = q_ref.shape[1]

    def all_pairs(short):
        @pl.loop(0, width // (2 * HD), step=BACKWARD_PAIRS)
        def _(first):
            attend_pairs_back(first, short, q_ref, k_ref, v_ref, dctx_ref, lse_ref, dqkv_ref)

    @pl.when(info_ref[0] == 1)
    def _():
        all_pairs(False)

    @pl.when(info_ref[0] != 1)
    def _():
        all_pairs(True)

    sum_ref[...] = jnp.zeros_like(sum_ref)
    cols = width // 2
    for half in range(2):
        core = info_ref[1] if half == 0 else 1 - info_ref[1]
        spot = pl.ds(pl.multiple_of(core * cols, cols), cols)
        for row, part in enumerate((0, 2)):
            start = (3 * half + part) * cols
            sum_ref[row : row + 1, spot] = row_sum(dqkv_ref[:, start : start + cols].astype(F32))


def attend_back(group, info, q, k, v, dctx, lse, kept=None):
    tok, width = q.shape
    tile = pl.BlockSpec((LONG, width), lambda i, *_: (group, 0))
    dqkv, sums = call(
        attend_back_kernel,
        (1,),
        [
            tile, tile, tile, tile,
            pl.BlockSpec((1, 2, 8, LONG), lambda i, *_: (group, 0, 0, 0)),
        ],
        [
            pl.BlockSpec((LONG, 3 * width), lambda i, *_: (group, 0)),
            pl.BlockSpec((8, width), lambda i, *_: (0, 0)),
        ],
        [struct((tok, 3 * width), BF), struct((8, width), F32)],
        [],
        1,
        2 * LONG * width * 10 * LONG,
        12 * 2**20,
        LONG * LONG * 12,
        kept,
    )(info, q, k, v, dctx, lse, *(kept or ()))
    return dqkv, sums


def token_grad_kernel(info_ref, dqkv_ref, dz_ref, *refs):
    parts, (gx_ref, w_ref, sem_ref) = refs[:4], refs[4:]
    copies = load_blocks(info_ref, parts, SHARES, w_ref, sem_ref)
    start_first(copies)
    first_time(copies)
    gx_ref[...] = (dz_ref[...].astype(F32) + dot_nt(dqkv_ref[...], w_ref[...])).astype(BF)


def token_grad(info, dqkv, dz, weights):
    tok, width = dz.shape
    tile = pl.BlockSpec((LONG, width), lambda i, *_: (i, 0))
    return call(
        token_grad_kernel,
        (tok // LONG,),
        [pl.BlockSpec((LONG, 3 * width), lambda i, *_: (i, 0)), tile] + [ANY] * 4,
        [tile],
        [struct((tok, width), BF)],
        [pltpu.VMEM((width, 3 * width), BF), pltpu.SemaphoreType.DMA((12,))],
        1,
        6 * tok * width * width,
        15 * 2**20,
    )(info, dqkv, dz, *weights)[0]


def adamw_update(weights_in, moment, square, average_in, gradient, rate, scalars):
    beta_one, beta_two, ema_decay, scale_one, scale_two = scalars
    moment_new = beta_one * moment + (1.0 - beta_one) * gradient
    square_new = beta_two * square + (1.0 - beta_two) * gradient * gradient
    moment_hat = moment_new * scale_one
    square_hat = square_new * scale_two
    weights_new = weights_in - rate * (
        moment_hat / (jnp.sqrt(square_hat) + 1e-08) + 0.01 * weights_in
    )
    average_new = ema_decay * average_in + (1.0 - ema_decay) * weights_new
    return weights_new, moment_new, square_new, average_new


SLOT_STEPS = 3
LATE = 3


def fetch_gradient(ref, table_ref, slot, held_ref, sem_ref, rows):
    spot = pl.ds(pl.multiple_of(table_ref[2, slot] * rows, rows), rows)
    return pltpu.make_async_copy(
        ref.at[table_ref[1, slot], spot], held_ref.at[slot], sem_ref.at[slot]
    )


def await_gradient(ref, slot, held_ref, sem_ref, rows):
    pltpu.make_async_copy(
        ref.at[0, pl.ds(0, rows)], held_ref.at[slot], sem_ref.at[slot]
    ).wait()


def adamw_kernel(table_ref, scale_ref, w_ref, m_ref, s_ref, a_ref, *refs):
    grads, outs, (held_ref, sem_ref) = refs[:5], refs[5:9], refs[9:]
    step = pl.program_id(0)
    count, rows, _ = w_ref.shape

    @pl.when(step == 0)
    def _():
        @pl.loop(0, held_ref.shape[0])
        def _(slot):
            for at, ref in enumerate(grads):
                chosen = table_ref[0, slot] == at + LATE
                if at == 0:
                    chosen = table_ref[0, slot] <= LATE

                @pl.when(chosen)
                def _():
                    fetch_gradient(ref, table_ref, slot, held_ref, sem_ref, rows).start()

    scalars = [scale_ref[at] for at in range(5)]

    @pl.loop(0, count)
    def _(at):
        slot = step * count + at
        await_gradient(grads[0], slot, held_ref, sem_ref, rows)
        gradient = held_ref[slot].astype(F32) * scale_ref[8 + 2 * slot]
        results = adamw_update(
            w_ref[at], m_ref[at], s_ref[at], a_ref[at], gradient,
            scale_ref[9 + 2 * slot], scalars,
        )
        for ref, value in zip(outs, results):
            ref[at] = value


def adamw_slots(table, scales, states, grads):
    cap, rows, cols = states[0].shape
    steps = SLOT_STEPS if cap % SLOT_STEPS == 0 else 1
    own = pl.BlockSpec((cap // steps, rows, cols), lambda i, *_: (i, 0, 0))
    return call(
        adamw_kernel,
        (steps,),
        [own] * 4 + [ANY] * 5,
        [own] * 4,
        [struct(states[0].shape, F32)] * 4,
        [pltpu.VMEM((cap, rows, cols), BF), pltpu.SemaphoreType.DMA((cap,))],
        2,
        20 * cap * rows * cols,
        40 * cap * rows * cols,
    )(table, scales, *states, *grads)


def late_kernel(table_ref, scale_ref, *refs):
    states, grads, outs, scratch = refs[:4], refs[4:7], refs[7:11], refs[11:]
    state_ref, result_ref, held_ref, sem_ref, state_sem_ref, out_sem_ref = scratch
    cap, rows, _ = held_ref.shape
    scalars = [scale_ref[at] for at in range(5)]

    def loads(slot):
        return [
            pltpu.make_async_copy(ref.at[slot], state_ref.at[slot, at], state_sem_ref.at[slot, at])
            for at, ref in enumerate(states)
        ]

    def stores(slot):
        return [
            pltpu.make_async_copy(result_ref.at[slot, at], ref.at[slot], out_sem_ref.at[slot, at])
            for at, ref in enumerate(outs)
        ]

    def each(work):
        @pl.loop(0, cap)
        def _(slot):
            @pl.when(table_ref[0, slot] < LATE)
            def _():
                work(slot)

    def begin(slot):
        for at, ref in enumerate(grads):
            @pl.when(table_ref[0, slot] == at)
            def _():
                fetch_gradient(ref, table_ref, slot, held_ref, sem_ref, rows).start()
        for copy in loads(slot):
            copy.start()

    def update(slot):
        await_gradient(grads[0], slot, held_ref, sem_ref, rows)
        for copy in loads(slot):
            copy.wait()
        gradient = held_ref[slot].astype(F32) * scale_ref[8 + 2 * slot]
        results = adamw_update(
            *[state_ref[slot, at] for at in range(4)], gradient, scale_ref[9 + 2 * slot], scalars
        )
        for at, value in enumerate(results):
            result_ref[slot, at] = value
        for copy in stores(slot):
            copy.start()

    def finish(slot):
        for copy in stores(slot):
            copy.wait()

    each(begin)
    each(update)
    each(finish)


def adamw_late(table, scales, states, grads, kept):
    cap, rows, cols = states[0].shape
    return call(
        late_kernel,
        (1,),
        [ANY] * 7,
        [ANY] * 4,
        [struct(states[0].shape, F32)] * 4,
        [
            pltpu.VMEM((cap, 4, rows, cols), F32),
            pltpu.VMEM((cap, 4, rows, cols), F32),
            pltpu.VMEM((cap, rows, cols), BF),
            pltpu.SemaphoreType.DMA((cap,)),
            pltpu.SemaphoreType.DMA((cap, 4)),
            pltpu.SemaphoreType.DMA((cap, 4)),
        ],
        2,
        20 * cap * rows * cols,
        40 * cap * rows * cols,
        0,
        kept,
    )(table, scales, *states, *grads, *kept)


def on_device(
    tokens,
    cotangent,
    phase_of,
    unit_slot,
    step_count,
    learn_rates,
    decay_rates,
    master,
    first_moment,
    second_moment,
    average,
    vector_state,
):
    cap, unit_rows, cols = master.shape
    tok_rows, width = tokens.shape
    batch_count = lax.axis_size("batch")
    row_blocks = width // unit_rows
    col_blocks = FF // width
    core = lax.axis_index("tensor")
    place = lax.axis_index("batch")
    fast = batch_count == FAST_BATCH
    plane, y_at, x_at = place // 4, (place // 2) % 2, place % 2
    up_base = 4 * row_blocks
    down_base = up_base + row_blocks * col_blocks
    chunks = [(0, 1, row_blocks), (up_base, col_blocks, 1), (down_base, col_blocks, 1)]
    corner = jnp.stack([place % 4, place % 4, plane]).astype(jnp.int32)

    def coords(orient):
        y_first = (core + orient) % 2 == 0
        first = jnp.where(y_first, y_at, x_at)
        second = jnp.where(y_first, x_at, y_at)
        return jnp.stack([first, second, plane]).astype(jnp.int32)

    places = [coords(orient) for orient in range(2)]

    def chunk_units(chunk):
        base, row_step, block_step = chunk
        return base + jnp.arange(4)[:, None] * block_step + jnp.arange(row_blocks)[None] * row_step

    def spreads(sources, which):
        first_bit = jnp.where(core == 0, 2, 1)
        inner = place % 4
        numbers = jnp.stack(
            [
                places[0][0] * 2 + places[0][1], plane, place,
                inner, inner ^ first_bit, inner ^ (3 - first_bit), inner ^ 3,
            ]
        ).astype(jnp.int32)
        return [spread(sources, unit_slot, numbers, chunks[at]) for at in which]

    def weights_chain(pieces):
        return Chain(spreading(pieces, 0, places[0]))

    def weights_plain(at):
        local = unit_slot[chunk_units(chunks[at])] - place * cap
        own = (local >= 0) & (local < cap)
        blocks = jnp.take(master, jnp.clip(local, 0, cap - 1), axis=0)
        blocks = jnp.where(own[..., None, None], blocks, 0.0).astype(BF)
        return lax.psum(blocks.reshape(4, width, cols), "batch")

    def grads_chain(terms, orient):
        return Chain(exchange(terms, orient, places[orient]))

    def shared(array_in):
        half = array_in.shape[1] // 2
        parts = [array_in[:, :half], array_in[:, half:]]
        return parts + [core_swap(part) for part in parts]

    def halves_of(array_in):
        other = lax.dynamic_slice_in_dim(array_in, (1 - core) * cols, cols, array_in.ndim - 1)
        return lax.dynamic_slice_in_dim(array_in, core * cols, cols, array_in.ndim - 1), other

    def swapped(array_in):
        return jnp.concatenate(halves_of(array_in), axis=-1)

    def both(here, there):
        low_first = core == 0
        return jnp.concatenate(
            [jnp.where(low_first, here, there), jnp.where(low_first, there, here)], axis=0
        )

    count_f = step_count[0].astype(F32)
    scalars = [
        decay_rates[0],
        decay_rates[1],
        decay_rates[2],
        1.0 / (1.0 - decay_rates[0] ** count_f),
        1.0 / (1.0 - decay_rates[1] ** count_f),
    ]

    def vec_update(sums):
        vector_grads = jnp.concatenate(
            [sums[0:2], sums[8:11], sums[12:16], sums[16:19]], axis=0
        )
        grads_scaled = vector_grads * float(tok_rows * batch_count) ** (-0.5)
        vec_weights, vec_first, vec_second, vec_average = adamw_update(
            vector_state[0], vector_state[1], vector_state[2], vector_state[3],
            grads_scaled, learn_rates[4], scalars,
        )
        return (
            jnp.stack([vec_weights, vec_average]),
            jnp.stack([grads_scaled, vec_first]),
            vec_second,
        )

    my_ids = place * cap + jnp.arange(cap, dtype=jnp.int32)
    matches = unit_slot[None, :] == my_ids[:, None]
    unit_ids = jnp.arange(unit_slot.shape[0], dtype=jnp.int32)
    unit = jnp.sum(jnp.where(matches, unit_ids[None, :], 0), axis=1)
    occupied = jnp.any(matches, axis=1)
    is_up = (unit >= up_base) & (unit < down_base)
    is_down = unit >= down_base
    is_other = (unit >= 3 * row_blocks) & (unit < up_base)
    is_wide = is_up | is_down
    chunk_at = jnp.where(is_down, 2, jnp.where(is_up | is_other, 1, 0))
    local = unit - jnp.where(is_down, down_base, up_base)
    block_at = jnp.where(
        is_wide, local % col_blocks, jnp.where(is_other, col_blocks, unit // row_blocks)
    )
    row_at = jnp.where(is_wide, local // col_blocks, unit % row_blocks)
    kind = jnp.where(
        occupied,
        (unit >= 3 * row_blocks).astype(jnp.int32) + is_up.astype(jnp.int32) + 2 * is_down,
        0,
    )
    rates = jnp.sum(
        jnp.where(kind[:, None] == jnp.arange(4)[None, :], learn_rates[None, :4], 0.0), axis=1
    )
    quarter_rows, half_rows = row_blocks // 4, row_blocks // 2
    first_quarter = corner[0] if fast else 0
    first_half = jnp.where(chunk_at == 1, places[1][0], places[0][0]) if fast else 0
    array_at = jnp.where(
        chunk_at == 0,
        (((row_at // quarter_rows) ^ first_quarter) + 3) % 4,
        2 + 2 * chunk_at + ((row_at // half_rows) ^ first_half),
    )
    row_at = jnp.where(chunk_at == 0, row_at % quarter_rows, row_at % half_rows)
    table = jnp.stack([array_at, block_at, row_at]).astype(jnp.int32)
    states = (master, first_moment, second_moment, average)
    scales = jnp.concatenate(
        [
            jnp.stack(scalars),
            jnp.zeros((3,), F32),
            jnp.stack([occupied.astype(F32), rates], axis=1).reshape(-1),
        ]
    )
    firsts = [places[0][0], places[1][0]] if fast else [0, 0]
    info = jnp.stack([phase_of[0], core, *firsts]).astype(jnp.int32)
    vectors = vector_state[0]
    rows = jnp.concatenate([swapped(vectors[0:2]), vectors[2:5], vectors[9:12]], axis=0)
    upper = vectors[5:9].reshape(2, FF // 2)
    turned = jnp.concatenate([upper[1:], upper[:1]], axis=0)
    bias_up = jnp.where(core == 0, upper, turned).reshape(4, width)

    if fast:
        low_master = master.astype(BF)
        beside = lax.ppermute(low_master, BOTH, swap_pairs(0, 1))
        across = lax.ppermute(low_master, BOTH, swap_pairs(0, 2))
        diagonal = lax.ppermute(beside, BOTH, swap_pairs(0, 2))
        sources = (low_master, beside, across, diagonal)
        io = weights_chain(spreads(sources, (0,))[0])
        _, (up, down) = phase([io], work=lambda _: spreads(sources, (1, 2)))
        up, down = weights_chain(up), weights_chain(down)
        _, (info, rows, bias_up, table, scales) = phase(
            [io], work=lambda _: (info, rows, bias_up, table, scales)
        )
        phase([io, up])
        theirs_first, _ = phase([io, up], io.ready)
        theirs_last, begun = phase(
            [up, down],
            io.result[1:],
            lambda late: forward(0, after(info, late), tokens, rows, io.result),
        )
        weights_io = [*io.result, *theirs_first, *theirs_last]
        theirs_first, stage = phase(
            [up, down],
            up.ready,
            lambda late: forward(1, after(info, late), tokens, rows, weights_io, begun),
        )
        theirs_last, _ = phase([down], up.result[1:])
        weights_up = [*up.result, *theirs_first, *theirs_last]
        q, k, v, ctx, lse, first = stage
        x_t = begun[6]
        theirs_first, (act, slope, hidden_t, hidden) = phase(
            [down],
            down.ready,
            lambda late: feed_up(after(info, late), first, rows, bias_up, weights_up),
        )
        theirs_last, _ = phase(swaps=down.result[1:])
        weights_down = [*down.result, *theirs_first, *theirs_last]
    else:
        weights_io, weights_up, weights_down = [shared(weights_plain(at)) for at in range(3)]
        begun = forward(0, info, tokens, rows, weights_io)
        q, k, v, ctx, lse, first = forward(1, info, tokens, rows, weights_io, begun)
        x_t = begun[6]
        act, slope, hidden_t, hidden = feed_up(info, first, rows, bias_up, weights_up)

    out_half, dz2, grad_two_t, down_theirs, sums_two = feed_down(
        info, hidden, act, cotangent, rows, weights_down
    )
    heads = (q, k, v)

    def back(info):
        return feed_back(
            info, first, dz2, slope, rows, weights_down, weights_up, weights_io
        )

    def heads_back(group, info, dctx, kept=None):
        return attend_back(group, info, *heads, dctx, lse, kept)

    if fast:
        (other,), (down_mine,) = phase(
            swaps=[down_theirs], work=lambda late: wide_grad(after(grad_two_t, late), act, (0,))
        )
        down = grads_chain([down_mine, other], 0)
        (out_other,), (dz1, dctx, dt_t, grad_up, sums_one) = phase(
            [down], [out_half], lambda late: back(after(info, late))
        )
        _, (up_mine, up_theirs) = phase(
            [down],
            work=lambda late: up_grad(after(hidden_t, late), dt_t, grad_up, ctx),
        )
        (other,), (dqkv, sums_zero) = phase(
            [down], [up_theirs], lambda late: heads_back(0, after(info, late), dctx)
        )
        up = grads_chain([up_mine, other], 1)
        _, (dqkv, sums_extra) = phase(
            [down, up],
            work=lambda late: heads_back(1, after(info, late), dctx, [dqkv]),
        )
        vec = Chain(doubling(jnp.concatenate([sums_zero + sums_extra, sums_one, sums_two])))
        _, (io_theirs, grad_x) = phase(
            [down, up, vec],
            work=lambda late: (
                share_grad(after(x_t, late), dqkv, 1),
                token_grad(info, dqkv, dz1, weights_io),
            ),
        )
        (other,), io_mine = phase(
            [down, up, vec], [io_theirs], lambda late: share_grad(after(x_t, late), dqkv, 0)
        )
        io = Chain(plane_exchange([io_mine, other], corner))
        (grad_x_other,), out = phase(
            [io, up, vec], [grad_x], lambda late: both(after(out_half, late), out_other)
        )
        _, input_grad = phase(
            [io, up, vec],
            work=lambda late: both(after(grad_x, late), grad_x_other).astype(F32),
        )
        phase([io, up, vec])
        nearest = io.ready[0]
        vec_outs = vec_update(vec.result)
        _, new_states = phase(
            [io],
            work=lambda late: adamw_slots(
                after(table, late), scales, states, [nearest, *up.result, *down.result]
            ),
        )
        grads = io.result[1:]
    else:
        dz1, dctx, dt_t, grad_up, sums_one = back(info)
        dqkv, sums_zero = heads_back(0, info, dctx)
        for group in range(1, tok_rows // 2 // LONG):
            dqkv, sums_extra = heads_back(group, info, dctx, [dqkv])
            sums_zero = sums_zero + sums_extra
        grad_x = token_grad(info, dqkv, dz1, weights_io)
        up_mine, up_theirs = up_grad(hidden_t, dt_t, grad_up, ctx)
        (down_mine,) = wide_grad(grad_two_t, act, (0,))
        grads = []
        for mine, theirs, parts in (
            (share_grad(x_t, dqkv, 0), share_grad(x_t, dqkv, 1), 4),
            (up_mine, up_theirs, 2),
            (down_mine, down_theirs, 2),
        ):
            grad = lax.psum(total(mine, core_swap(theirs)), "batch")
            grads += jnp.split(grad, parts, axis=1)
        new_states = adamw_slots(table, scales, states, [grads[0], *grads[4:]])
        grads = grads[1:4]
        vec_outs = vec_update(
            lax.psum(jnp.concatenate([sums_zero, sums_one, sums_two]), BOTH)
        )
        out = both(out_half, core_swap(out_half))
        input_grad = both(grad_x, core_swap(grad_x)).astype(F32)

    new_states = adamw_late(table, scales, states, grads, new_states)
    return (out, input_grad, *new_states, *vec_outs)


def solution(mesh):
    return jax.shard_map(
        on_device,
        mesh=mesh,
        in_specs=(
            P("batch", None),
            P("batch", None),
            P("batch"),
            P(),
            P(),
            P(),
            P(),
            P("batch", None, "tensor"),
            P("batch", None, "tensor"),
            P("batch", None, "tensor"),
            P("batch", None, "tensor"),
            P(),
        ),
        out_specs=(
            P("batch", None),
            P("batch", None),
            P("batch", None, "tensor"),
            P("batch", None, "tensor"),
            P("batch", None, "tensor"),
            P("batch", None, "tensor"),
            P(),
            P(),
            P(),
        ),
        check_vma=False,
    )
```
